32 devices in a mesh: dp: 8 (over y, x, core), table: 4 (over z).
Axes of the slice: x: 2, y: 2, z: 4, core: 2. Of those that a mesh axis runs over, the one named last changes fastest.
Arguments:
- features: bfloat16 [3, 8, 2048, 100], P(None, 'dp', 'table'), may hold values from -6 to 6
- feature_mask: int32 [3, 8, 100], P(None, 'dp'), may hold values 0 or 1
- support_count: int32 [3, 8], P(None, 'dp'), may hold values from 1537 to 2047
- embed_weight: bfloat16 [100, 512], P(None, 'dp'), may hold values from -0.625 to 0.625
- embed_bias: bfloat16 [512], P('dp'), may hold values from -3 to 3
- gain_first: bfloat16 [512], P('dp'), may hold values from 0.5 to 1.5
- shift_first: bfloat16 [512], P('dp'), may hold values from -2 to 2
- query_weight: bfloat16 [512, 512], P('dp'), may hold values from -0.375 to 0.375
- key_weight: bfloat16 [512, 512], P('dp'), may hold values from -0.375 to 0.375
- value_weight: bfloat16 [512, 512], P('dp'), may hold values from -0.25 to 0.25
- out_weight: bfloat16 [512, 512], P('dp'), may hold values from -1.5 to 1.5
- gain_second: bfloat16 [512], P('dp'), may hold values from 0.5 to 1.5
- shift_second: bfloat16 [512], P('dp'), may hold values from -2 to 2
- up_weight: bfloat16 [512, 2048], P('dp'), may hold values from -0.25 to 0.25
- up_bias: bfloat16 [2048], P('dp'), may hold values from -3 to 3
- down_weight: bfloat16 [2048, 512], P('dp'), may hold values from -0.125 to 0.125
- down_bias: bfloat16 [512], P('dp'), may hold values from -2 to 2
- cotangent: bfloat16 [3, 8, 2048, 512], P(None, 'dp', 'table'), may hold values from -6 to 6
Outputs:
- activations: bfloat16 [3, 8, 2048, 512], P(None, 'dp', 'table')
- input_grad: float32 [3, 8, 2048, 100], P(None, 'dp', 'table')
- grad_embed_weight: float32 [100, 512], P(None, 'dp')
- grad_embed_bias: float32 [512], P('dp')
- grad_gain_first: float32 [512], P('dp')
- grad_shift_first: float32 [512], P('dp')
- grad_query_weight: float32 [512, 512], P('dp')
- grad_key_weight: float32 [512, 512], P('dp')
- grad_value_weight: float32 [512, 512], P('dp')
- grad_out_weight: float32 [512, 512], P('dp')
- grad_gain_second: float32 [512], P('dp')
- grad_shift_second: float32 [512], P('dp')
- grad_up_weight: float32 [512, 2048], P('dp')
- grad_up_bias: float32 [2048], P('dp')
- grad_down_weight: float32 [2048, 512], P('dp')
- grad_down_bias: float32 [512], P('dp')
The draws below stay inside these ranges and needn't reach their ends.
Inputs may be any that keep to these rules, and one draw needn't show every extreme that they name: A table's first support_count rows are its support rows; the other rows are queries. Every row attends to the support rows only.
All inputs are finite; a program needn't handle non-finite values. No bound on the sum of `feature_mask` on one device may be relied on, other than what follows from the above.
Results may differ from the reference program's by a relative error of at most 0.014.
Values may be sent and summed in bfloat16 or wider, within the bound.
A program may use at most 256 MiB of HBM per device.

```python
import jax
import jax.numpy as jnp
from jax import lax

D = 512
HEADS = 4
HEAD_DIM = 128
FF = 2048
FEAT = 100
ROWS_DEV = 512
MICRO = 3
ROWS = 2048
TABLES = 8


def place_ends(values, own_key, least, high):
    extent = values.shape
    index_at = [jax.random.randint(jax.random.fold_in(own_key, axis), (), 0, extent[axis]) for axis in range(len(extent))]
    values = values.at[tuple(index_at)].set(least)
    longest = extent.index(max(extent))
    index_at[longest] = (index_at[longest] + 1) % extent[longest]
    return values.at[tuple(index_at)].set(high)


def level_of(stream_key, shape, split, smallest, high):
    def one(dim, shards_of):
        steps = jax.random.uniform(jax.random.fold_in(jax.random.fold_in(stream_key, 6), dim), (shards_of,), jnp.float32, smallest / len(split), high / len(split))
        return jnp.repeat(jnp.exp(steps), shape[dim] // shards_of).reshape((-1,) + (1,) * (len(shape) - dim - 1))

    level = one(*split[0])
    for cut in split[1:]:
        level = level * one(*cut)
    return level


def bell_draw(rng, shape, deviation, reach, shards=(), held_as=jnp.bfloat16):
    factor_of = level_of(rng, shape, shards, -0.22, 0.18) if shards else 1.0
    entries = jax.random.normal(rng, shape, jnp.float32) * deviation * factor_of
    return jnp.minimum(jnp.maximum(entries, -reach), reach).astype(held_as)


def setup_inputs(seed: int = 0) -> dict:
    key_list = jax.random.split(jax.random.key(seed), 19)
    features = bell_draw(key_list[0], (MICRO, TABLES, ROWS, FEAT), 1.0, 6.0, ((1, 8), (2, 4)))
    feature_mask = place_ends((jax.random.randint(key_list[1], (MICRO, TABLES, FEAT), 0, 4) < 3).astype(jnp.int32), jax.random.fold_in(key_list[1], 1), 0, 1)
    support_count = place_ends(jax.random.randint(key_list[2], (MICRO, TABLES), ROWS - ROWS_DEV + 1, ROWS), jax.random.fold_in(key_list[2], 1), ROWS - ROWS_DEV + 1, ROWS - 1).astype(jnp.int32)
    embed_weight = bell_draw(key_list[3], (FEAT, D), FEAT ** -0.5, 0.625, ((1, 8),))
    embed_bias = bell_draw(key_list[4], (D,), 0.5, 3.0, ((0, 8),))
    gain_first = jnp.clip(1.0 + 0.1 * jax.random.normal(key_list[5], (D,), jnp.float32), 0.5, 1.5).astype(jnp.bfloat16)
    shift_first = bell_draw(key_list[6], (D,), 0.3, 2.0, ((0, 8),))
    query_weight = bell_draw(key_list[7], (D, D), (D // 2) ** -0.5, 0.375, ((0, 8),))
    key_weight = bell_draw(key_list[8], (D, D), (D // 2) ** -0.5, 0.375, ((0, 8),))
    value_weight = bell_draw(key_list[9], (D, D), D ** -0.5, 0.25, ((0, 8),))
    out_weight = bell_draw(key_list[10], (D, D), (D // 32) ** -0.5, 1.5, ((0, 8),))
    gain_second = jnp.clip(1.0 + 0.1 * jax.random.normal(key_list[11], (D,), jnp.float32), 0.5, 1.5).astype(jnp.bfloat16)
    shift_second = bell_draw(key_list[12], (D,), 0.3, 2.0, ((0, 8),))
    up_weight = bell_draw(key_list[13], (D, FF), D ** -0.5, 0.25, ((0, 8),))
    up_bias = bell_draw(key_list[14], (FF,), 0.5, 3.0, ((0, 8),))
    down_weight = bell_draw(key_list[15], (FF, D), FF ** -0.5, 0.125, ((0, 8),))
    down_bias = bell_draw(key_list[16], (D,), 0.3, 2.0, ((0, 8),))
    cotangent = bell_draw(key_list[17], (MICRO, TABLES, ROWS, D), 1.0, 6.0, ((1, 8), (2, 4)))
    return {"features": features, "feature_mask": feature_mask, "support_count": support_count, "embed_weight": embed_weight, "embed_bias": embed_bias, "gain_first": gain_first, "shift_first": shift_first, "query_weight": query_weight, "key_weight": key_weight, "value_weight": value_weight, "out_weight": out_weight, "gain_second": gain_second, "shift_second": shift_second, "up_weight": up_weight, "up_bias": up_bias, "down_weight": down_weight, "down_bias": down_bias, "cotangent": cotangent}


@jax.custom_vjp
def low(v):
    return lax.optimization_barrier(v.astype(jnp.bfloat16)).astype(jnp.float32)

@jax.custom_vjp
def low_back(v):
    return v

def low_keep(v):
    return (low(v), None)

def low_pass(kept, grad):
    return (grad,)

def back_keep(v):
    return (v, None)

def back_low(kept, grad):
    return (low(grad),)
low.defvjp(low_keep, low_pass)
low_back.defvjp(back_keep, back_low)
precise = lax.Precision.HIGHEST
epsilon = 1e-05

def matmul(left_side, right_side):
    return jnp.dot(left_side, right_side, precision=precise, preferred_element_type=jnp.float32)

def layer_norm(values_in, gain_vec, shift_vec):
    row_mean = lax.optimization_barrier(jnp.mean(values_in, axis=-1, keepdims=True))
    centred = values_in - row_mean
    variance = lax.optimization_barrier(jnp.mean(centred * centred, axis=-1, keepdims=True))
    return centred * lax.rsqrt(variance + epsilon) * gain_vec + shift_vec

def forward(table_feats, mask_float, support_rows, params):
    embed_weight, embed_bias, gain_first, shift_first, query_weight, key_weight, value_weight, out_weight, gain_second, shift_second, up_weight, up_bias, down_weight, down_bias = params
    row_count = table_feats.shape[0]
    embedded = low_back(matmul(table_feats * mask_float, embed_weight) + embed_bias)
    normed = low(layer_norm(embedded, gain_first, shift_first))
    queries = low(low_back(matmul(normed, query_weight))).reshape(row_count, HEADS, HEAD_DIM)
    all_keys = low(low_back(matmul(normed, key_weight))).reshape(row_count, HEADS, HEAD_DIM)
    all_values = low(low_back(matmul(normed, value_weight))).reshape(row_count, HEADS, HEAD_DIM)
    raw_scores = jnp.einsum('rhd,lhd->hrl', queries, all_keys, precision=precise) * HEAD_DIM ** (-0.5)
    is_support = jnp.arange(row_count, dtype=jnp.int32) < support_rows
    scores = low_back(jnp.where(is_support[None, None, :], raw_scores, -1e+30))
    row_max = lax.optimization_barrier(jnp.max(scores, axis=-1, keepdims=True))
    expd = jnp.exp(scores - row_max)
    attn_low = low(expd / lax.optimization_barrier(jnp.sum(expd, axis=-1, keepdims=True)))
    mixed = jnp.einsum('hrl,lhd->rhd', attn_low, all_values, precision=precise).reshape(row_count, HEADS * HEAD_DIM)
    mixed = low(low_back(mixed))
    hidden = embedded + low_back(matmul(mixed, out_weight))
    normed_two = low(layer_norm(hidden, gain_second, shift_second))
    pre_act = low_back(matmul(normed_two, up_weight) + up_bias)
    activated = low(jax.nn.gelu(pre_act, approximate=False))
    return hidden + matmul(activated, down_weight) + down_bias

def reference(features, feature_mask, support_count, embed_weight, embed_bias, gain_first, shift_first, query_weight, key_weight, value_weight, out_weight, gain_second, shift_second, up_weight, up_bias, down_weight, down_bias, cotangent):
    params = tuple((weight.astype(jnp.float32) for weight in (embed_weight, embed_bias, gain_first, shift_first, query_weight, key_weight, value_weight, out_weight, gain_second, shift_second, up_weight, up_bias, down_weight, down_bias)))
    count_all = MICRO * TABLES
    flat_feats = features.reshape(count_all, ROWS, FEAT).astype(jnp.float32)
    flat_mask = feature_mask.reshape(count_all, FEAT).astype(jnp.float32)
    flat_support = support_count.reshape(count_all).astype(jnp.int32)
    flat_grad = cotangent.reshape(count_all, ROWS, D).astype(jnp.float32)

    def per_table(summed, inputs):
        table_feats, mask_float, support_rows, table_grad = inputs

        def apply_layer(feats_in, params_in):
            return forward(feats_in, mask_float, support_rows, params_in)
        result, pullback = jax.vjp(apply_layer, table_feats, params)
        grad_feats, grad_params = pullback(table_grad)
        summed = tuple((carried + adding for carried, adding in zip(summed, grad_params)))
        return (summed, (result.astype(jnp.bfloat16), grad_feats))
    start = tuple((jnp.zeros_like(weight) for weight in params))
    grads, (results, feat_grads) = lax.scan(per_table, start, (flat_feats, flat_mask, flat_support, flat_grad))
    activations = results.reshape(MICRO, TABLES, ROWS, D)
    input_grad = feat_grads.reshape(MICRO, TABLES, ROWS, FEAT)
    return (activations, input_grad, grads[0], grads[1], grads[2], grads[3], grads[4], grads[5], grads[6], grads[7], grads[8], grads[9], grads[10], grads[11], grads[12], grads[13])
```

```python
import functools

import jax
import jax.numpy as jnp
from jax import lax
from jax.experimental import pallas as pl
from jax.experimental.pallas import tpu as pltpu
from jax.sharding import PartitionSpec as P

HEADS = 4
HEAD_DIM = 128
LANES = 128
EPSILON = 1e-5
SCALE = HEAD_DIM**-0.5
LOG2E = 1.4426950408889634
ROW_BLOCK = 256
KEY_BLOCK = 512
INV_SQRT_TWO = 0.7071067811865476
INV_SQRT_TWO_PI = 0.3989422804014327
BF16 = jnp.bfloat16
F32 = jnp.float32
MESH = pl.DeviceIdType.MESH


def dot_nn(a, b):
    return lax.dot_general(a, b, (((1,), (0,)), ((), ())), preferred_element_type=F32)


def dot_nt(a, b):
    return lax.dot_general(a, b, (((1,), (1,)), ((), ())), preferred_element_type=F32)


def dot_tn(a, b):
    return lax.dot_general(a, b, (((0,), (0,)), ((), ())), preferred_element_type=F32)


def norm_parts(v):
    mean = jnp.mean(v, axis=-1, keepdims=True)
    centred = v - mean
    inv = lax.rsqrt(jnp.mean(centred * centred, axis=-1, keepdims=True) + EPSILON)
    return centred * inv, inv


def norm_back(grad, unit, inv, gain):
    q = grad * gain
    return inv * (
        q
        - jnp.mean(q, axis=-1, keepdims=True)
        - unit * jnp.mean(q * unit, axis=-1, keepdims=True)
    )


def row_sum(v):
    return jnp.sum(v, axis=0, keepdims=True)


def const_spec(shape):
    return pl.BlockSpec(shape, lambda *g: (0,) * len(shape))


def micro_spec(shape):
    return pl.BlockSpec((1,) + shape, lambda m, *g: (m,) + (0,) * len(shape))


def head_spec(shape):
    return pl.BlockSpec((1, 1) + shape, lambda m, h: (m, h) + (0,) * len(shape))


def head_cols_spec(rows):
    return pl.BlockSpec((1, rows, HEAD_DIM), lambda m, h: (m, 0, h))


def vmem(mib, **extra):
    return pltpu.CompilerParams(vmem_limit_bytes=mib * 2**20, **extra)


def toggled(index, hop):
    return index + hop * (1 - 2 * ((index // hop) % 2))


def toggled_by(index, hops):
    for hop in hops:
        index = toggled(index, hop)
    return index


def subsets(hops):
    out = [()]
    for hop in hops:
        out = out + [s + (hop,) for s in out]
    return out


def hops_of(size):
    return [1 << i for i in range(size.bit_length() - 1)]


class Place:
    def __init__(self, dp_size, table_size):
        self.size = {"dp": dp_size, "table": table_size}
        self.hops = {axis: hops_of(n) for axis, n in self.size.items()}
        self.me = {"dp": lax.axis_index("dp"), "table": lax.axis_index("table")}

    def partner(self, axis, hop):
        there = dict(self.me)
        there[axis] = toggled(there[axis], hop)
        return (there["dp"], there["table"])

    def signal_all(self, barrier):
        for axis in ("dp", "table"):
            for hop in self.hops[axis]:
                pl.semaphore_signal(
                    barrier, inc=1, device_id=self.partner(axis, hop), device_id_type=MESH
                )

    def wait_all(self, barrier):
        pl.semaphore_wait(barrier, len(self.hops["dp"]) + len(self.hops["table"]))


def remote(place, axis, hop, src, dst, sems, index):
    return pltpu.make_async_remote_copy(
        src_ref=src, dst_ref=dst, send_sem=sems[0].at[index], recv_sem=sems[1].at[index],
        device_id=place.partner(axis, hop), device_id_type=MESH,
    )


class Gather:
    def __init__(self, place, axis, hops, full, sems, base, own=None):
        self.place, self.axis, self.hops = place, axis, hops
        self.full, self.sems, self.base, self.own = full, sems, base, own
        self.steps = len(hops)

    def whole(self, step):
        part = self.full.at[pl.ds(0, 1 << step)]
        return remote(self.place, self.axis, self.hops[step], part, part, self.sems, self.base + step)

    def start(self, step):
        for s in subsets(self.hops[:step]):
            block = self.full.at[toggled_by(self.place.me[self.axis], s)]
            src = block if s or self.own is None else self.own
            remote(
                self.place, self.axis, self.hops[step], src, block, self.sems, self.base + step
            ).start()

    def arrive(self, step):
        self.whole(step).wait_recv()

    def sent(self):
        for step in range(self.steps):
            self.whole(step).wait_send()


def add_into(into, other):
    lead = into.shape[:-2]
    rows, cols = into.shape[-2:]
    if lead:
        for i in range(lead[0]):
            add_into(into.at[i], other.at[i])
        return
    piece = min(rows, max(16, 65536 // cols))
    piece = rows if rows % piece else piece

    def body(i, carry):
        at = pl.ds(pl.multiple_of(i * piece, piece), piece)
        into[at, :] = (into[at, :].astype(F32) + other[at, :].astype(F32)).astype(into.dtype)
        return carry

    if rows == piece:
        into[...] = (into[...].astype(F32) + other[...].astype(F32)).astype(into.dtype)
    else:
        lax.fori_loop(0, rows // piece, body, 0)


class Reduce:
    def __init__(self, place, axis, hops, blocks, bufs, sems, base, near=None):
        self.place, self.axis, self.hops = place, axis, hops
        self.held, self.near = blocks, near
        self.bufs, self.sems, self.base = bufs, sems, base
        self.steps = len(hops)

    def mine(self, step, s):
        if step == 0:
            return self.held(s)
        order = [set(t) for t in subsets(self.hops[step:])]
        return self.bufs[step - 1].at[order.index(set(s))]

    def copy(self, step, src, dst):
        return remote(self.place, self.axis, self.hops[step], src, dst, self.sems, self.base + step)

    def start(self, step):
        for i, s in enumerate(subsets(self.hops[step + 1 :])):
            self.copy(step, self.mine(step, s + (self.hops[step],)), self.bufs[step].at[i]).start()

    def arrive(self, step):
        self.copy(step, self.bufs[step], self.bufs[step]).wait_recv()
        for i, s in enumerate(subsets(self.hops[step + 1 :])):
            near = step == 0 and self.near is not None
            add_into(self.bufs[step].at[i], self.near.at[i] if near else self.mine(step, s))

    def total(self):
        return self.bufs[-1].at[0]

    def sent(self):
        for step in range(self.steps):
            self.copy(step, self.bufs[step], self.bufs[step]).wait_send()


class Shard:
    def __init__(self, place, dp_hops, grad, scratch, sems, base, near=None):
        n, m = len(dp_hops), len(place.hops["table"])
        dp_bufs, table_bufs, full = scratch[:n], scratch[n : n + m], scratch[n + m]
        self.place, self.grad, self.near = place, grad, near

        def blocks(s):
            return grad.at[toggled_by(place.me["dp"], s)]

        self.dp = Reduce(place, "dp", dp_hops, blocks, dp_bufs, sems, base, near)
        table_hops = place.hops["table"]
        base += self.dp.steps

        def parts(s):
            return self.dp.total().at[toggled_by(place.me["table"], s)]

        self.table = Reduce(place, "table", table_hops, parts, table_bufs, sems, base)
        base += self.table.steps
        self.full = full
        self.back = Gather(place, "table", table_hops[::-1], full, sems, base)
        self.flows = [(f, i) for f in (self.dp, self.table, self.back) for i in range(f.steps)]
        self.steps = len(self.flows)

    def near_copies(self, sem):
        halves = subsets(self.dp.hops[1:])
        return [
            pltpu.make_async_copy(self.dp.held(s), self.near.at[i], sem) for i, s in enumerate(halves)
        ]

    def near_wait(self, sem):
        pltpu.make_async_copy(self.near, self.near, sem).wait()

    def start(self, step):
        flow, i = self.flows[step]
        if flow is self.back and i == 0:
            self.full[self.place.me["table"]] = self.table.total()[...]
        flow.start(i)

    def arrive(self, step):
        flow, i = self.flows[step]
        flow.arrive(i)

    def sent(self):
        for flow in (self.dp, self.table, self.back):
            flow.sent()


class Total:
    def __init__(self, place, hops, sums, got, sems, base):
        self.place, self.hops, self.sums, self.got = place, hops, sums, got
        self.sems, self.base, self.steps = sems, base, len(hops)

    def copy(self, step):
        axis, hop = self.hops[step]
        return remote(
            self.place, axis, hop, self.sums.at[step], self.got.at[step], self.sems, self.base + step
        )

    def start(self, step):
        self.copy(step).start()

    def arrive(self, step):
        self.copy(step).wait_recv()
        self.sums[step + 1] = self.sums[step] + self.got[step]

    def sent(self):
        for step in range(self.steps):
            self.copy(step).wait_send()


def shard_scratch(dp_size, table_size, block, dtype):
    out = [pltpu.VMEM((dp_size >> (i + 1),) + block, dtype) for i in range(len(hops_of(dp_size)))]
    out += [
        pltpu.VMEM((table_size >> (i + 1),) + block[1:], dtype) for i in range(len(hops_of(table_size)))
    ]
    out.append(pltpu.VMEM(block, dtype))
    return out


def attend_core(
    support, get_x, own_x, wet_ref, vec_ref, wq, wk, wv,
    q_ref, k_ref, v_ref, n_ref, u_ref, inv_ref, emb_ref, mixed_ref, p_ref, linv_ref,
):
    length, rows = n_ref.shape[1], q_ref.shape[1]
    own = lax.axis_index("table") * rows
    bias, gain, shift = vec_ref[0:1, :], vec_ref[1:2, :], vec_ref[2:3, :]
    chunk = 256

    @pl.when(pl.program_id(1) == 0)
    def _():
        def project(i, carry):
            at = pl.ds(pl.multiple_of(i * chunk, chunk), chunk)
            embedded = dot_nt(get_x(i, chunk), wet_ref[...]) + bias
            unit, inv = norm_parts(embedded)
            normed = (unit * gain + shift).astype(BF16)
            n_ref[0, at, :] = normed
            u_ref[0, at, :] = unit.astype(BF16)
            inv_ref[0, at, :] = jnp.broadcast_to(inv, (chunk, LANES))
            k_ref[0, at, :] = dot_nn(normed, wk()).astype(BF16)
            v_ref[0, at, :] = dot_nn(normed, wv()).astype(BF16)
            return carry

        lax.fori_loop(0, length // chunk, project, 0, unroll=2)
        here = pl.ds(pl.multiple_of(own, rows), rows)
        emb_ref[0] = dot_nt(own_x(), wet_ref[...]) + bias
        q_ref[0] = dot_nn(n_ref[0, here, :], wq()).astype(BF16)

    block = ROW_BLOCK
    sure = length - rows
    columns = sure + lax.broadcasted_iota(jnp.int32, (1, rows), 1)
    allowed = columns < support
    cols = pl.ds(pl.multiple_of(pl.program_id(1) * HEAD_DIM, HEAD_DIM), HEAD_DIM)

    for i in range(rows // block):
        at = slice(i * block, (i + 1) * block)
        qh = q_ref[0, at, cols]
        first = dot_nt(qh, k_ref[0, :sure, cols])
        last = dot_nt(qh, k_ref[0, sure:, cols])
        last = jnp.where(allowed, last, -1e30)
        top = jnp.maximum(
            jnp.max(first, axis=-1, keepdims=True), jnp.max(last, axis=-1, keepdims=True)
        )
        pf = jnp.exp2((first - top) * (SCALE * LOG2E))
        pt = jnp.exp2((last - top) * (SCALE * LOG2E))
        total = jnp.sum(pf, axis=-1, keepdims=True) + jnp.sum(pt, axis=-1, keepdims=True)
        pf, pt = pf.astype(BF16), pt.astype(BF16)
        p_ref[0, 0, at, :sure] = pf
        p_ref[0, 0, at, sure:] = pt
        linv = 1.0 / total
        linv_ref[0, 0, at, :] = jnp.broadcast_to(linv, (block, LANES))
        out = dot_nn(pf, v_ref[0, :sure, cols]) + dot_nn(pt, v_ref[0, sure:, cols])
        mixed_ref[0, at, cols] = out * linv


def attend_kernel(support_ref, x_ref, wet_ref, vec_ref, wq_ref, wk_ref, wv_ref, *outs):
    rows = outs[0].shape[1]
    own = lax.axis_index("table") * rows

    def get_x(i, chunk):
        return x_ref[0, pl.ds(pl.multiple_of(i * chunk, chunk), chunk), :]

    attend_core(
        support_ref[pl.program_id(0)],
        get_x,
        lambda: x_ref[0, pl.ds(pl.multiple_of(own, rows), rows), :],
        wet_ref, vec_ref, lambda: wq_ref[...], lambda: wk_ref[...], lambda: wv_ref[...], *outs,
    )


def attend_gather_kernel(
    dp_size, table_size, support_ref, feat_ref, mask_ref, ew_ref, packed_ref, wq_in, wk_in, wv_in, wo_in, wu_in, wd_in,
    q_ref, k_ref, v_ref, n_ref, u_ref, inv_ref, emb_ref, mixed_ref, p_ref, linv_ref,
    x_out, wet_out, wq_out, wk_out, wv_out, vec_ref, bu_ref, wo_out, wu_out, wd_out,
    x_buf, wet_buf, packed_buf, wq_buf, wk_buf, wv_buf, own_sem, send_sem, recv_sem,
):
    micro_id, head = pl.program_id(0), pl.program_id(1)
    micro, rows, feat = feat_ref.shape
    shard = wq_in.shape[0]
    width = wq_in.shape[1]
    place = Place(dp_size, table_size)
    dp, table = place.me["dp"], place.me["table"]
    sems = (send_sem, recv_sem)
    hops = place.hops["dp"]
    forth, back = hops[1:] + hops[:1], hops[:0:-1] + hops[:1]
    base = 0

    def gather(axis, order, full, own=None):
        nonlocal base
        flow = Gather(place, axis, order, full, sems, base, own)
        base += flow.steps
        return flow

    table_order = place.hops["table"][::-1]
    feats = [gather("table", table_order, x_buf.at[m]) for m in range(micro)]
    early = [
        gather("dp", forth, wk_buf),
        gather("dp", back, wv_buf),
        gather("dp", forth, wet_buf),
        gather("dp", back, packed_buf),
        gather("dp", back, wq_buf),
    ]
    late = [
        gather("dp", forth, wo_out, wo_in),
        gather("dp", forth, wu_out, wu_in),
        gather("dp", back, wd_out, wd_in),
    ]
    own_copies = [
        pltpu.make_async_copy(src, dst.at[dp], own_sem.at[i])
        for i, (src, dst) in enumerate(((wo_in, wo_out), (wu_in, wu_out), (wd_in, wd_out)))
    ]
    out_copies = [
        pltpu.make_async_copy(src, dst, own_sem.at[3 + i])
        for i, (src, dst) in enumerate(
            ((wet_buf, wet_out), (wq_buf, wq_out), (wk_buf, wk_out), (wv_buf, wv_out))
        )
    ]

    def at_step(m, h):
        return pl.when((micro_id == m) & (head == h))

    @at_step(0, 0)
    def _():
        barrier = pltpu.get_barrier_semaphore()
        place.signal_all(barrier)
        for m in range(micro):
            mask = mask_ref[m].astype(F32)
            x_buf[m, table] = jnp.zeros((rows, LANES), BF16)
            x_buf[m, table, :, :feat] = (feat_ref[m].astype(F32) * mask).astype(BF16)
        tall = jnp.concatenate(
            [ew_ref[...].astype(F32), jnp.zeros((LANES - feat, shard), F32)], axis=0
        )
        wet_buf[dp] = tall.T.astype(BF16)
        packed_buf[dp] = packed_ref[...]
        wq_buf[dp] = wq_in[...]
        wk_buf[dp] = wk_in[...]
        wv_buf[dp] = wv_in[...]
        place.wait_all(barrier)
        feats[0].start(0)
        for flow in early:
            flow.start(0)
        for copy in own_copies:
            copy.start()
        for step in range(1, len(hops)):
            if step < feats[0].steps:
                feats[0].arrive(step - 1)
                feats[0].start(step)
            for flow in early:
                flow.arrive(step - 1)
                flow.start(step)
        for flow in early:
            flow.arrive(len(hops) - 1)
        for flow in late:
            flow.start(0)
        feats[0].arrive(feats[0].steps - 1)
        if micro > 1:
            feats[1].start(0)
        for copy in out_copies:
            copy.start()
        lane = lax.broadcasted_iota(jnp.int32, (8, LANES), 1)
        for d in range(0, dp_size, 2):
            pair = jnp.where(lane < shard, packed_buf[d], pltpu.roll(packed_buf[d + 1], shard, 1))
            vec_ref[:, d * shard : (d + 2) * shard] = pair
        for d in range(dp_size):
            bu_ref[:, 2 * d * LANES : (2 * d + 1) * LANES] = packed_buf[d, 6:7, :]
            bu_ref[:, (2 * d + 1) * LANES : (2 * d + 2) * LANES] = packed_buf[d, 7:8, :]

    @at_step(0, 1)
    def _():
        for flow in late:
            flow.arrive(0)
            flow.start(1)
        feats[1].arrive(0)
        feats[1].start(1)

    @at_step(1, 0)
    def _():
        feats[1].arrive(1)
        feats[2].start(0)

    @at_step(1, 1)
    def _():
        for flow in late:
            flow.arrive(1)
            flow.start(2)
        feats[2].arrive(0)
        feats[2].start(1)

    @at_step(2, 0)
    def _():
        feats[2].arrive(1)
        for flow in late:
            flow.arrive(2)

    def get_x(i, chunk):
        per = rows // chunk
        x = x_buf[micro_id, i // per, pl.ds(pl.multiple_of((i % per) * chunk, chunk), chunk), :]
        x_out[0, pl.ds(pl.multiple_of(i * chunk, chunk), chunk), :] = x
        return x

    def full(buf):
        return lambda: buf[...].reshape(width, width)

    attend_core(
        support_ref[micro_id], get_x, lambda: x_buf[micro_id, table], WetView(wet_buf), vec_ref,
        full(wq_buf), full(wk_buf), full(wv_buf),
        q_ref, k_ref, v_ref, n_ref, u_ref, inv_ref, emb_ref, mixed_ref, p_ref, linv_ref,
    )

    @at_step(micro - 1, HEADS - 1)
    def _():
        for flow in feats + early + late:
            flow.sent()
        for copy in own_copies + out_copies:
            copy.wait()


class WetView:
    def __init__(self, buf):
        self.buf = buf

    def __getitem__(self, _):
        return self.buf[...].reshape(-1, self.buf.shape[-1])


def attend_shapes(rows, length, width):
    out = [
        ((rows, width), BF16),
        ((length, width), BF16),
        ((length, width), BF16),
        ((length, width), BF16),
        ((length, width), BF16),
        ((length, LANES), F32),
        ((rows, width), F32),
        ((rows, width), F32),
    ]
    return out, [((rows, length), BF16), ((rows, LANES), F32)]


def attend_forward_gather(dp_size, table_size, support, feat, mask, ew, packed, wq, wk, wv, wo, wu, wd):
    micro, rows, _ = feat.shape
    length = rows * table_size
    width = wq.shape[1]
    out, heads = attend_shapes(rows, length, width)
    whole = pl.BlockSpec(memory_space=pltpu.VMEM)
    far = pl.BlockSpec(memory_space=pl.ANY)

    def gathered(a):
        return jax.ShapeDtypeStruct((dp_size,) + a.shape, a.dtype)

    wet = jax.ShapeDtypeStruct((dp_size, wq.shape[0], LANES), BF16)
    steps = len(hops_of(dp_size))
    table_steps = len(hops_of(table_size))
    count = micro * table_steps + 8 * steps
    return pl.pallas_call(
        functools.partial(attend_gather_kernel, dp_size, table_size),
        grid=(micro, HEADS),
        in_specs=[pl.BlockSpec(memory_space=pltpu.SMEM)] + [whole] * 7 + [far] * 3,
        out_specs=[micro_spec(s) for s, _ in out]
        + [head_spec(s) for s, _ in heads]
        + [micro_spec((length, LANES))]
        + [far] * 4
        + [const_spec((8, width)), const_spec((1, wu.shape[1]))]
        + [far] * 3,
        out_shape=[jax.ShapeDtypeStruct((micro,) + s, d) for s, d in out]
        + [jax.ShapeDtypeStruct((micro, HEADS) + s, d) for s, d in heads]
        + [jax.ShapeDtypeStruct((micro, length, LANES), BF16)]
        + [wet, gathered(wq), gathered(wk), gathered(wv)]
        + [jax.ShapeDtypeStruct((8, width), F32), jax.ShapeDtypeStruct((1, wu.shape[1]), F32)]
        + [gathered(wo), gathered(wu), gathered(wd)],
        scratch_shapes=[
            pltpu.VMEM((micro, table_size, rows, LANES), BF16),
            pltpu.VMEM(wet.shape, BF16),
            pltpu.VMEM((dp_size,) + packed.shape, F32),
            pltpu.VMEM((dp_size,) + wq.shape, BF16),
            pltpu.VMEM((dp_size,) + wk.shape, BF16),
            pltpu.VMEM((dp_size,) + wv.shape, BF16),
            pltpu.SemaphoreType.DMA((7,)),
            pltpu.SemaphoreType.DMA((count,)),
            pltpu.SemaphoreType.DMA((count,)),
        ],
        compiler_params=vmem(54, collective_id=0, has_side_effects=True),
        name="attend_forward_gather",
    )(support, feat, mask, ew, packed, wq, wk, wv, wo, wu, wd)


def attend_forward(support, x_all, wet, vec, wq, wk, wv, rows):
    micro, length, lanes = x_all.shape
    width = wq.shape[0]
    out, heads = attend_shapes(rows, length, width)
    return pl.pallas_call(
        attend_kernel,
        grid=(micro, HEADS),
        in_specs=[
            pl.BlockSpec(memory_space=pltpu.SMEM),
            micro_spec((length, lanes)),
            const_spec(wet.shape),
            const_spec(vec.shape),
            const_spec(wq.shape),
            const_spec(wk.shape),
            const_spec(wv.shape),
        ],
        out_specs=[micro_spec(s) for s, _ in out] + [head_spec(s) for s, _ in heads],
        out_shape=[jax.ShapeDtypeStruct((micro,) + s, d) for s, d in out]
        + [jax.ShapeDtypeStruct((micro, HEADS) + s, d) for s, d in heads],
        compiler_params=vmem(50),
        name="attend_forward",
    )(support, x_all, wet, vec, wq, wk, wv)


def mlp_kernel(
    mixed_ref, emb_ref, cot_ref, wo_ref, wu_ref, wd_ref, vec_ref, bu_ref,
    act_ref, ghid_ref, gmix_ref, dwo_ref, dwu_ref, dwd_ref, dvec_ref,
    acc_o, acc_u, acc_d, gn2_ref, out_ref,
):
    step, last = pl.program_id(0), pl.num_programs(0) - 1
    hidden_units = wu_ref.shape[1]
    chunk = 512

    @pl.when(step == 0)
    def _():
        acc_o[...] = jnp.zeros_like(acc_o)
        acc_u[...] = jnp.zeros_like(acc_u)
        acc_d[...] = jnp.zeros_like(acc_d)
        dvec_ref[...] = jnp.zeros_like(dvec_ref)

    gain, shift, dbias = vec_ref[3:4, :], vec_ref[4:5, :], vec_ref[5:6, :]
    mixed = mixed_ref[0].astype(BF16)
    g_out = cot_ref[0]
    hidden = emb_ref[0] + dot_nn(mixed, wo_ref[...])
    unit, inv = norm_parts(hidden)
    normed = (unit * gain + shift).astype(BF16)
    out_ref[...] = hidden + dbias
    normed_t = normed.T
    g_out_t = g_out.T
    for f in range(hidden_units // chunk):
        cols = slice(f * chunk, (f + 1) * chunk)
        pre = dot_nn(normed, wu_ref[:, cols]) + bu_ref[:, cols]
        cdf = 0.5 * (1.0 + lax.erf(pre * INV_SQRT_TWO))
        pdf = jnp.exp(-0.5 * pre * pre) * INV_SQRT_TWO_PI
        act = (pre * cdf).astype(BF16)
        out_ref[...] += dot_nn(act, wd_ref[cols, :])
        g_act = dot_nt(g_out, wd_ref[cols, :])
        g_pre_f = g_act * (cdf + pre * pdf)
        g_pre = g_pre_f.astype(BF16)
        acc_u[:, cols] += dot_nn(normed_t, g_pre)
        acc_d[:, cols] += dot_nn(g_out_t, act)
        dvec_ref[8 + f : 9 + f, :] += row_sum(g_pre_f)
        g_part = dot_nt(g_pre, wu_ref[:, cols])
        if f == 0:
            gn2_ref[...] = g_part
        else:
            gn2_ref[...] += g_part
    act_ref[0] = out_ref[...].astype(BF16)
    g_norm = gn2_ref[...]
    g_out_f = g_out.astype(F32)
    dvec_ref[3:4, :] += row_sum(g_norm * unit)
    dvec_ref[4:5, :] += row_sum(g_norm)
    dvec_ref[5:6, :] += row_sum(g_out_f)
    g_hidden = g_out_f + norm_back(g_norm, unit, inv, gain)
    ghid_ref[0] = g_hidden
    branch = g_hidden.astype(BF16)
    acc_o[...] += dot_tn(mixed, branch)
    gmix_ref[0] = dot_nt(branch, wo_ref[...]).astype(BF16)

    @pl.when(step == last)
    def _():
        dwo_ref[...] = acc_o[...].astype(BF16)
        dwu_ref[...] = acc_u[...].astype(BF16)
        for f in range(hidden_units // chunk):
            cols = slice(f * chunk, (f + 1) * chunk)
            dwd_ref[cols, :] = acc_d[:, cols].T.astype(BF16)


def mlp_both(mixed, emb, cot, wo, wu, wd, vec, bu):
    micro, rows, width = mixed.shape
    hidden_units = wu.shape[1]
    per_micro = [((rows, width), BF16), ((rows, width), F32), ((rows, width), BF16)]
    summed = [
        ((width, width), BF16),
        ((width, hidden_units), BF16),
        ((hidden_units, width), BF16),
        ((16, width), F32),
    ]
    return pl.pallas_call(
        mlp_kernel,
        grid=(micro,),
        in_specs=[micro_spec((rows, width))] * 3
        + [const_spec(a.shape) for a in (wo, wu, wd, vec, bu)],
        out_specs=[micro_spec(s) for s, _ in per_micro] + [const_spec(s) for s, _ in summed],
        out_shape=[jax.ShapeDtypeStruct((micro,) + s, d) for s, d in per_micro]
        + [jax.ShapeDtypeStruct(s, d) for s, d in summed],
        scratch_shapes=[
            pltpu.VMEM((width, width), F32),
            pltpu.VMEM((width, hidden_units), F32),
            pltpu.VMEM((width, hidden_units), F32),
            pltpu.VMEM((rows, width), F32),
            pltpu.VMEM((rows, width), F32),
        ],
        compiler_params=vmem(50),
        name="mlp_both",
    )(mixed, emb, cot, wo, wu, wd, vec, bu)


def attend_back_core(
    hooks, p_ref, linv_ref, k_ref, v_ref, q_ref, gmix_ref, mixed_ref, n_ref, u_ref, inv_ref, x_ref, ghid_ref,
    mask_ref, wet_ref, vec_ref, wq_ref, wk_ref, wv_ref,
    dvec_ref, dkv_ref, dq_ref, ig_acc, wkv_t, acc_e, acc_q, acc_kv,
):
    step, head = pl.program_id(0), pl.program_id(1)
    length, rows, width = n_ref.shape[1], dq_ref.shape[0], dq_ref.shape[1]
    own = lax.axis_index("table") * rows
    here = pl.ds(pl.multiple_of(own, rows), rows)

    @pl.when((step == 0) & (head == 0))
    def _():
        acc_e[...] = jnp.zeros_like(acc_e)
        acc_q[...] = jnp.zeros_like(acc_q)
        acc_kv[...] = jnp.zeros_like(acc_kv)
        dvec_ref[...] = jnp.zeros_like(dvec_ref)
        wkv_t[:width, :] = wk_ref[...].T
        wkv_t[width:, :] = wv_ref[...].T

    keys = KEY_BLOCK
    linv = linv_ref[0, 0][:, :1]
    g_low = (gmix_ref[0].astype(F32) * linv).astype(BF16)
    delta = jnp.sum(mixed_ref[0] * g_low.astype(F32), axis=-1, keepdims=True)
    g_low_t = g_low.T
    q_t = q_ref[0].T
    k_rows = pl.ds(pl.multiple_of(head * HEAD_DIM, HEAD_DIM), HEAD_DIM)
    v_rows = pl.ds(pl.multiple_of(width + head * HEAD_DIM, HEAD_DIM), HEAD_DIM)
    dq = None
    for j in range(length // keys):
        at = slice(j * keys, (j + 1) * keys)
        p = p_ref[0, 0, :, at]
        dp = dot_nt(g_low, v_ref[0, at, :])
        ds = (p.astype(F32) * (dp - delta)).astype(BF16)
        dkv_ref[v_rows, at] = dot_nn(g_low_t, p).astype(BF16)
        dkv_ref[k_rows, at] = (dot_nn(q_t, ds) * SCALE).astype(BF16)
        dq_part = dot_nn(ds, k_ref[0, at, :])
        dq = dq_part if dq is None else dq + dq_part
    dq_ref[:, k_rows] = (dq * SCALE).astype(BF16)

    @pl.when(head == HEADS - 1)
    def _():
        gain = vec_ref[1:2, :]
        mask = mask_ref[0].astype(F32)
        part = 256
        for i in range(2 * width // part):
            at = slice(i * part, (i + 1) * part)
            acc_kv[at, :] += dot_nn(dkv_ref[at, :], n_ref[0])
        dq = dq_ref[...]
        acc_q[...] += dot_tn(n_ref[0, here, :], dq)
        hooks.projections_done()

        def embed_back(g_norm, unit, inv, extra, x):
            dvec_ref[1:2, :] += row_sum(g_norm * unit)
            dvec_ref[2:3, :] += row_sum(g_norm)
            g_emb = norm_back(g_norm, unit, inv, gain)
            if extra is not None:
                g_emb = g_emb + extra
            dvec_ref[0:1, :] += row_sum(g_emb)
            g_emb = g_emb.astype(BF16)
            acc_e[...] += dot_tn(x, g_emb)
            return dot_nn(g_emb, wet_ref[...]) * mask

        def others(i, carry):
            at = pl.ds(pl.multiple_of(i * part, part), part)
            g_norm = dot_tn(dkv_ref[:, at], wkv_t[...])
            ig_acc[at, :] = embed_back(
                g_norm, u_ref[0, at, :].astype(F32), inv_ref[0, at, :][:, :1], None, x_ref[0, at, :]
            )
            return carry

        count = length // part
        groups = 4
        for g in range(groups):
            lax.fori_loop(g * count // groups, (g + 1) * count // groups, others, 0, unroll=2)
            hooks.group_done(g)
        ig_acc[here, :] += embed_back(
            dot_nt(dq, wq_ref[...]),
            u_ref[0, here, :].astype(F32),
            inv_ref[0, here, :][:, :1],
            ghid_ref[0],
            x_ref[0, here, :],
        )
        hooks.rows_done()


class Alone:
    def __init__(self, ig_ref, ig_acc):
        self.ig_ref, self.ig_acc = ig_ref, ig_acc

    def projections_done(self):
        pass

    def group_done(self, g):
        pass

    def rows_done(self):
        self.ig_ref[0] = self.ig_acc[...].astype(BF16)


def attend_back_kernel(*refs):
    ins, rest = refs[:18], refs[18:]
    ig_ref, dwe_ref, dwq_ref, dwk_ref, dwv_ref, dvec_ref = rest[:6]
    scratch = rest[6:]
    ig_acc, acc_e, acc_q, acc_kv = scratch[2], scratch[4], scratch[5], scratch[6]
    width = acc_q.shape[0]
    attend_back_core(Alone(ig_ref, ig_acc), *ins, dvec_ref, *scratch)

    @pl.when((pl.program_id(0) == pl.num_programs(0) - 1) & (pl.program_id(1) == HEADS - 1))
    def _():
        dwe_ref[...] = acc_e[...].T.astype(BF16)
        dwq_ref[...] = acc_q[...].astype(BF16)
        dwk_ref[...] = acc_kv[:width, :].T.astype(BF16)
        dwv_ref[...] = acc_kv[width:, :].T.astype(BF16)


class Sums:
    def __init__(self, mlp, tail, small, igs, ig_bufs, ig_out, near_sem, write_tail, write_embed, write_small):
        self.mlp, self.tail, self.small, self.igs = mlp, tail, small, igs
        self.ig_bufs, self.ig_out, self.near_sem = ig_bufs, ig_out, near_sem
        self.write_tail, self.write_embed, self.write_small = write_tail, write_embed, write_small
        self.micro, self.head = pl.program_id(0), pl.program_id(1)
        self.count = len(igs)

    def at(self, m, h):
        return pl.when((self.micro == m) & (self.head == h))

    def mlp_step(self, i):
        for flow in self.mlp:
            if i:
                flow.arrive(i - 1)
            if i < flow.steps:
                flow.start(i)

    def ig_step(self, m, i):
        flow = self.igs[m]
        if i:
            flow.arrive(i - 1)
        if i < flow.steps:
            flow.start(i)
        else:
            self.ig_out[m] = flow.total()[...].astype(F32)

    def ticks(self, place):
        @self.at(0, 0)
        def _():
            barrier = pltpu.get_barrier_semaphore()
            place.signal_all(barrier)
            for i, flow in enumerate(self.mlp):
                for copy in flow.near_copies(self.near_sem.at[i]):
                    copy.start()
            place.wait_all(barrier)
            self.mlp_step(0)

        @self.at(0, 1)
        def _():
            for i, flow in enumerate(self.mlp):
                flow.near_wait(self.near_sem.at[i])
            self.mlp_step(1)

        @self.at(1, 0)
        def _():
            self.mlp_step(2)

        @self.at(1, 2)
        def _():
            self.ig_step(0, 1)
            self.mlp_step(3)

        @self.at(2, 0)
        def _():
            self.mlp_step(5)

        @self.at(2, 2)
        def _():
            self.ig_step(1, 1)

        @self.at(2, 3)
        def _():
            self.mlp_step(6)

    def last(self):
        return pl.when(self.micro == self.count - 1)

    def projections_done(self):
        @pl.when(self.micro == 1)
        def _():
            self.ig_step(0, 2)
            self.mlp_step(4)

        @self.last()
        def _():
            self.ig_step(1, 2)
            self.write_tail()
            for flow in self.tail[1:]:
                flow.start(0)

    def group_done(self, g):
        step = {0: 1, 1: 2, 3: 3}.get(g)
        if step is None:
            return

        @self.last()
        def _():
            for flow in self.tail[1:]:
                flow.arrive(step - 1)
                flow.start(step)

    def rows_done(self):
        for m in range(self.count):

            @pl.when(self.micro == m)
            def _():
                self.ig_bufs[m][...] = self.ig_value()
                self.ig_step(m, 0)

        @self.last()
        def _():
            self.write_embed()
            self.write_small()
            first, others = self.tail[0], self.tail[1:]
            done = 3
            lagging = [first, self.small]
            m = self.count - 1
            for i in range(first.steps + 1):
                for flow in lagging:
                    if 0 < i <= flow.steps:
                        flow.arrive(i - 1)
                    if i < flow.steps:
                        flow.start(i)
                if 0 < i <= self.igs[m].steps:
                    self.ig_step(m, i)
                if done < others[0].steps:
                    for flow in others:
                        flow.arrive(done)
                        if done + 1 < flow.steps:
                            flow.start(done + 1)
                    done += 1
                if i == 0:
                    self.mlp_step(7)
            for flow in self.mlp + self.tail + [self.small] + self.igs:
                flow.sent()


def attend_back_reduce_kernel(dp_size, table_size, *refs):
    refs = list(refs)

    def take(n):
        out = refs[:n]
        del refs[:n]
        return out

    ins = take(18)
    grads = take(3)
    (small_in,) = take(1)
    ig_out, small_out = take(2)
    totals = take(7)
    (dvec_ref,) = take(1)
    core = take(7)
    ig_acc, acc_e, acc_q, acc_kv = core[2], core[4], core[5], core[6]
    width = acc_q.shape[0]
    place = Place(dp_size, table_size)
    steps = len(place.hops["dp"]) + len(place.hops["table"]) + 1
    nears = take(3)
    mlp_scratch = [take(steps) for _ in range(3)]
    tail_grads = take(4)
    tail_scratch = [take(steps) for _ in range(4)]
    sums, got = take(2)
    micro = ig_out.shape[0]
    ig_bufs = take(micro)
    ig_scratch = [take(len(place.hops["table"])) for _ in range(micro)]
    near_sem, send_sem, recv_sem = refs
    sems = (send_sem, recv_sem)
    hops = place.hops["dp"]
    forth, back = hops, hops[:1] + hops[:0:-1]
    base = 0

    def shard(order, grad, scratch, near=None):
        nonlocal base
        flow = Shard(place, order, grad, scratch, sems, base, near)
        base += flow.steps
        return flow

    mlp = [shard(o, g, s, n) for o, g, s, n in zip((forth, forth, back), grads, mlp_scratch, nears)]
    tail = [shard(o, g, s) for o, g, s in zip((forth, back, forth, back), tail_grads, tail_scratch)]
    both = [("dp", hop) for hop in hops] + [("table", hop) for hop in place.hops["table"]]
    small = Total(place, both, sums, got, sems, base)
    base += small.steps
    igs = []
    for m in range(micro):
        buf = ig_bufs[m]
        igs.append(
            Reduce(
                place, "table", place.hops["table"],
                lambda s, buf=buf: buf.at[toggled_by(place.me["table"], s)],
                ig_scratch[m], sems, base,
            )
        )
        base += igs[-1].steps

    def write_tail():
        tail_grads[1][...] = acc_q[...].astype(BF16).reshape(tail_grads[1].shape)
        tail_grads[2][...] = acc_kv[:width, :].T.astype(BF16).reshape(tail_grads[2].shape)
        tail_grads[3][...] = acc_kv[width:, :].T.astype(BF16).reshape(tail_grads[3].shape)

    def write_embed():
        tail_grads[0][...] = acc_e[...].T.astype(BF16).reshape(tail_grads[0].shape)

    def write_small():
        sums[0] = small_in[...] + jnp.concatenate([dvec_ref[...], jnp.zeros_like(dvec_ref)], axis=0)

    hooks = Sums(
        mlp, tail, small, igs, ig_bufs, ig_out, near_sem, write_tail, write_embed, write_small
    )
    hooks.ig_value = lambda: ig_acc[...].astype(BF16).reshape(ig_bufs[0].shape)
    hooks.ticks(place)
    attend_back_core(hooks, *ins, dvec_ref, *core)

    @hooks.at(micro - 1, HEADS - 1)
    def _():
        for flow, out in zip(tail + mlp, totals):
            out[...] = flow.full[...]
        small_out[...] = sums[small.steps]


def back_scratch(length, rows, width):
    return [
        pltpu.VMEM((2 * width, length), BF16),
        pltpu.VMEM((rows, width), BF16),
        pltpu.VMEM((length, LANES), F32),
        pltpu.VMEM((2 * width, width), BF16),
        pltpu.VMEM((LANES, width), F32),
        pltpu.VMEM((width, width), F32),
        pltpu.VMEM((2 * width, width), F32),
    ]


def back_specs(by_head, cols, varied, fixed):
    return (
        [head_spec(a.shape[2:]) for a in by_head]
        + [head_cols_spec(a.shape[1]) for a in cols]
        + [micro_spec(a.shape[1:]) for a in varied]
        + [const_spec(a.shape) for a in fixed]
    )


def attend_backward(p, linv, k, v, q, gmix, mixed, n, u, inv, x, ghid, mask, wet, vec, wq, wk, wv):
    micro, rows, width = q.shape
    length = k.shape[1]
    varied = (n, u, inv, x, ghid, mask)
    fixed = (wet, vec, wq, wk, wv)
    summed = [(wet.shape, BF16)] + [((width, width), BF16)] * 3 + [((8, width), F32)]
    return pl.pallas_call(
        attend_back_kernel,
        grid=(micro, HEADS),
        in_specs=back_specs((p, linv), (k, v, q, gmix, mixed), varied, fixed),
        out_specs=[micro_spec((length, LANES))] + [const_spec(s) for s, _ in summed],
        out_shape=[jax.ShapeDtypeStruct((micro, length, LANES), BF16)]
        + [jax.ShapeDtypeStruct(s, d) for s, d in summed],
        scratch_shapes=back_scratch(length, rows, width),
        compiler_params=vmem(50),
        name="attend_backward",
    )(p, linv, k, v, q, gmix, mixed, *varied, *fixed)


def attend_backward_reduce(
    dp_size, table_size, grads, small, p, linv, k, v, q, gmix, mixed, n, u, inv, x, ghid, mask, wet, vec, wq, wk, wv
):
    micro, rows, width = q.shape
    length = k.shape[1]
    varied = (n, u, inv, x, ghid, mask)
    fixed = (wet, vec, wq, wk, wv)
    far = pl.BlockSpec(memory_space=pl.ANY)
    tail = [(dp_size, table_size, width // dp_size // table_size, c) for c in (LANES, width, width, width)]
    blocks = [t[1:] for t in tail] + [g.shape[1:] for g in grads]
    hops = len(hops_of(dp_size)) + len(hops_of(table_size))
    table_hops = hops_of(table_size)
    scratch = [pltpu.VMEM((8, width), F32)] + back_scratch(length, rows, width)
    scratch += [pltpu.VMEM((dp_size // 2,) + g.shape[1:], BF16) for g in grads]
    for g in grads:
        scratch += shard_scratch(dp_size, table_size, g.shape[1:], BF16)
    scratch += [pltpu.VMEM(t, BF16) for t in tail]
    for t in tail:
        scratch += shard_scratch(dp_size, table_size, t[1:], BF16)
    scratch += [pltpu.VMEM((hops + 1,) + small.shape, F32), pltpu.VMEM((hops,) + small.shape, F32)]
    scratch += [pltpu.VMEM((table_size, rows, LANES), BF16)] * micro
    for _ in range(micro):
        scratch += [pltpu.VMEM((table_size >> (i + 1), rows, LANES), BF16) for i in range(len(table_hops))]
    count = 7 * (hops + len(table_hops)) + hops + micro * len(table_hops)
    scratch += [pltpu.SemaphoreType.DMA((3,))] + [pltpu.SemaphoreType.DMA((count,))] * 2
    return pl.pallas_call(
        functools.partial(attend_back_reduce_kernel, dp_size, table_size),
        grid=(micro, HEADS),
        in_specs=back_specs((p, linv), (k, v, q, gmix, mixed), varied, fixed)
        + [far] * 3
        + [const_spec(small.shape)],
        out_specs=[const_spec((micro, rows, LANES)), const_spec(small.shape)]
        + [const_spec(b) for b in blocks],
        out_shape=[
            jax.ShapeDtypeStruct((micro, rows, LANES), F32),
            jax.ShapeDtypeStruct(small.shape, F32),
        ]
        + [jax.ShapeDtypeStruct(b, BF16) for b in blocks],
        scratch_shapes=scratch,
        compiler_params=vmem(60, collective_id=1, has_side_effects=True),
        name="attend_backward_reduce",
    )(p, linv, k, v, q, gmix, mixed, *varied, *fixed, *grads, small)


def finish_kernel(feat, shard, ig_in, small_in, *refs):
    ins, outs = refs[:7], refs[7:]
    ig_out, dwe, others, vecs, bu = outs[0], outs[1], outs[2:8], outs[8:14], outs[14]
    ig_out[...] = ig_in[:, :, :feat]
    dwe[...] = ins[0][...].astype(F32).T[:feat, :]
    for src, dst in zip(ins[1:], others):
        dst[...] = src[...].astype(F32)
    small = small_in[...]
    width = small.shape[1]
    dp = lax.axis_index("dp")
    turned = pltpu.roll(small, lax.rem(width - dp * shard, width), 1)
    for i, out in enumerate(vecs):
        out[...] = turned[i : i + 1, :shard]
    per_row = width // bu.shape[1]
    rows = small[8 : 8 + 4, :]
    row = dp // per_row
    pick = lax.broadcasted_iota(jnp.int32, rows.shape, 0) == row
    line = jnp.sum(jnp.where(pick, rows, 0.0), axis=0, keepdims=True)
    at = (dp % per_row) * bu.shape[1]
    bu[...] = pltpu.roll(jnp.broadcast_to(line, (8, width)), lax.rem(width - at, width), 1)[:1, : bu.shape[1]]


def finish(feat, ff_shard, ig, small, totals):
    micro, rows, _ = ig.shape
    shard = totals[0].shape[0]
    out_shape = (
        [jax.ShapeDtypeStruct((micro, rows, feat), F32), jax.ShapeDtypeStruct((feat, shard), F32)]
        + [jax.ShapeDtypeStruct(t.shape, F32) for t in totals[1:]]
        + [jax.ShapeDtypeStruct((1, shard), F32)] * 6
        + [jax.ShapeDtypeStruct((1, ff_shard), F32)]
    )
    return pl.pallas_call(
        functools.partial(finish_kernel, feat, shard),
        out_shape=out_shape,
        compiler_params=vmem(50),
        name="finish",
    )(ig, small, *totals)


def body(
    dp_size, table_size, features, feature_mask, support_count, embed_weight, embed_bias, gain_first, shift_first,
    query_weight, key_weight, value_weight, out_weight, gain_second, shift_second, up_weight, up_bias,
    down_weight, down_bias, cotangent,
):
    micro, _, rows, feat = features.shape
    shard, width = query_weight.shape
    hidden_units = up_weight.shape[1]
    ff_shard = up_bias.shape[0]
    features, cotangent, support = features[:, 0], cotangent[:, 0], support_count[:, 0]
    mask = jnp.pad(feature_mask[:, 0].astype(F32), ((0, 0), (0, LANES - feat)))[:, None, :]
    smalls = jnp.stack([embed_bias, gain_first, shift_first, gain_second, shift_second, down_bias])
    if 2 * shard == LANES and micro == 3:
        packed = jnp.concatenate(
            [jnp.pad(smalls, ((0, 0), (0, LANES - shard))), up_bias.reshape(2, LANES)]
        ).astype(F32)
        got = attend_forward_gather(
            dp_size, table_size, support, features, feature_mask, embed_weight, packed,
            query_weight, key_weight, value_weight, out_weight, up_weight, down_weight,
        )
        q, k, v, n, u, inv, emb, mixed, p, linv, x = got[:11]
        wet, wq, wk, wv = (g.reshape(-1, g.shape[-1]) for g in got[11:15])
        vec, bu = got[15:17]
        wo, wu, wd = (g.reshape(-1, g.shape[-1]) for g in got[17:])
        activations, ghid, gmix, dwo, dwu, dwd, small = mlp_both(mixed, emb, cotangent, wo, wu, wd, vec, bu)
        grads = [g.reshape(dp_size, table_size, -1, g.shape[1]) for g in (dwo, dwu, dwd)]
        ig, small, *totals = attend_backward_reduce(
            dp_size, table_size, grads, small, p, linv, k, v, q, gmix, mixed, n, u, inv, x, ghid, mask,
            wet, vec, wq, wk, wv,
        )
        totals = [t.reshape(-1, t.shape[-1]) for t in totals]
        out = finish(feat, ff_shard, ig, small, totals)
        ig, dwe, dwq, dwk, dwv, dwo, dwu, dwd = out[:8]
        smalls = [o.reshape(-1) for o in out[8:14]]
        dbu = out[14].reshape(-1)
    else:
        x = jnp.pad(features, ((0, 0), (0, 0), (0, LANES - feat))) * mask.astype(BF16)
        wet = jnp.pad(embed_weight, ((0, LANES - feat), (0, 0))).T
        shards = [wet, query_weight, key_weight, value_weight, out_weight, up_weight, down_weight]
        wet, wq, wk, wv, wo, wu, wd = (lax.all_gather(s, "dp", axis=0, tiled=True) for s in shards)
        vec = jnp.pad(lax.all_gather(smalls, "dp", axis=1, tiled=True).astype(F32), ((0, 2), (0, 0)))
        bu = lax.all_gather(up_bias, "dp", axis=0, tiled=True).astype(F32)[None]
        x = lax.all_gather(x, "table", axis=1, tiled=True)
        q, k, v, n, u, inv, emb, mixed, p, linv = attend_forward(support, x, wet, vec, wq, wk, wv, rows)
        activations, ghid, gmix, dwo, dwu, dwd, small = mlp_both(mixed, emb, cotangent, wo, wu, wd, vec, bu)
        ig, dwe, dwq, dwk, dwv, dvec = attend_backward(
            p, linv, k, v, q, gmix, mixed, n, u, inv, x, ghid, mask, wet, vec, wq, wk, wv
        )
        big = [dwe, dwq, dwk, dwv, dwo, dwu, dwd]
        own = [lax.psum_scatter(g.astype(F32), "dp", scatter_dimension=0, tiled=True) for g in big]
        dwe, dwq, dwk, dwv, dwo, dwu, dwd = (lax.psum(g, "table") for g in own)
        dwe = dwe[:, :feat].T
        dvec = jnp.concatenate([dvec[:3], small[3:6]])
        smalls = lax.psum(lax.psum_scatter(dvec, "dp", scatter_dimension=1, tiled=True), "table")
        dbu = small[8:].reshape(-1)[:hidden_units]
        dbu = lax.psum(lax.psum_scatter(dbu, "dp", scatter_dimension=0, tiled=True), "table")
        ig = lax.psum_scatter(ig.astype(F32), "table", scatter_dimension=1, tiled=True)[:, :, :feat]
    return (
        activations[:, None], ig[:, None], dwe, smalls[0], smalls[1], smalls[2],
        dwq, dwk, dwv, dwo, smalls[3], smalls[4], dwu, dbu, dwd, smalls[5],
    )


def solution(mesh):
    rows, cols, vecs = P("dp", None), P(None, "dp"), P("dp")
    table = P(None, "dp", "table", None)
    return jax.shard_map(
        functools.partial(body, mesh.shape["dp"], mesh.shape["table"]),
        mesh=mesh,
        in_specs=(
            table, P(None, "dp", None), cols, cols, vecs, vecs, vecs, rows, rows, rows, rows,
            vecs, vecs, rows, vecs, rows, vecs, table,
        ),
        out_specs=(
            table, table, cols, vecs, vecs, vecs, rows, rows, rows, rows, vecs, vecs, rows, vecs, rows, vecs,
        ),
        check_vma=False,
    )
```

```python
import functools

import jax
import jax.numpy as jnp
from jax import lax
from jax.experimental import pallas as pl
from jax.experimental.pallas import tpu as pltpu
from jax.sharding import PartitionSpec as P

HEADS = 4
HEAD_DIM = 128
LANES = 128
EPSILON = 1e-5
SCALE = HEAD_DIM**-0.5
LOG2E = 1.4426950408889634
ROW_BLOCK = 256
KEY_BLOCK = 512
INV_SQRT_TWO = 0.7071067811865476
INV_SQRT_TWO_PI = 0.3989422804014327
BF16 = jnp.bfloat16
F32 = jnp.float32
MESH = pl.DeviceIdType.MESH


def dot_nn(a, b):
    return lax.dot_general(a, b, (((1,), (0,)), ((), ())), preferred_element_type=F32)


def dot_nt(a, b):
    return lax.dot_general(a, b, (((1,), (1,)), ((), ())), preferred_element_type=F32)


def dot_tn(a, b):
    return lax.dot_general(a, b, (((0,), (0,)), ((), ())), preferred_element_type=F32)


def norm_parts(v):
    mean = jnp.mean(v, axis=-1, keepdims=True)
    centred = v - mean
    inv = lax.rsqrt(jnp.mean(centred * centred, axis=-1, keepdims=True) + EPSILON)
    return centred * inv, inv


def norm_back(grad, unit, inv, gain):
    q = grad * gain
    return inv * (
        q
        - jnp.mean(q, axis=-1, keepdims=True)
        - unit * jnp.mean(q * unit, axis=-1, keepdims=True)
    )


def row_sum(v):
    return jnp.sum(v, axis=0, keepdims=True)


def const_spec(shape):
    return pl.BlockSpec(shape, lambda *g: (0,) * len(shape))


def micro_spec(shape):
    return pl.BlockSpec((1,) + shape, lambda m, *g: (m,) + (0,) * len(shape))


def head_spec(shape):
    return pl.BlockSpec((1, 1) + shape, lambda m, h: (m, h) + (0,) * len(shape))


def head_cols_spec(rows):
    return pl.BlockSpec((1, rows, HEAD_DIM), lambda m, h: (m, 0, h))


def vmem(mib, **extra):
    return pltpu.CompilerParams(vmem_limit_bytes=mib * 2**20, **extra)


def toggled(index, hop):
    return index + hop * (1 - 2 * ((index // hop) % 2))


def toggled_by(index, hops):
    for hop in hops:
        index = toggled(index, hop)
    return index


def subsets(hops):
    out = [()]
    for hop in hops:
        out = out + [s + (hop,) for s in out]
    return out


def hops_of(size):
    return [1 << i for i in range(size.bit_length() - 1)]


class Place:
    def __init__(self, dp_size, table_size):
        self.size = {"dp": dp_size, "table": table_size}
        self.hops = {axis: hops_of(n) for axis, n in self.size.items()}
        self.me = {"dp": lax.axis_index("dp"), "table": lax.axis_index("table")}

    def partner(self, axis, hop):
        there = dict(self.me)
        there[axis] = toggled(there[axis], hop)
        return (there["dp"], there["table"])

    def at(self, axis, shift):
        n = self.size[axis]
        return lax.rem(self.me[axis] + (shift + n), n)

    def ahead(self, axis, shift):
        there = dict(self.me)
        there[axis] = self.at(axis, shift)
        return (there["dp"], there["table"])

    def greet(self, all_dp):
        barrier = pltpu.get_barrier_semaphore()
        peers = [self.ahead("table", s) for s in range(1, self.size["table"])]
        if all_dp:
            peers += [self.ahead("dp", s) for s in range(1, self.size["dp"])]
        else:
            peers += [self.partner("dp", hop) for hop in self.hops["dp"]]
        for peer in peers:
            pl.semaphore_signal(barrier, inc=1, device_id=peer, device_id_type=MESH)
        return lambda: pl.semaphore_wait(barrier, len(peers))


class Swap:
    def __init__(self, place, axis, sems, base, send, put):
        self.place, self.axis, self.sems, self.base = place, axis, sems, base
        self.send, self.put = send, put
        self.shifts = range(1, place.size[axis])

    def copy(self, shift, src, dst):
        index = self.base + shift - 1
        return pltpu.make_async_remote_copy(
            src_ref=src, dst_ref=dst, send_sem=self.sems[0].at[index], recv_sem=self.sems[1].at[index],
            device_id=self.place.ahead(self.axis, shift), device_id_type=MESH,
        )

    def start_one(self, shift):
        to = self.place.at(self.axis, shift)
        self.copy(shift, self.send(to), self.put(self.place.me[self.axis], shift)).start()

    def start(self):
        for shift in self.shifts:
            self.start_one(shift)

    def arrive_one(self, shift):
        here = self.put(self.place.at(self.axis, -shift), shift)
        self.copy(shift, here, here).wait_recv()
        return here

    def arrive(self):
        return [self.arrive_one(shift) for shift in self.shifts]

    def sent(self):
        for shift in self.shifts:
            out = self.send(self.place.at(self.axis, shift))
            self.copy(shift, out, out).wait_send()


def remote(place, axis, hop, src, dst, sems, index):
    return pltpu.make_async_remote_copy(
        src_ref=src, dst_ref=dst, send_sem=sems[0].at[index], recv_sem=sems[1].at[index],
        device_id=place.partner(axis, hop), device_id_type=MESH,
    )


class Gather:
    def __init__(self, place, axis, hops, full, sems, base, own=None):
        self.place, self.axis, self.hops = place, axis, hops
        self.full, self.sems, self.base, self.own = full, sems, base, own
        self.steps = len(hops)

    def whole(self, step):
        part = self.full.at[pl.ds(0, 1 << step)]
        return remote(self.place, self.axis, self.hops[step], part, part, self.sems, self.base + step)

    def start(self, step):
        for s in subsets(self.hops[:step]):
            block = self.full.at[toggled_by(self.place.me[self.axis], s)]
            src = block if s or self.own is None else self.own
            remote(
                self.place, self.axis, self.hops[step], src, block, self.sems, self.base + step
            ).start()

    def arrive(self, step):
        self.whole(step).wait_recv()

    def sent(self):
        for step in range(self.steps):
            self.whole(step).wait_send()


def add_into(into, other):
    lead = into.shape[:-2]
    rows, cols = into.shape[-2:]
    if lead:
        for i in range(lead[0]):
            add_into(into.at[i], other.at[i])
        return
    piece = min(rows, max(16, 65536 // cols))
    piece = rows if rows % piece else piece

    def body(i, carry):
        at = pl.ds(pl.multiple_of(i * piece, piece), piece)
        into[at, :] = (into[at, :].astype(F32) + other[at, :].astype(F32)).astype(into.dtype)
        return carry

    if rows == piece:
        into[...] = (into[...].astype(F32) + other[...].astype(F32)).astype(into.dtype)
    else:
        lax.fori_loop(0, rows // piece, body, 0)


class Reduce:
    def __init__(self, place, axis, hops, blocks, bufs, sems, base, near=None):
        self.place, self.axis, self.hops = place, axis, hops
        self.held, self.near = blocks, near
        self.bufs, self.sems, self.base = bufs, sems, base
        self.steps = len(hops)

    def mine(self, step, s):
        if step == 0:
            return self.held(s)
        order = [set(t) for t in subsets(self.hops[step:])]
        return self.bufs[step - 1].at[order.index(set(s))]

    def copy(self, step, src, dst):
        return remote(self.place, self.axis, self.hops[step], src, dst, self.sems, self.base + step)

    def start(self, step):
        for i, s in enumerate(subsets(self.hops[step + 1 :])):
            self.copy(step, self.mine(step, s + (self.hops[step],)), self.bufs[step].at[i]).start()

    def arrive(self, step):
        self.copy(step, self.bufs[step], self.bufs[step]).wait_recv()
        for i, s in enumerate(subsets(self.hops[step + 1 :])):
            near = step == 0 and self.near is not None
            add_into(self.bufs[step].at[i], self.near.at[i] if near else self.mine(step, s))

    def total(self):
        return self.bufs[-1].at[0]

    def sent(self):
        for step in range(self.steps):
            self.copy(step, self.bufs[step], self.bufs[step]).wait_send()


class Shard:
    def __init__(self, place, dp_hops, grad, scratch, sems, base, near=None):
        n, m = len(dp_hops), len(place.hops["table"])
        dp_bufs, table_bufs, full = scratch[:n], scratch[n : n + m], scratch[n + m]
        self.place, self.grad, self.near = place, grad, near

        def blocks(s):
            return grad.at[toggled_by(place.me["dp"], s)]

        self.dp = Reduce(place, "dp", dp_hops, blocks, dp_bufs, sems, base, near)
        table_hops = place.hops["table"]
        base += self.dp.steps

        def parts(s):
            return self.dp.total().at[toggled_by(place.me["table"], s)]

        self.table = Reduce(place, "table", table_hops, parts, table_bufs, sems, base)
        base += self.table.steps
        self.full = full
        self.back = Gather(place, "table", table_hops[::-1], full, sems, base)
        self.flows = [(f, i) for f in (self.dp, self.table, self.back) for i in range(f.steps)]
        self.steps = len(self.flows)

    def near_copies(self, sem):
        halves = subsets(self.dp.hops[1:])
        return [
            pltpu.make_async_copy(self.dp.held(s), self.near.at[i], sem) for i, s in enumerate(halves)
        ]

    def near_wait(self, sem):
        pltpu.make_async_copy(self.near, self.near, sem).wait()

    def start(self, step):
        flow, i = self.flows[step]
        if flow is self.back and i == 0:
            self.full[self.place.me["table"]] = self.table.total()[...]
        flow.start(i)

    def arrive(self, step):
        flow, i = self.flows[step]
        flow.arrive(i)

    def sent(self):
        for flow in (self.dp, self.table, self.back):
            flow.sent()


class QuickShard:
    def __init__(self, place, dp_hops, grad, scratch, sems, base):
        n = len(dp_hops)
        got, full = scratch[n], scratch[n + 1]
        self.place, self.full = place, full

        def blocks(s):
            return grad.at[toggled_by(place.me["dp"], s)]

        self.dp = Reduce(place, "dp", dp_hops, blocks, scratch[:n], sems, base)
        base += n
        self.out = Swap(
            place, "table", sems, base, lambda t: self.dp.total().at[t], lambda t, s: got.at[s - 1]
        )
        base += place.size["table"] - 1
        self.back = Swap(
            place, "table", sems, base, lambda t: full.at[place.me["table"]], lambda t, s: full.at[t]
        )
        self.steps = n + 2

    def start(self, step):
        n = self.dp.steps
        if step < n:
            self.dp.start(step)
        elif step == n:
            self.out.start()
        else:
            self.back.start()

    def arrive(self, step):
        n = self.dp.steps
        if step < n:
            self.dp.arrive(step)
        elif step == n:
            me = self.place.me["table"]
            total = self.dp.total()[me].astype(F32)
            for got in self.out.arrive():
                total = total + got[...].astype(F32)
            self.full[me] = total.astype(self.full.dtype)
        else:
            self.back.arrive()

    def sent(self):
        self.dp.sent()
        self.out.sent()
        self.back.sent()


def quick_scratch(dp_size, table_size, block, dtype):
    out = [pltpu.VMEM((dp_size >> (i + 1),) + block, dtype) for i in range(len(hops_of(dp_size)))]
    return out + [pltpu.VMEM((table_size - 1,) + block[1:], dtype), pltpu.VMEM(block, dtype)]


def quick_sems(dp_size, table_size):
    return len(hops_of(dp_size)) + 2 * (table_size - 1)


class Small:
    def __init__(self, place, block, got_dp, part, got_table, sems, base):
        self.place, self.block, self.part = place, block, part
        self.first = Swap(place, "dp", sems, base, block, lambda t, s: got_dp.at[s - 1])
        base += place.size["dp"] - 1
        self.second = Swap(
            place, "table", sems, base, lambda t: part, lambda t, s: got_table.at[s - 1]
        )
        self.steps = 2

    def start(self, step):
        (self.first, self.second)[step].start()

    def arrive(self, step):
        if step == 0:
            total = self.block(self.place.me["dp"])[...].astype(F32)
            for got in self.first.arrive():
                total = total + got[...].astype(F32)
            self.part[...] = total.astype(self.part.dtype)
        else:
            total = self.part[...].astype(F32)
            for got in self.second.arrive():
                total = total + got[...].astype(F32)
            self.total = total

    def sent(self):
        self.first.sent()
        self.second.sent()


def small_scratch(dp_size, table_size, block, dtype):
    return [
        pltpu.VMEM((dp_size - 1,) + block, dtype),
        pltpu.VMEM(block, dtype),
        pltpu.VMEM((table_size - 1,) + block, dtype),
    ]


def shard_scratch(dp_size, table_size, block, dtype):
    out = [pltpu.VMEM((dp_size >> (i + 1),) + block, dtype) for i in range(len(hops_of(dp_size)))]
    out += [
        pltpu.VMEM((table_size >> (i + 1),) + block[1:], dtype) for i in range(len(hops_of(table_size)))
    ]
    out.append(pltpu.VMEM(block, dtype))
    return out


def attend_core(
    support, order, get_x, wet_ref, vec_ref, wk, wv, wq,
    q_ref, k_ref, v_ref, n_ref, u_ref, inv_ref, emb_ref, mixed_ref, p_ref, linv_ref,
):
    length, rows = n_ref.shape[1], q_ref.shape[1]
    own = lax.axis_index("table")
    bias, gain, shift = vec_ref[0:1, :], vec_ref[1:2, :], vec_ref[2:3, :]
    chunk = 256

    @pl.when(pl.program_id(1) == 0)
    def _():
        for ready, block in order:
            ready()

            def project(i, carry):
                at = pl.ds(pl.multiple_of(block * rows + i * chunk, chunk), chunk)
                part = pl.ds(pl.multiple_of(i * chunk, chunk), chunk)
                embedded = dot_nt(get_x(block, part), wet_ref[...]) + bias
                unit, inv = norm_parts(embedded)
                normed = (unit * gain + shift).astype(BF16)
                n_ref[0, at, :] = normed
                u_ref[0, at, :] = unit.astype(BF16)
                inv_ref[0, at, :] = jnp.broadcast_to(inv, (chunk, LANES))
                k_ref[0, at, :] = dot_nn(normed, wk()).astype(BF16)
                v_ref[0, at, :] = dot_nn(normed, wv()).astype(BF16)
                return carry

            lax.fori_loop(0, rows // chunk, project, 0, unroll=True)
        here = pl.ds(pl.multiple_of(own * rows, rows), rows)
        emb_ref[0] = dot_nt(get_x(own, slice(None)), wet_ref[...]) + bias
        q_ref[0] = dot_nn(n_ref[0, here, :], wq()).astype(BF16)

    block = ROW_BLOCK
    sure = length - rows
    columns = sure + lax.broadcasted_iota(jnp.int32, (1, rows), 1)
    allowed = columns < support
    cols = pl.ds(pl.multiple_of(pl.program_id(1) * HEAD_DIM, HEAD_DIM), HEAD_DIM)

    for i in range(rows // block):
        at = slice(i * block, (i + 1) * block)
        qh = q_ref[0, at, cols]
        first = dot_nt(qh, k_ref[0, :sure, cols])
        last = dot_nt(qh, k_ref[0, sure:, cols])
        last = jnp.where(allowed, last, -1e30)
        top = jnp.maximum(
            jnp.max(first, axis=-1, keepdims=True), jnp.max(last, axis=-1, keepdims=True)
        )
        pf = jnp.exp2((first - top) * (SCALE * LOG2E))
        pt = jnp.exp2((last - top) * (SCALE * LOG2E))
        total = jnp.sum(pf, axis=-1, keepdims=True) + jnp.sum(pt, axis=-1, keepdims=True)
        pf, pt = pf.astype(BF16), pt.astype(BF16)
        p_ref[0, 0, at, :sure] = pf
        p_ref[0, 0, at, sure:] = pt
        linv = 1.0 / total
        linv_ref[0, 0, at, :] = jnp.broadcast_to(linv, (block, LANES))
        out = dot_nn(pf, v_ref[0, :sure, cols]) + dot_nn(pt, v_ref[0, sure:, cols])
        mixed_ref[0, at, cols] = out * linv


def attend_kernel(support_ref, x_ref, wet_ref, vec_ref, wq_ref, wk_ref, wv_ref, *outs):
    rows = outs[0].shape[1]

    def get_x(block, part):
        x = x_ref[0, pl.ds(pl.multiple_of(block * rows, rows), rows), :]
        return x if part == slice(None) else x_ref[0, pl.ds(block * rows + part.start, part.size), :]

    attend_core(
        support_ref[pl.program_id(0)],
        [(lambda: None, block) for block in range(x_ref.shape[1] // rows)],
        get_x, wet_ref, vec_ref, lambda: wk_ref[...], lambda: wv_ref[...], lambda: wq_ref[...], *outs,
    )


def attend_gather_kernel(
    dp_size, table_size, support_ref, feat_ref, mask_ref, ew_ref,
    v0_ref, v1_ref, v2_ref, v3_ref, v4_ref, v5_ref, ub_ref, wq_in, wk_in, wv_in, wo_in, wu_in, wd_in,
    q_ref, k_ref, v_ref, n_ref, u_ref, inv_ref, emb_ref, mixed_ref, p_ref, linv_ref,
    x_out, wet_out, wq_out, wk_out, wv_out, vec_ref, bu_ref, wo_out, wu_out, wd_out,
    x_buf, wet_buf, packed_buf, wq_buf, wk_buf, wv_buf, own_sem, send_sem, recv_sem,
):
    micro_id, head = pl.program_id(0), pl.program_id(1)
    micro, feat, rows = feat_ref.shape
    shard = wq_in.shape[0]
    width = wq_in.shape[1]
    place = Place(dp_size, table_size)
    dp, table = place.me["dp"], place.me["table"]
    sems = (send_sem, recv_sem)
    hops = place.hops["dp"]
    forth, back = hops[1:] + hops[:1], hops[:0:-1] + hops[:1]
    last = len(hops) - 1
    base = 0

    def gather(order, full, own=None):
        nonlocal base
        flow = Gather(place, "dp", order, full, sems, base, own)
        base += flow.steps
        return flow

    early = [
        gather(forth, wk_buf),
        gather(back, wv_buf),
        gather(forth, wet_buf),
        gather(back, packed_buf),
    ]
    query = gather(forth, wq_buf)
    late = [gather(forth, wo_out, wo_in), gather(forth, wu_out, wu_in), gather(back, wd_out, wd_in)]
    feats = []
    for m in range(micro):
        own_x = x_buf.at[m, table]
        feats.append(
            Swap(
                place, "table", sems, base,
                lambda t, own_x=own_x: own_x,
                lambda t, s, m=m: x_buf.at[m, t],
            )
        )
        base += table_size - 1
    own_copies = [
        pltpu.make_async_copy(src, dst.at[dp], own_sem.at[i])
        for i, (src, dst) in enumerate(((wo_in, wo_out), (wu_in, wu_out), (wd_in, wd_out)))
    ]
    out_copies = [
        pltpu.make_async_copy(src, dst, own_sem.at[3 + i])
        for i, (src, dst) in enumerate(
            ((wet_buf, wet_out), (wq_buf, wq_out), (wk_buf, wk_out), (wv_buf, wv_out))
        )
    ]

    def at_step(m, h):
        return pl.when((micro_id == m) & (head == h))

    @at_step(0, 0)
    def _():
        wait_all = place.greet(False)
        wet_buf[dp] = jnp.zeros((shard, LANES), BF16)
        wet_buf[dp, :, :feat] = ew_ref[...]
        packed_buf[dp] = jnp.zeros((8, LANES), F32)
        for i, ref in enumerate((v0_ref, v1_ref, v2_ref, v3_ref, v4_ref, v5_ref)):
            packed_buf[dp, i : i + 1, :shard] = ref[...].astype(F32)
        packed_buf[dp, 6:8, :] = ub_ref[...].astype(F32)
        wk_buf[dp] = wk_in[...]
        wv_buf[dp] = wv_in[...]
        wq_buf[dp] = wq_in[...]

        def fill(m):
            tall = jnp.concatenate(
                [feat_ref[m].astype(F32), jnp.zeros((LANES - feat, rows), F32)], axis=0
            ).T
            x_buf[m, table] = jnp.zeros((rows, LANES), BF16)
            x_buf[m, table, :, :feat] = (tall[:, :feat] * mask_ref[m].astype(F32)).astype(BF16)

        fill(0)
        wait_all()
        for flow in early:
            flow.start(0)
        feats[0].start()
        for copy in own_copies:
            copy.start()
        for m in range(1, micro):
            fill(m)
        for step in range(last):
            for flow in early:
                flow.arrive(step)
                flow.start(step + 1)
            if step == 0:
                query.start(0)
            else:
                query.arrive(step - 1)
                query.start(step)
        for flow in early:
            flow.arrive(last)
        for flow in late:
            flow.start(0)
        lane = lax.broadcasted_iota(jnp.int32, (8, LANES), 1)
        for d in range(0, dp_size, 2):
            pair = jnp.where(lane < shard, packed_buf[d], pltpu.roll(packed_buf[d + 1], shard, 1))
            vec_ref[:, d * shard : (d + 2) * shard] = pair
        for d in range(dp_size):
            bu_ref[:, 2 * d * LANES : (2 * d + 1) * LANES] = packed_buf[d, 6:7, :]
            bu_ref[:, (2 * d + 1) * LANES : (2 * d + 2) * LANES] = packed_buf[d, 7:8, :]

    @at_step(0, 1)
    def _():
        for flow in late:
            flow.arrive(0)
            flow.start(1)
        for copy in out_copies:
            copy.start()
        feats[1].start()

    @at_step(1, 1)
    def _():
        for flow in late:
            flow.arrive(1)
            flow.start(2)
        feats[2].start()

    @at_step(2, 0)
    def _():
        for flow in late:
            flow.arrive(2)

    def get_x(block, part):
        return x_buf[micro_id, block, part, :]

    shifts = sorted(range(1, table_size), key=lambda s: (min(s, table_size - s), s))

    def ready(i, shift):
        def wait():
            if i == 1:

                @pl.when(micro_id == 0)
                def _():
                    query.arrive(last - 1)
                    query.start(last)

            if shift:
                for m in range(micro):

                    @pl.when(micro_id == m)
                    def _():
                        feats[m].arrive_one(shift)

            if i == table_size - 1:
                x_out[0] = x_buf[micro_id].reshape(x_out.shape[1:])

                @pl.when(micro_id == 0)
                def _():
                    query.arrive(last)

        return wait

    order = [(ready(i, shift), place.at("table", -shift)) for i, shift in enumerate([0] + shifts)]

    def full(buf):
        return lambda: buf[...].reshape(width, width)

    attend_core(
        support_ref[micro_id], order, get_x, WetView(wet_buf), vec_ref, full(wk_buf), full(wv_buf), full(wq_buf),
        q_ref, k_ref, v_ref, n_ref, u_ref, inv_ref, emb_ref, mixed_ref, p_ref, linv_ref,
    )

    @at_step(micro - 1, HEADS - 1)
    def _():
        for flow in feats + early + [query] + late:
            flow.sent()
        for copy in own_copies + out_copies:
            copy.wait()


class WetView:
    def __init__(self, buf):
        self.buf = buf

    def __getitem__(self, _):
        return self.buf[...].reshape(-1, self.buf.shape[-1])


def attend_shapes(rows, length, width):
    out = [
        ((rows, width), BF16),
        ((length, width), BF16),
        ((length, width), BF16),
        ((length, width), BF16),
        ((length, width), BF16),
        ((length, LANES), F32),
        ((rows, width), F32),
        ((rows, width), F32),
    ]
    return out, [((rows, length), BF16), ((rows, LANES), F32)]


def attend_forward_gather(dp_size, table_size, support, feat, mask, ew, vecs, ub, wq, wk, wv, wo, wu, wd):
    micro, _, rows = feat.shape
    length = rows * table_size
    width = wq.shape[1]
    out, heads = attend_shapes(rows, length, width)
    whole = pl.BlockSpec(memory_space=pltpu.VMEM)
    far = pl.BlockSpec(memory_space=pl.ANY)

    def gathered(a):
        return jax.ShapeDtypeStruct((dp_size,) + a.shape, a.dtype)

    wet = jax.ShapeDtypeStruct((dp_size, wq.shape[0], LANES), BF16)
    count = micro * (table_size - 1) + 8 * len(hops_of(dp_size))
    return pl.pallas_call(
        functools.partial(attend_gather_kernel, dp_size, table_size),
        grid=(micro, HEADS),
        in_specs=[pl.BlockSpec(memory_space=pltpu.SMEM)] + [whole] * 13 + [far] * 3,
        out_specs=[micro_spec(s) for s, _ in out]
        + [head_spec(s) for s, _ in heads]
        + [micro_spec((length, LANES))]
        + [far] * 4
        + [const_spec((8, width)), const_spec((1, wu.shape[1]))]
        + [far] * 3,
        out_shape=[jax.ShapeDtypeStruct((micro,) + s, d) for s, d in out]
        + [jax.ShapeDtypeStruct((micro, HEADS) + s, d) for s, d in heads]
        + [jax.ShapeDtypeStruct((micro, length, LANES), BF16)]
        + [wet, gathered(wq), gathered(wk), gathered(wv)]
        + [jax.ShapeDtypeStruct((8, width), F32), jax.ShapeDtypeStruct((1, wu.shape[1]), F32)]
        + [gathered(wo), gathered(wu), gathered(wd)],
        scratch_shapes=[
            pltpu.VMEM((micro, table_size, rows, LANES), BF16),
            pltpu.VMEM(wet.shape, BF16),
            pltpu.VMEM((dp_size, 8, LANES), F32),
            pltpu.VMEM((dp_size,) + wq.shape, BF16),
            pltpu.VMEM((dp_size,) + wk.shape, BF16),
            pltpu.VMEM((dp_size,) + wv.shape, BF16),
            pltpu.SemaphoreType.DMA((7,)),
            pltpu.SemaphoreType.DMA((count,)),
            pltpu.SemaphoreType.DMA((count,)),
        ],
        compiler_params=vmem(60, collective_id=0, has_side_effects=True),
        name="attend_forward_gather",
    )(support, feat, mask, ew, *vecs, ub, wq, wk, wv, wo, wu, wd)


def attend_forward(support, x_all, wet, vec, wq, wk, wv, rows):
    micro, length, lanes = x_all.shape
    width = wq.shape[0]
    out, heads = attend_shapes(rows, length, width)
    return pl.pallas_call(
        attend_kernel,
        grid=(micro, HEADS),
        in_specs=[
            pl.BlockSpec(memory_space=pltpu.SMEM),
            micro_spec((length, lanes)),
            const_spec(wet.shape),
            const_spec(vec.shape),
            const_spec(wq.shape),
            const_spec(wk.shape),
            const_spec(wv.shape),
        ],
        out_specs=[micro_spec(s) for s, _ in out] + [head_spec(s) for s, _ in heads],
        out_shape=[jax.ShapeDtypeStruct((micro,) + s, d) for s, d in out]
        + [jax.ShapeDtypeStruct((micro, HEADS) + s, d) for s, d in heads],
        compiler_params=vmem(50),
        name="attend_forward",
    )(support, x_all, wet, vec, wq, wk, wv)


def mlp_kernel(
    mixed_ref, emb_ref, cot_ref, wo_ref, wu_ref, wd_ref, vec_ref, bu_ref,
    act_ref, ghid_ref, gmix_ref, dwo_ref, dwu_ref, dwd_ref, dvec_ref,
    acc_o, acc_u, acc_d, gn2_ref, out_ref,
):
    step, last = pl.program_id(0), pl.num_programs(0) - 1
    hidden_units = wu_ref.shape[1]
    chunk = 512

    @pl.when(step == 0)
    def _():
        acc_o[...] = jnp.zeros_like(acc_o)
        acc_u[...] = jnp.zeros_like(acc_u)
        acc_d[...] = jnp.zeros_like(acc_d)
        dvec_ref[...] = jnp.zeros_like(dvec_ref)

    gain, shift, dbias = vec_ref[3:4, :], vec_ref[4:5, :], vec_ref[5:6, :]
    mixed = mixed_ref[0].astype(BF16)
    g_out = cot_ref[0]
    hidden = emb_ref[0] + dot_nn(mixed, wo_ref[...])
    unit, inv = norm_parts(hidden)
    normed = (unit * gain + shift).astype(BF16)
    out_ref[...] = hidden + dbias
    normed_t = normed.T
    g_out_t = g_out.T
    for f in range(hidden_units // chunk):
        cols = slice(f * chunk, (f + 1) * chunk)
        pre = dot_nn(normed, wu_ref[:, cols]) + bu_ref[:, cols]
        cdf = 0.5 * (1.0 + lax.erf(pre * INV_SQRT_TWO))
        pdf = jnp.exp(-0.5 * pre * pre) * INV_SQRT_TWO_PI
        act = (pre * cdf).astype(BF16)
        out_ref[...] += dot_nn(act, wd_ref[cols, :])
        g_act = dot_nt(g_out, wd_ref[cols, :])
        g_pre_f = g_act * (cdf + pre * pdf)
        g_pre = g_pre_f.astype(BF16)
        acc_u[:, cols] += dot_nn(normed_t, g_pre)
        acc_d[:, cols] += dot_nn(g_out_t, act)
        dvec_ref[8 + f : 9 + f, :] += row_sum(g_pre_f)
        g_part = dot_nt(g_pre, wu_ref[:, cols])
        if f == 0:
            gn2_ref[...] = g_part
        else:
            gn2_ref[...] += g_part
    act_ref[0] = out_ref[...].astype(BF16)
    g_norm = gn2_ref[...]
    g_out_f = g_out.astype(F32)
    dvec_ref[3:4, :] += row_sum(g_norm * unit)
    dvec_ref[4:5, :] += row_sum(g_norm)
    dvec_ref[5:6, :] += row_sum(g_out_f)
    g_hidden = g_out_f + norm_back(g_norm, unit, inv, gain)
    ghid_ref[0] = g_hidden
    branch = g_hidden.astype(BF16)
    acc_o[...] += dot_tn(mixed, branch)
    gmix_ref[0] = dot_nt(branch, wo_ref[...]).astype(BF16)

    @pl.when(step == last)
    def _():
        dwo_ref[...] = acc_o[...].astype(BF16)
        dwu_ref[...] = acc_u[...].astype(BF16)
        for f in range(hidden_units // chunk):
            cols = slice(f * chunk, (f + 1) * chunk)
            dwd_ref[cols, :] = acc_d[:, cols].T.astype(BF16)


def mlp_both(mixed, emb, cot, wo, wu, wd, vec, bu):
    micro, rows, width = mixed.shape
    hidden_units = wu.shape[1]
    per_micro = [((rows, width), BF16), ((rows, width), F32), ((rows, width), BF16)]
    summed = [
        ((width, width), BF16),
        ((width, hidden_units), BF16),
        ((hidden_units, width), BF16),
        ((16, width), F32),
    ]
    return pl.pallas_call(
        mlp_kernel,
        grid=(micro,),
        in_specs=[micro_spec((rows, width))] * 3
        + [const_spec(a.shape) for a in (wo, wu, wd, vec, bu)],
        out_specs=[micro_spec(s) for s, _ in per_micro] + [const_spec(s) for s, _ in summed],
        out_shape=[jax.ShapeDtypeStruct((micro,) + s, d) for s, d in per_micro]
        + [jax.ShapeDtypeStruct(s, d) for s, d in summed],
        scratch_shapes=[
            pltpu.VMEM((width, width), F32),
            pltpu.VMEM((width, hidden_units), F32),
            pltpu.VMEM((width, hidden_units), F32),
            pltpu.VMEM((rows, width), F32),
            pltpu.VMEM((rows, width), F32),
        ],
        compiler_params=vmem(60),
        name="mlp_both",
    )(mixed, emb, cot, wo, wu, wd, vec, bu)


def attend_back_core(
    hooks, order, p_ref, linv_ref, k_ref, v_ref, q_ref, gmix_ref, mixed_ref, n_ref, u_ref, inv_ref, x_ref, ghid_ref,
    wet_ref, vec_ref, wq_ref, wk_ref, wv_ref,
    dvec_ref, dkv_ref, dq_ref, wkv_t, acc_e, acc_q, acc_kv,
):
    step, head = pl.program_id(0), pl.program_id(1)
    length, rows, width = n_ref.shape[1], dq_ref.shape[0], dq_ref.shape[1]
    own = lax.axis_index("table")
    here = pl.ds(pl.multiple_of(own * rows, rows), rows)

    @pl.when((step == 0) & (head == 0))
    def _():
        acc_e[...] = jnp.zeros_like(acc_e)
        acc_q[...] = jnp.zeros_like(acc_q)
        acc_kv[...] = jnp.zeros_like(acc_kv)
        dvec_ref[...] = jnp.zeros_like(dvec_ref)
        for h in range(HEADS):
            cols = slice(h * HEAD_DIM, (h + 1) * HEAD_DIM)
            wkv_t[2 * h * HEAD_DIM : (2 * h + 1) * HEAD_DIM, :] = wk_ref[:, cols].T
            wkv_t[(2 * h + 1) * HEAD_DIM : (2 * h + 2) * HEAD_DIM, :] = wv_ref[:, cols].T

    keys = KEY_BLOCK
    linv = linv_ref[0, 0][:, :1]
    g_low = (gmix_ref[0].astype(F32) * linv).astype(BF16)
    delta = jnp.sum(mixed_ref[0] * g_low.astype(F32), axis=-1, keepdims=True)
    g_low_t = g_low.T
    q_t = q_ref[0].T
    cols = pl.ds(pl.multiple_of(head * HEAD_DIM, HEAD_DIM), HEAD_DIM)
    k_rows = pl.ds(pl.multiple_of(2 * head * HEAD_DIM, HEAD_DIM), HEAD_DIM)
    v_rows = pl.ds(pl.multiple_of((2 * head + 1) * HEAD_DIM, HEAD_DIM), HEAD_DIM)
    dq = None
    for j in range(length // keys):
        at = slice(j * keys, (j + 1) * keys)
        p = p_ref[0, 0, :, at]
        dp = dot_nt(g_low, v_ref[0, at, :])
        ds = (p.astype(F32) * (dp - delta)).astype(BF16)
        dkv_ref[v_rows, at] = dot_nn(g_low_t, p).astype(BF16)
        dkv_ref[k_rows, at] = (dot_nn(q_t, ds) * SCALE).astype(BF16)
        dq_part = dot_nn(ds, k_ref[0, at, :])
        dq = dq_part if dq is None else dq + dq_part
    dq_ref[:, cols] = (dq * SCALE).astype(BF16)

    @pl.when(lax.rem(head, 2) == 1)
    def _():
        part = 2 * HEAD_DIM
        for i in range(2):
            at = pl.ds(pl.multiple_of((head - 1 + i) * part, part), part)
            acc_kv[at, :] += dot_nn(dkv_ref[at, :], n_ref[0])
        pair = pl.ds(pl.multiple_of((head - 1) * HEAD_DIM, part), part)
        acc_q[:, pair] += dot_tn(n_ref[0, here, :], dq_ref[:, pair])

    hooks.pair_done()

    @pl.when(head == HEADS - 1)
    def _():
        gain = vec_ref[1:2, :]
        part = 256
        hooks.tick(HEADS)
        for g, (block, mine) in enumerate(order):

            def others(i, carry):
                at = pl.ds(pl.multiple_of(block * rows + i * part, part), part)
                inner = pl.ds(pl.multiple_of(i * part, part), part)
                unit, inv = u_ref[0, at, :].astype(F32), inv_ref[0, at, :][:, :1]
                g_norm = dot_tn(dkv_ref[:, at], wkv_t[...])
                if mine:
                    g_norm = g_norm + dot_nt(dq_ref[inner, :], wq_ref[...])
                dvec_ref[1:2, :] += row_sum(g_norm * unit)
                dvec_ref[2:3, :] += row_sum(g_norm)
                g_emb = norm_back(g_norm, unit, inv, gain)
                if mine:
                    g_emb = g_emb + ghid_ref[0, inner, :]
                dvec_ref[0:1, :] += row_sum(g_emb)
                g_emb = g_emb.astype(BF16)
                acc_e[...] += dot_tn(x_ref[0, at, :], g_emb)
                hooks.put(block, mine, inner, dot_nn(g_emb, wet_ref[...]))
                return carry

            lax.fori_loop(0, rows // part, others, 0, unroll=True)
            hooks.block_done(g, block, mine)
            hooks.tick(HEADS + 1 + g)


class Alone:
    def __init__(self, ig_ref, rows):
        self.ig_ref, self.rows = ig_ref, rows

    def tick(self, k):
        pass

    def pair_done(self):
        pass

    def put(self, block, mine, inner, value):
        self.ig_ref[0, pl.ds(block * self.rows + inner.start, inner.size), :] = value.astype(BF16)

    def block_done(self, g, block, mine):
        pass


def attend_back_kernel(*refs):
    ins, rest = refs[:17], refs[17:]
    ig_ref, dwe_ref, dwq_ref, dwk_ref, dwv_ref, dvec_ref = rest[:6]
    scratch = rest[6:]
    acc_e, acc_q, acc_kv = scratch[3:6]
    rows = scratch[1].shape[0]
    table = lax.axis_index("table")
    size = ig_ref.shape[1] // rows
    order = [(lax.rem(table + i, size), i == size) for i in range(1, size + 1)]
    attend_back_core(Alone(ig_ref, rows), order, *ins, dvec_ref, *scratch)

    @pl.when((pl.program_id(0) == pl.num_programs(0) - 1) & (pl.program_id(1) == HEADS - 1))
    def _():
        dwe_ref[...] = acc_e[...].T.astype(BF16)
        dwq_ref[...] = acc_q[...].astype(BF16)
        for h in range(HEADS):
            cols = slice(h * HEAD_DIM, (h + 1) * HEAD_DIM)
            dwk_ref[:, cols] = acc_kv[2 * h * HEAD_DIM : (2 * h + 1) * HEAD_DIM, :].T.astype(BF16)
            dwv_ref[:, cols] = acc_kv[(2 * h + 1) * HEAD_DIM : (2 * h + 2) * HEAD_DIM, :].T.astype(BF16)


class Sums:
    def __init__(self, place, mlp, tail, smalls, igs):
        self.place, self.mlp, self.tail, self.smalls, self.igs = place, mlp, tail, smalls, igs
        self.micro, self.head = pl.program_id(0), pl.program_id(1)
        self.count = len(igs)
        self.todo = {}

    def tick(self, k):
        for m in range(self.count):
            actions = self.todo.get((m, k), [])
            if not actions:
                continue

            @pl.when((self.micro == m) & (self.head == k) if k < HEADS else self.micro == m)
            def _():
                for action in actions:
                    action()

    def start_of_step(self):
        for k in range(HEADS):
            self.tick(k)

    def at(self, m, k, action):
        self.todo.setdefault((m, k), []).append(action)

    def step(self, flows, i):
        def action():
            for flow in flows:
                if i:
                    flow.arrive(i - 1)
                if i < flow.steps:
                    flow.start(i)

        return action

    def pair_done(self):
        for g in range(HEADS // 2):

            @pl.when((self.micro == self.count - 1) & (self.head == 2 * g + 1))
            def _():
                self.write_pair(g)
                self.step(self.tail[g], 0)()

    def put(self, block, mine, inner, value):
        if mine:
            self.ig_own[inner, :] = value
            return
        for m in range(self.count):

            @pl.when(self.micro == m)
            def _():
                self.ig_bufs[m][block, inner, :] = value.astype(BF16)

    def block_done(self, g, block, mine):
        for m in range(self.count):

            @pl.when(self.micro == m)
            def _():
                if mine:
                    self.ig_out[m] = self.ig_own[...]
                else:
                    self.igs[m].start_one(g + 1)

    def ig_finish(self, m):
        def action():
            total = self.ig_out[m]
            for got in self.igs[m].arrive():
                total = total + got[...].astype(F32)
            self.ig_out[m] = total

        return action


def attend_back_reduce_kernel(dp_size, table_size, *refs):
    refs = list(refs)

    def take(n):
        out = refs[:n]
        del refs[:n]
        return out

    ins = take(17)
    grads = take(3)
    (small_in,) = take(1)
    ig_out, small_out, embed_out = take(3)
    totals = take(7)
    (dvec_ref,) = take(1)
    core = take(6)
    acc_e, acc_q, acc_kv = core[3:6]
    place = Place(dp_size, table_size)
    hops = place.hops["dp"]
    steps = len(hops) + len(place.hops["table"]) + 1
    nears = take(3)
    mlp_scratch = [take(steps) for _ in range(3)]
    tail_grads = take(4)
    tail_scratch = [take(len(hops) + 2) for _ in range(4)]
    embed_grad, small_grad = take(2)
    embed_scratch, small_scratch_ = take(3), take(3)
    micro = ig_out.shape[0]
    ig_bufs = take(micro)
    ig_got = take(micro)
    (ig_own,) = take(1)
    near_sem, send_sem, recv_sem = refs
    sems = (send_sem, recv_sem)
    forth, back = hops, hops[:1] + hops[:0:-1]
    base = 0

    def count_up(n):
        nonlocal base
        base += n
        return base - n

    mlp = []
    for order, grad, scratch, near in zip((forth, forth, back), grads, mlp_scratch, nears):
        mlp.append(Shard(place, order, grad, scratch, sems, base, near))
        count_up(mlp[-1].steps)
    tail = []
    for g in range(2):
        pair = []
        for i, order in enumerate((forth, back)):
            at = count_up(quick_sems(dp_size, table_size))
            pair.append(
                QuickShard(place, order, tail_grads[2 * g + i], tail_scratch[2 * g + i], sems, at)
            )
        tail.append(pair)
    others = dp_size + table_size - 2
    embed = Small(place, lambda d: embed_grad.at[d], *embed_scratch, sems, count_up(others))
    small = Small(place, lambda d: small_grad, *small_scratch_, sems, count_up(others))
    igs = []
    for m in range(micro):
        igs.append(
            Swap(
                place, "table", sems, count_up(table_size - 1),
                lambda t, m=m: ig_bufs[m].at[t],
                lambda t, s, m=m: ig_got[m].at[s - 1],
            )
        )
    hooks = Sums(place, mlp, tail, (embed, small), igs)
    hooks.ig_bufs, hooks.ig_own, hooks.ig_out = ig_bufs, ig_own, ig_out

    def write_pair(g):
        one, two = tail_grads[2 * g], tail_grads[2 * g + 1]
        shape = one.shape[:-1]

        def put(ref, at, value):
            ref[:, :, :, at * HEAD_DIM : at * HEAD_DIM + value.shape[1]] = value.astype(BF16).reshape(
                shape + (value.shape[1],)
            )

        def rows_of(h, side):
            at = (2 * h + side) * HEAD_DIM
            return acc_kv[at : at + HEAD_DIM, :].T

        put(one, 0, acc_q[:, 2 * g * HEAD_DIM : (2 * g + 2) * HEAD_DIM])
        put(one, 2, rows_of(2 * g, 0))
        put(two, 0, rows_of(2 * g + 1, 0))
        put(two, 1, rows_of(2 * g, 1))
        put(two, 2, rows_of(2 * g + 1, 1))

    hooks.write_pair = write_pair

    def enter():
        wait_all = place.greet(True)
        for i, flow in enumerate(mlp):
            for copy in flow.near_copies(near_sem.at[i]):
                copy.start()
        wait_all()

    def nears_there():
        for i, flow in enumerate(mlp):
            flow.near_wait(near_sem.at[i])

    last = micro - 1
    hooks.at(0, 0, enter)
    hooks.at(0, 0, hooks.step(mlp, 0))
    hooks.at(0, 2, nears_there)
    hooks.at(0, 2, hooks.step(mlp, 1))
    hooks.at(0, 8, hooks.step(mlp, 2))
    hooks.at(1, 2, hooks.step(mlp, 3))
    hooks.at(1, 4, hooks.ig_finish(0))
    hooks.at(1, 4, hooks.step(mlp, 4))
    hooks.at(2, 1, hooks.step(mlp, 5))
    hooks.at(2, 2, hooks.step(tail[0], 1))
    hooks.at(2, 3, hooks.step(tail[0], 2))
    hooks.at(2, 3, hooks.step(mlp, 6))
    hooks.at(2, 4, hooks.ig_finish(1))
    hooks.at(2, 4, hooks.step(tail[0], 3))
    hooks.at(2, 5, hooks.step(tail[1], 1))
    hooks.at(2, 6, hooks.step(tail[0], 4))
    hooks.at(2, 7, hooks.step(tail[1], 2))

    def finish():
        embed_grad[...] = acc_e[...].T.astype(BF16).reshape(embed_grad.shape)
        small_grad[...] = small_in[...] + jnp.concatenate(
            [dvec_ref[...], jnp.zeros_like(dvec_ref)], axis=0
        )
        ends = [embed, small]
        hooks.step(ends, 0)()
        hooks.step(tail[1], 3)()
        hooks.step(mlp, 7)()
        hooks.step(ends, 1)()
        hooks.step(tail[0], 5)()
        hooks.step(tail[1], 4)()
        hooks.ig_finish(last)()
        hooks.step(ends, 2)()
        hooks.step(tail[1], 5)()
        for flow in mlp + tail[0] + tail[1] + ends + igs:
            flow.sent()
        embed_out[...] = embed.total
        small_out[...] = small.total
        for flow, out in zip(mlp + tail[0] + tail[1], totals):
            out[...] = flow.full[...]

    hooks.at(last, 8, finish)
    hooks.start_of_step()
    order = [(place.at("table", i), i == table_size) for i in range(1, table_size + 1)]
    attend_back_core(hooks, order, *ins, dvec_ref, *core)


def back_scratch(length, rows, width):
    return [
        pltpu.VMEM((2 * width, length), BF16),
        pltpu.VMEM((rows, width), BF16),
        pltpu.VMEM((2 * width, width), BF16),
        pltpu.VMEM((LANES, width), F32),
        pltpu.VMEM((width, width), F32),
        pltpu.VMEM((2 * width, width), F32),
    ]


def back_specs(by_head, cols, varied, fixed):
    return (
        [head_spec(a.shape[2:]) for a in by_head]
        + [head_cols_spec(a.shape[1]) for a in cols]
        + [micro_spec(a.shape[1:]) for a in varied]
        + [const_spec(a.shape) for a in fixed]
    )


def attend_backward(p, linv, k, v, q, gmix, mixed, n, u, inv, x, ghid, wet, vec, wq, wk, wv):
    micro, rows, width = q.shape
    length = k.shape[1]
    varied = (n, u, inv, x, ghid)
    fixed = (wet, vec, wq, wk, wv)
    summed = [(wet.shape, BF16)] + [((width, width), BF16)] * 3 + [((8, width), F32)]
    return pl.pallas_call(
        attend_back_kernel,
        grid=(micro, HEADS),
        in_specs=back_specs((p, linv), (k, v, q, gmix, mixed), varied, fixed),
        out_specs=[micro_spec((length, LANES))] + [const_spec(s) for s, _ in summed],
        out_shape=[jax.ShapeDtypeStruct((micro, length, LANES), BF16)]
        + [jax.ShapeDtypeStruct(s, d) for s, d in summed],
        scratch_shapes=back_scratch(length, rows, width),
        compiler_params=vmem(50),
        name="attend_backward",
    )(p, linv, k, v, q, gmix, mixed, *varied, *fixed)


def attend_backward_reduce(
    dp_size, table_size, grads, small, p, linv, k, v, q, gmix, mixed, n, u, inv, x, ghid, wet, vec, wq, wk, wv
):
    micro, rows, width = q.shape
    length = k.shape[1]
    varied = (n, u, inv, x, ghid)
    fixed = (wet, vec, wq, wk, wv)
    far = pl.BlockSpec(memory_space=pl.ANY)
    shard = width // dp_size
    tail = (dp_size, table_size, shard // table_size, 3 * HEAD_DIM)
    blocks = [g.shape[1:] for g in grads] + [tail[1:]] * 4
    hops = len(hops_of(dp_size)) + len(hops_of(table_size))
    scratch = [pltpu.VMEM((8, width), F32)] + back_scratch(length, rows, width)
    scratch += [pltpu.VMEM((dp_size // 2,) + g.shape[1:], BF16) for g in grads]
    for g in grads:
        scratch += shard_scratch(dp_size, table_size, g.shape[1:], BF16)
    scratch += [pltpu.VMEM(tail, BF16)] * 4
    for _ in range(4):
        scratch += quick_scratch(dp_size, table_size, tail[1:], BF16)
    scratch += [pltpu.VMEM((dp_size, shard, LANES), BF16), pltpu.VMEM(small.shape, F32)]
    scratch += small_scratch(dp_size, table_size, (shard, LANES), BF16)
    scratch += small_scratch(dp_size, table_size, small.shape, F32)
    scratch += [pltpu.VMEM((table_size, rows, LANES), BF16)] * micro
    scratch += [pltpu.VMEM((table_size - 1, rows, LANES), BF16)] * micro
    scratch += [pltpu.VMEM((rows, LANES), F32)]
    count = 3 * (hops + len(hops_of(table_size))) + 4 * quick_sems(dp_size, table_size)
    count += 2 * (dp_size + table_size - 2) + micro * (table_size - 1)
    scratch += [pltpu.SemaphoreType.DMA((3,))] + [pltpu.SemaphoreType.DMA((count,))] * 2
    outs = [((micro, rows, LANES), F32), (small.shape, F32), ((shard, LANES), F32)]
    outs += [(b, BF16) for b in blocks]
    return pl.pallas_call(
        functools.partial(attend_back_reduce_kernel, dp_size, table_size),
        grid=(micro, HEADS),
        in_specs=back_specs((p, linv), (k, v, q, gmix, mixed), varied, fixed)
        + [far] * 3
        + [const_spec(small.shape)],
        out_specs=[const_spec(shape) for shape, _ in outs],
        out_shape=[jax.ShapeDtypeStruct(shape, dtype) for shape, dtype in outs],
        scratch_shapes=scratch,
        compiler_params=vmem(60, collective_id=1, has_side_effects=True),
        name="attend_backward_reduce",
    )(p, linv, k, v, q, gmix, mixed, *varied, *fixed, *grads, small)


def finish_kernel(feat, shard, mask_ref, ig_in, small_in, embed_in, *refs):
    ins, outs = refs[:7], refs[7:]
    ig_out, dwe, dwq, dwk, dwv, dwo, dwu, dwd = outs[:8]
    vecs, bu = outs[8:14], outs[14]
    for m in range(ig_in.shape[0]):
        ig_out[m] = ig_in[m].T[:feat, :] * mask_ref[m].astype(F32)
    dwe[...] = embed_in[:, :feat]
    for src, dst in zip(ins[:3], (dwo, dwu, dwd)):
        dst[...] = src[...].astype(F32)
    for g in range(HEADS // 2):
        one, two = ins[3 + 2 * g], ins[4 + 2 * g]
        at = 2 * g * HEAD_DIM
        dwq[:, at : at + 2 * HEAD_DIM] = one[:, : 2 * HEAD_DIM].astype(F32)
        dwk[:, at : at + HEAD_DIM] = one[:, 2 * HEAD_DIM :].astype(F32)
        dwk[:, at + HEAD_DIM : at + 2 * HEAD_DIM] = two[:, :HEAD_DIM].astype(F32)
        dwv[:, at : at + 2 * HEAD_DIM] = two[:, HEAD_DIM:].astype(F32)
    small = small_in[...]
    width = small.shape[1]
    dp = lax.axis_index("dp")
    turned = pltpu.roll(small, lax.rem(width - dp * shard, width), 1)
    for i, out in enumerate(vecs):
        out[...] = turned[i : i + 1, :shard]
    per_row = width // bu.shape[1]
    rows = small[8 : 8 + 4, :]
    row = dp // per_row
    pick = lax.broadcasted_iota(jnp.int32, rows.shape, 0) == row
    line = jnp.sum(jnp.where(pick, rows, 0.0), axis=0, keepdims=True)
    at = (dp % per_row) * bu.shape[1]
    bu[...] = pltpu.roll(jnp.broadcast_to(line, (8, width)), lax.rem(width - at, width), 1)[:1, : bu.shape[1]]


def finish(feat, ff_shard, mask, ig, small, embed, totals):
    micro, rows, _ = ig.shape
    shard = embed.shape[0]
    width = small.shape[1]
    out_shape = (
        [jax.ShapeDtypeStruct((micro, feat, rows), F32), jax.ShapeDtypeStruct((shard, feat), F32)]
        + [jax.ShapeDtypeStruct((shard, width), F32)] * 3
        + [jax.ShapeDtypeStruct(t.shape, F32) for t in totals[:3]]
        + [jax.ShapeDtypeStruct((1, shard), F32)] * 6
        + [jax.ShapeDtypeStruct((1, ff_shard), F32)]
    )
    return pl.pallas_call(
        functools.partial(finish_kernel, feat, shard),
        out_shape=out_shape,
        compiler_params=vmem(60),
        name="finish",
    )(mask, ig, small, embed, *totals)


def body(
    dp_size, table_size, features, feature_mask, support_count, embed_weight, embed_bias, gain_first, shift_first,
    query_weight, key_weight, value_weight, out_weight, gain_second, shift_second, up_weight, up_bias,
    down_weight, down_bias, cotangent,
):
    micro, _, rows, feat = features.shape
    shard, width = query_weight.shape
    hidden_units = up_weight.shape[1]
    ff_shard = up_bias.shape[0]
    features, cotangent, support = features[:, 0], cotangent[:, 0], support_count[:, 0]
    vectors = (embed_bias, gain_first, shift_first, gain_second, shift_second, down_bias)
    if 2 * shard == LANES and micro == 3 and table_size == 4:
        got = attend_forward_gather(
            dp_size, table_size, support, features.transpose(0, 2, 1), feature_mask, embed_weight.T,
            [a[None] for a in vectors], up_bias.reshape(-1, LANES),
            query_weight, key_weight, value_weight, out_weight, up_weight, down_weight,
        )
        q, k, v, n, u, inv, emb, mixed, p, linv, x = got[:11]
        wet, wq, wk, wv = (g.reshape(-1, g.shape[-1]) for g in got[11:15])
        vec, bu = got[15:17]
        wo, wu, wd = (g.reshape(-1, g.shape[-1]) for g in got[17:])
        activations, ghid, gmix, dwo, dwu, dwd, small = mlp_both(mixed, emb, cotangent, wo, wu, wd, vec, bu)
        grads = [g.reshape(dp_size, table_size, -1, g.shape[1]) for g in (dwo, dwu, dwd)]
        ig, small, embed, *totals = attend_backward_reduce(
            dp_size, table_size, grads, small, p, linv, k, v, q, gmix, mixed, n, u, inv, x, ghid,
            wet, vec, wq, wk, wv,
        )
        totals = [t.reshape(-1, t.shape[-1]) for t in totals]
        out = finish(feat, ff_shard, feature_mask.reshape(micro, feat, 1), ig, small, embed, totals)
        ig, dwe, dwq, dwk, dwv, dwo, dwu, dwd = out[:8]
        ig, dwe = ig.transpose(0, 2, 1), dwe.T
        smalls = [o.reshape(-1) for o in out[8:14]]
        dbu = out[14].reshape(-1)
    else:
        smalls = jnp.stack(vectors)
        mask = jnp.pad(feature_mask[:, 0], ((0, 0), (0, LANES - feat)))[:, None, :]
        x = jnp.pad(features, ((0, 0), (0, 0), (0, LANES - feat))) * mask.astype(BF16)
        wet = jnp.pad(embed_weight, ((0, LANES - feat), (0, 0))).T
        shards = [wet, query_weight, key_weight, value_weight, out_weight, up_weight, down_weight]
        wet, wq, wk, wv, wo, wu, wd = (lax.all_gather(s, "dp", axis=0, tiled=True) for s in shards)
        vec = jnp.pad(lax.all_gather(smalls, "dp", axis=1, tiled=True).astype(F32), ((0, 2), (0, 0)))
        bu = lax.all_gather(up_bias, "dp", axis=0, tiled=True).astype(F32)[None]
        x = lax.all_gather(x, "table", axis=1, tiled=True)
        q, k, v, n, u, inv, emb, mixed, p, linv = attend_forward(support, x, wet, vec, wq, wk, wv, rows)
        activations, ghid, gmix, dwo, dwu, dwd, small = mlp_both(mixed, emb, cotangent, wo, wu, wd, vec, bu)
        ig, dwe, dwq, dwk, dwv, dvec = attend_backward(
            p, linv, k, v, q, gmix, mixed, n, u, inv, x, ghid, wet, vec, wq, wk, wv
        )
        big = [dwe, dwq, dwk, dwv, dwo, dwu, dwd]
        own = [lax.psum_scatter(g.astype(F32), "dp", scatter_dimension=0, tiled=True) for g in big]
        dwe, dwq, dwk, dwv, dwo, dwu, dwd = (lax.psum(g, "table") for g in own)
        dwe = dwe[:, :feat].T
        dvec = jnp.concatenate([dvec[:3], small[3:6]])
        smalls = lax.psum(lax.psum_scatter(dvec, "dp", scatter_dimension=1, tiled=True), "table")
        dbu = small[8:].reshape(-1)[:hidden_units]
        dbu = lax.psum(lax.psum_scatter(dbu, "dp", scatter_dimension=0, tiled=True), "table")
        ig = lax.psum_scatter(ig.astype(F32) * mask, "table", scatter_dimension=1, tiled=True)[:, :, :feat]
    return (
        activations[:, None], ig[:, None], dwe, smalls[0], smalls[1], smalls[2],
        dwq, dwk, dwv, dwo, smalls[3], smalls[4], dwu, dbu, dwd, smalls[5],
    )


def solution(mesh):
    rows, cols, vecs = P("dp", None), P(None, "dp"), P("dp")
    table = P(None, "dp", "table", None)
    return jax.shard_map(
        functools.partial(body, mesh.shape["dp"], mesh.shape["table"]),
        mesh=mesh,
        in_specs=(
            table, P(None, "dp", None), cols, cols, vecs, vecs, vecs, rows, rows, rows, rows,
            vecs, vecs, rows, vecs, rows, vecs, table,
        ),
        out_specs=(
            table, table, cols, vecs, vecs, vecs, rows, rows, rows, rows, vecs, vecs, rows, vecs, rows, vecs,
        ),
        check_vma=False,
    )
```

```python
import functools

import jax
import jax.numpy as jnp
from jax import lax
from jax.experimental import pallas as pl
from jax.experimental.pallas import tpu as pltpu
from jax.sharding import PartitionSpec as P

HEADS = 4
HEAD_DIM = 128
LANES = 128
EPSILON = 1e-5
SCALE = HEAD_DIM**-0.5
LOG2E = 1.4426950408889634
ROW_BLOCK = 256
KEY_BLOCK = 512
BACK_BLOCK = 256
GROUPS = 4
NORM_BLOCK = 256
HEADS_STEP = 2
PAIRS = HEADS // HEADS_STEP
CHUNKS = 4
TABLE_STEPS = 3
INV_SQRT_TWO = 0.7071067811865476
INV_SQRT_TWO_PI = 0.3989422804014327
BF16 = jnp.bfloat16
F32 = jnp.float32
MESH = pl.DeviceIdType.MESH


def dot_nn(a, b):
    return lax.dot_general(a, b, (((1,), (0,)), ((), ())), preferred_element_type=F32)


def dot_nt(a, b):
    return lax.dot_general(a, b, (((1,), (1,)), ((), ())), preferred_element_type=F32)


def dot_tn(a, b):
    return lax.dot_general(a, b, (((0,), (0,)), ((), ())), preferred_element_type=F32)


def norm_parts(v):
    mean = jnp.mean(v, axis=-1, keepdims=True)
    centred = v - mean
    inv = lax.rsqrt(jnp.mean(centred * centred, axis=-1, keepdims=True) + EPSILON)
    return centred * inv, inv


def norm_back(grad, unit, inv, gain):
    q = grad * gain
    return inv * (
        q
        - jnp.mean(q, axis=-1, keepdims=True)
        - unit * jnp.mean(q * unit, axis=-1, keepdims=True)
    )


def row_sum(v):
    return jnp.sum(v, axis=0, keepdims=True)


def const_spec(shape):
    return pl.BlockSpec(shape, lambda *g: (0,) * len(shape))


def micro_spec(shape):
    return pl.BlockSpec((1,) + shape, lambda m, *g: (m,) + (0,) * len(shape))


def head_spec(shape):
    return pl.BlockSpec((1, 1) + shape, lambda m, h: (m, h) + (0,) * len(shape))


def heads_spec(shape):
    return pl.BlockSpec((1, HEADS_STEP) + shape, lambda m, h: (m, h) + (0,) * len(shape))


def head_cols_spec(rows):
    return pl.BlockSpec((1, rows, HEAD_DIM), lambda m, h: (m, 0, h))


def vmem(mib, **extra):
    return pltpu.CompilerParams(vmem_limit_bytes=mib * 2**20, **extra)


def toggled(index, hop):
    return index + hop * (1 - 2 * ((index // hop) % 2))


def toggled_by(index, hops):
    for hop in hops:
        index = toggled(index, hop)
    return index


def subsets(hops):
    out = [()]
    for hop in hops:
        out = out + [s + (hop,) for s in out]
    return out


def hops_of(size):
    return [1 << i for i in range(size.bit_length() - 1)]


class Place:
    def __init__(self, dp_size, table_size):
        self.size = {"dp": dp_size, "table": table_size}
        self.hops = {axis: hops_of(n) for axis, n in self.size.items()}
        self.me = {"dp": lax.axis_index("dp"), "table": lax.axis_index("table")}

    def partner(self, axis, hop):
        there = dict(self.me)
        there[axis] = toggled(there[axis], hop)
        return (there["dp"], there["table"])

    def at(self, axis, shift):
        n = self.size[axis]
        return lax.rem(self.me[axis] + (shift + n), n)

    def ahead(self, axis, shift):
        there = dict(self.me)
        there[axis] = self.at(axis, shift)
        return (there["dp"], there["table"])

    def greet(self, all_dp):
        barrier = pltpu.get_barrier_semaphore()
        peers = [self.ahead("table", s) for s in range(1, self.size["table"])]
        if all_dp:
            peers += [self.ahead("dp", s) for s in range(1, self.size["dp"])]
        else:
            peers += [self.partner("dp", hop) for hop in self.hops["dp"]]
        for peer in peers:
            pl.semaphore_signal(barrier, inc=1, device_id=peer, device_id_type=MESH)
        return lambda: pl.semaphore_wait(barrier, len(peers))


class Swap:
    def __init__(self, place, axis, sems, base, send, put):
        self.place, self.axis, self.sems, self.base = place, axis, sems, base
        self.send, self.put = send, put
        self.shifts = range(1, place.size[axis])

    def copy(self, shift, src, dst):
        index = self.base + shift - 1
        return pltpu.make_async_remote_copy(
            src_ref=src, dst_ref=dst, send_sem=self.sems[0].at[index], recv_sem=self.sems[1].at[index],
            device_id=self.place.ahead(self.axis, shift), device_id_type=MESH,
        )

    def start_one(self, shift):
        to = self.place.at(self.axis, shift)
        self.copy(shift, self.send(to), self.put(self.place.me[self.axis], shift)).start()

    def start(self):
        for shift in self.shifts:
            self.start_one(shift)

    def arrive_one(self, shift):
        here = self.put(self.place.at(self.axis, -shift), shift)
        self.copy(shift, here, here).wait_recv()
        return here

    def arrive(self):
        return [self.arrive_one(shift) for shift in self.shifts]

    def sent(self):
        for shift in self.shifts:
            out = self.send(self.place.at(self.axis, shift))
            self.copy(shift, out, out).wait_send()


def remote(place, axis, hop, src, dst, sems, index):
    return pltpu.make_async_remote_copy(
        src_ref=src, dst_ref=dst, send_sem=sems[0].at[index], recv_sem=sems[1].at[index],
        device_id=place.partner(axis, hop), device_id_type=MESH,
    )


class Gather:
    def __init__(self, place, axis, hops, full, sems, base, own=None):
        self.place, self.axis, self.hops = place, axis, hops
        self.full, self.sems, self.base, self.own = full, sems, base, own
        self.steps = len(hops)

    def whole(self, step):
        part = self.full.at[pl.ds(0, 1 << step)]
        return remote(self.place, self.axis, self.hops[step], part, part, self.sems, self.base + step)

    def start(self, step):
        for s in subsets(self.hops[:step]):
            block = self.full.at[toggled_by(self.place.me[self.axis], s)]
            src = block if s or self.own is None else self.own
            remote(
                self.place, self.axis, self.hops[step], src, block, self.sems, self.base + step
            ).start()

    def arrive(self, step):
        self.whole(step).wait_recv()

    def sent(self):
        for step in range(self.steps):
            self.whole(step).wait_send()


def add_into(into, other):
    into[...] = (into[...].astype(F32) + other[...].astype(F32)).astype(into.dtype)


class Reduce:
    def __init__(self, place, axis, hops, blocks, bufs, sems, base):
        self.place, self.axis, self.hops = place, axis, hops
        self.held = blocks
        self.bufs, self.sems, self.base = bufs, sems, base
        self.steps = len(hops)

    def mine(self, step, s):
        if step == 0:
            return self.held(s)
        order = [set(t) for t in subsets(self.hops[step:])]
        return self.bufs[step - 1].at[order.index(set(s))]

    def copy(self, step, src, dst):
        return remote(self.place, self.axis, self.hops[step], src, dst, self.sems, self.base + step)

    def start(self, step):
        for i, s in enumerate(subsets(self.hops[step + 1 :])):
            self.copy(step, self.mine(step, s + (self.hops[step],)), self.bufs[step].at[i]).start()

    def arrive(self, step):
        self.copy(step, self.bufs[step], self.bufs[step]).wait_recv()
        for i, s in enumerate(subsets(self.hops[step + 1 :])):
            add_into(self.bufs[step].at[i], self.mine(step, s))

    def total(self):
        return self.bufs[-1].at[0]

    def sent_one(self, step):
        self.copy(step, self.bufs[step], self.bufs[step]).wait_send()


class QuickShard:
    def __init__(self, place, dp_hops, blocks, scratch, sems, base, back_only=False):
        n = len(dp_hops)
        self.place, self.full, self.blocks = place, scratch[-1], blocks
        got = None if back_only else scratch[n]
        self.dp = Reduce(place, "dp", dp_hops, blocks, scratch[:n], sems, base)
        base += n
        self.out = self.back = None
        if not back_only:
            self.out = Swap(
                place, "table", sems, base, lambda t: self.dp_total().at[t], lambda t, s: got.at[s - 1]
            )
            base += place.size["table"] - 1
        self.back = Swap(
            place, "table", sems, base, lambda t: self.full.at[place.me["table"]], lambda t, s: self.full.at[t]
        )
        self.stages = [(self.dp, i) for i in range(n)] + ([] if back_only else [(self.out, 0)]) + [(self.back, 0)]
        self.steps = len(self.stages)
        self.done = 0

    def dp_total(self):
        return self.dp.total() if self.dp.steps else self.blocks(())

    def start(self, step):
        flow, i = self.stages[step]
        self.done = max(self.done, step + 1)
        if flow is self.dp:
            flow.start(i)
            return
        if flow is self.back and self.out is None:
            self.full[self.place.me["table"]] = self.blocks(())[...]
        flow.start()

    def arrive(self, step):
        flow, i = self.stages[step]
        if flow is self.dp:
            flow.arrive(i)
        elif flow is self.out:
            me = self.place.me["table"]
            total = self.dp_total()[me].astype(F32)
            for got in flow.arrive():
                total = total + got[...].astype(F32)
            self.full[me] = total.astype(self.full.dtype)
        else:
            flow.arrive()

    def sent(self):
        for flow, i in self.stages[: self.done]:
            if flow is self.dp:
                flow.sent_one(i)
            else:
                flow.sent()


def quick_scratch(dp_hops, table_size, block, dtype, back_only=False):
    out = [pltpu.VMEM((1 << (dp_hops - 1 - i),) + block, dtype) for i in range(dp_hops)]
    if not back_only:
        out.append(pltpu.VMEM((table_size - 1,) + block[1:], dtype))
    return out + [pltpu.VMEM(block, dtype)]


def quick_sems(dp_hops, table_size, back_only=False):
    return dp_hops + (1 if back_only else 2) * (table_size - 1)


class Small:
    def __init__(self, place, block, got_dp, part, got_table, sems, base):
        self.place, self.block, self.part = place, block, part
        self.first = Swap(place, "dp", sems, base, block, lambda t, s: got_dp.at[s - 1])
        base += place.size["dp"] - 1
        self.second = Swap(
            place, "table", sems, base, lambda t: part, lambda t, s: got_table.at[s - 1]
        )
        self.steps = 2

    def start(self, step):
        (self.first, self.second)[step].start()

    def arrive(self, step):
        if step == 0:
            total = self.block(self.place.me["dp"])[...].astype(F32)
            for got in self.first.arrive():
                total = total + got[...].astype(F32)
            self.part[...] = total.astype(self.part.dtype)
        else:
            total = self.part[...].astype(F32)
            for got in self.second.arrive():
                total = total + got[...].astype(F32)
            self.total = total

    def sent(self):
        self.first.sent()
        self.second.sent()


def small_scratch(dp_size, table_size, block, dtype):
    return [
        pltpu.VMEM((dp_size - 1,) + block, dtype),
        pltpu.VMEM(block, dtype),
        pltpu.VMEM((table_size - 1,) + block, dtype),
    ]


def attend_core(
    support, project_all, wq, q_ref, k_ref, v_ref, n_ref, emb_ref, mixed_ref, mixed_low_ref, p_ref, linv_ref, s_bufs, get_x, wet,
):
    length, rows = n_ref.shape[1], q_ref.shape[1]
    own = lax.axis_index("table")

    @pl.when(pl.program_id(1) == 0)
    def _():
        project_all()
        here = pl.ds(pl.multiple_of(own * rows, rows), rows)
        emb_ref[0] = dot_nt(get_x(own, slice(0, rows)), wet())
        q_ref[0] = dot_nn(n_ref[0, here, :], wq()).astype(BF16)

    block = s_bufs[0].shape[0]
    sure = length - rows
    columns = sure + lax.broadcasted_iota(jnp.int32, (1, rows), 1)
    allowed = columns < support
    heads = p_ref.shape[1]
    units = [(h, i) for h in range(heads) for i in range(rows // block)]
    first_head = pl.program_id(1) * heads

    def cols_of(h):
        return pl.ds(pl.multiple_of((first_head + h) * HEAD_DIM, HEAD_DIM), HEAD_DIM)

    def score(j):
        h, i = units[j]
        q = q_ref[0, i * block : (i + 1) * block, cols_of(h)]
        s_bufs[j % 2][...] = dot_nt(q, k_ref[0, :, cols_of(h)])

    score(0)
    for j, (h, i) in enumerate(units):
        if j + 1 < len(units):
            score(j + 1)
        at = slice(i * block, (i + 1) * block)
        first = s_bufs[j % 2][:, :sure]
        last = jnp.where(allowed, s_bufs[j % 2][:, sure:], -1e30)
        top = jnp.maximum(
            jnp.max(first, axis=-1, keepdims=True), jnp.max(last, axis=-1, keepdims=True)
        )
        pf = jnp.exp2((first - top) * (SCALE * LOG2E))
        pt = jnp.exp2((last - top) * (SCALE * LOG2E))
        total = jnp.sum(pf, axis=-1, keepdims=True) + jnp.sum(pt, axis=-1, keepdims=True)
        pf, pt = pf.astype(BF16), pt.astype(BF16)
        p_ref[0, h, at, :sure] = pf
        p_ref[0, h, at, sure:] = pt
        linv = 1.0 / total
        linv_ref[0, h, at, :] = jnp.broadcast_to(linv, (block, LANES))
        out = dot_nn(pf, v_ref[0, :sure, cols_of(h)]) + dot_nn(pt, v_ref[0, sure:, cols_of(h)])
        out = out * linv
        mixed_ref[0, at, cols_of(h)] = out
        mixed_low_ref[0, at, cols_of(h)] = out.astype(BF16)


def project(blocks, rows, get_x, wet, vec_ref, wk, wv, k_ref, v_ref, n_ref, e_bufs):
    gain, shift = vec_ref[1:2, :], vec_ref[2:3, :]
    chunk = e_bufs[0].shape[0]
    units = [(b, i) for b in blocks for i in range(rows // chunk)]

    def embed(j):
        b, i = units[j]
        e_bufs[j % 2][...] = dot_nt(get_x(b, slice(i * chunk, (i + 1) * chunk)), wet())

    embed(0)
    for j, (b, i) in enumerate(units):
        if j + 1 < len(units):
            embed(j + 1)
        at = pl.ds(pl.multiple_of(b * rows + i * chunk, chunk), chunk)
        unit, _ = norm_parts(e_bufs[j % 2][...])
        normed = (unit * gain + shift).astype(BF16)
        n_ref[0, at, :] = normed
        k_ref[0, at, :] = dot_nn(normed, wk()).astype(BF16)
        v_ref[0, at, :] = dot_nn(normed, wv()).astype(BF16)


def attend_kernel(support_ref, x_ref, wet_ref, vec_ref, wq_ref, wk_ref, wv_ref, *rest):
    outs, bufs = rest[:9], rest[9:]
    q_ref, k_ref, v_ref, n_ref = outs[:4]
    rows = q_ref.shape[1]

    def get_x(block, part):
        at = pl.ds(pl.multiple_of(block * rows + part.start, NORM_BLOCK), part.stop - part.start)
        return x_ref[0, at, :]

    def project_all():
        project(
            range(x_ref.shape[1] // rows), rows, get_x, lambda: wet_ref[...], vec_ref,
            lambda: wk_ref[...], lambda: wv_ref[...], k_ref, v_ref, n_ref, bufs[:2],
        )

    attend_core(
        support_ref[pl.program_id(0)], project_all, lambda: wq_ref[...], *outs, bufs[2:], get_x, lambda: wet_ref[...]
    )


def attend_scratch(length, width):
    return [pltpu.VMEM((NORM_BLOCK, width), F32)] * 2 + [pltpu.VMEM((ROW_BLOCK, length), F32)] * 2


def attend_gather_kernel(
    dp_size, table_size, support_ref, feat_ref, mask_ref, ew_ref,
    v0_ref, v1_ref, v2_ref, v3_ref, v4_ref, v5_ref, ub_ref, wq_in, wk_in, wv_in, wo_in, wu_in, wd_in,
    q_ref, k_ref, v_ref, n_ref, emb_ref, mixed_ref, mixed_low_ref, p_ref, linv_ref,
    x_out, wet_out, wq_out, wk_out, wv_out, vec_ref, bu_ref, wo_out, wu_out, wd_out,
    x_buf, wet_buf, packed_buf, wq_buf, wk_buf, wv_buf, e_one, e_two, s_one, s_two, own_sem, send_sem, recv_sem,
):
    micro_id, head = pl.program_id(0), pl.program_id(1)
    micro, feat, rows = feat_ref.shape
    shard = wq_in.shape[0]
    width = wq_in.shape[1]
    place = Place(dp_size, table_size)
    dp, table = place.me["dp"], place.me["table"]
    sems = (send_sem, recv_sem)
    hops = place.hops["dp"]
    forth, back = hops[1:] + hops[:1], hops[:0:-1] + hops[:1]
    last = len(hops) - 1
    base = 0

    def gather(order, full, own=None):
        nonlocal base
        flow = Gather(place, "dp", order, full, sems, base, own)
        base += flow.steps
        return flow

    early = [
        gather(forth, wk_buf),
        gather(back, wv_buf),
        gather(forth, wet_buf),
        gather(back, packed_buf),
    ]
    query = gather(forth, wq_buf)
    late = [gather(forth, wo_out, wo_in), gather(forth, wu_out, wu_in), gather(back, wd_out, wd_in)]
    feats = []
    for m in range(micro):
        own_x = x_buf.at[m, table]
        feats.append(
            Swap(
                place, "table", sems, base,
                lambda t, own_x=own_x: own_x,
                lambda t, s, m=m: x_buf.at[m, t],
            )
        )
        base += table_size - 1
    own_copies = [
        pltpu.make_async_copy(src, dst.at[dp], own_sem.at[i])
        for i, (src, dst) in enumerate(((wo_in, wo_out), (wu_in, wu_out), (wd_in, wd_out)))
    ]
    out_copies = [
        pltpu.make_async_copy(src, dst, own_sem.at[3 + i])
        for i, (src, dst) in enumerate(
            ((wet_buf, wet_out), (wq_buf, wq_out), (wk_buf, wk_out), (wv_buf, wv_out))
        )
    ]

    def at_step(m, h):
        return pl.when((micro_id == m) & (head == h))

    @at_step(0, 0)
    def _():
        wait_all = place.greet(False)
        packed_buf[dp] = jnp.zeros((8, LANES), F32)
        for i, ref in enumerate((v0_ref, v1_ref, v2_ref, v3_ref, v4_ref, v5_ref)):
            packed_buf[dp, i : i + 1, :shard] = ref[...].astype(F32)
        place_of = lax.broadcasted_iota(jnp.int32, (LANES, LANES), 0) == feat
        bias = jnp.where(place_of, jnp.broadcast_to(packed_buf[dp, 0:1, :], (LANES, LANES)), 0.0)
        wet_buf[dp] = bias.T[:shard, :].astype(BF16)
        wet_buf[dp, :, :feat] = ew_ref[...]
        packed_buf[dp, 6:8, :] = ub_ref[...].astype(F32)
        wk_buf[dp] = wk_in[...]
        wv_buf[dp] = wv_in[...]
        wq_buf[dp] = wq_in[...]

        def fill(m):
            tall = jnp.concatenate(
                [feat_ref[m].astype(F32), jnp.zeros((LANES - feat, rows), F32)], axis=0
            ).T
            lane = lax.broadcasted_iota(jnp.int32, (rows, LANES), 1)
            x_buf[m, table] = jnp.where(lane == feat, 1.0, 0.0).astype(BF16)
            x_buf[m, table, :, :feat] = (tall[:, :feat] * mask_ref[m].astype(F32)).astype(BF16)

        fill(0)
        wait_all()
        for flow in early:
            flow.start(0)
        feats[0].start()
        for copy in own_copies:
            copy.start()
        for m in range(1, micro):
            fill(m)
        for step in range(last):
            for flow in early:
                flow.arrive(step)
                flow.start(step + 1)
            if step == 0:
                query.start(0)
            else:
                query.arrive(step - 1)
                query.start(step)
        for flow in early:
            flow.arrive(last)
        for flow in late:
            flow.start(0)
        lane = lax.broadcasted_iota(jnp.int32, (8, LANES), 1)
        for d in range(0, dp_size, 2):
            pair = jnp.where(lane < shard, packed_buf[d], pltpu.roll(packed_buf[d + 1], shard, 1))
            vec_ref[:, d * shard : (d + 2) * shard] = pair
        for d in range(dp_size):
            bu_ref[:, 2 * d * LANES : (2 * d + 1) * LANES] = packed_buf[d, 6:7, :]
            bu_ref[:, (2 * d + 1) * LANES : (2 * d + 2) * LANES] = packed_buf[d, 7:8, :]

    @at_step(0, 1)
    def _():
        for flow in late:
            flow.arrive(0)
            flow.start(1)
        for copy in out_copies:
            copy.start()

    @at_step(1, 0)
    def _():
        feats[1].arrive()
        feats[2].start()

    @at_step(2, 0)
    def _():
        feats[2].arrive()
        for flow in late:
            flow.arrive(1)
            flow.start(2)

    def get_x(block, part):
        return x_buf[micro_id, block, part, :]

    shifts = sorted(range(1, table_size), key=lambda s: (min(s, table_size - s), s))

    def full(buf):
        return lambda: buf[...].reshape(-1, buf.shape[-1])

    def some(blocks):
        project(
            blocks, rows, get_x, full(wet_buf), vec_ref, full(wk_buf), full(wv_buf), k_ref, v_ref, n_ref, (e_one, e_two)
        )

    def project_all():
        @pl.when(micro_id == 0)
        def _():
            query.arrive(last - 1)
            query.start(last)
            for shift in shifts:
                feats[0].arrive_one(shift)
            feats[1].start()
            query.arrive(last)

        some([place.at("table", shift) for shift in range(table_size)])

        x_out[0] = x_buf[micro_id].reshape(x_out.shape[1:])

    attend_core(
        support_ref[micro_id], project_all, full(wq_buf),
        q_ref, k_ref, v_ref, n_ref, emb_ref, mixed_ref, mixed_low_ref, p_ref, linv_ref, (s_one, s_two), get_x, full(wet_buf),
    )

    @at_step(micro - 1, HEADS // HEADS_STEP - 1)
    def _():
        for flow in late:
            flow.arrive(2)
        for flow in feats + early + [query] + late:
            flow.sent()
        for copy in own_copies + out_copies:
            copy.wait()


def attend_shapes(rows, length, width):
    out = [
        ((rows, width), BF16),
        ((length, width), BF16),
        ((length, width), BF16),
        ((length, width), BF16),
        ((rows, width), F32),
        ((rows, width), F32),
        ((rows, width), BF16),
    ]
    return out, [((rows, length), BF16), ((rows, LANES), F32)]


def attend_forward_gather(dp_size, table_size, support, feat, mask, ew, vecs, ub, wq, wk, wv, wo, wu, wd):
    micro, _, rows = feat.shape
    length = rows * table_size
    width = wq.shape[1]
    out, heads = attend_shapes(rows, length, width)
    whole = pl.BlockSpec(memory_space=pltpu.VMEM)
    far = pl.BlockSpec(memory_space=pl.ANY)

    def gathered(a):
        return jax.ShapeDtypeStruct((dp_size,) + a.shape, a.dtype)

    wet = jax.ShapeDtypeStruct((dp_size, wq.shape[0], LANES), BF16)
    count = micro * (table_size - 1) + 8 * len(hops_of(dp_size))
    return pl.pallas_call(
        functools.partial(attend_gather_kernel, dp_size, table_size),
        grid=(micro, HEADS // HEADS_STEP),
        in_specs=[pl.BlockSpec(memory_space=pltpu.SMEM)] + [whole] * 13 + [far] * 3,
        out_specs=[micro_spec(s) for s, _ in out]
        + [heads_spec(s) for s, _ in heads]
        + [micro_spec((length, LANES))]
        + [far] * 4
        + [const_spec((8, width)), const_spec((1, wu.shape[1]))]
        + [far] * 3,
        out_shape=[jax.ShapeDtypeStruct((micro,) + s, d) for s, d in out]
        + [jax.ShapeDtypeStruct((micro, HEADS) + s, d) for s, d in heads]
        + [jax.ShapeDtypeStruct((micro, length, LANES), BF16)]
        + [wet, gathered(wq), gathered(wk), gathered(wv)]
        + [jax.ShapeDtypeStruct((8, width), F32), jax.ShapeDtypeStruct((1, wu.shape[1]), F32)]
        + [gathered(wo), gathered(wu), gathered(wd)],
        scratch_shapes=[
            pltpu.VMEM((micro, table_size, rows, LANES), BF16),
            pltpu.VMEM(wet.shape, BF16),
            pltpu.VMEM((dp_size, 8, LANES), F32),
            pltpu.VMEM((dp_size,) + wq.shape, BF16),
            pltpu.VMEM((dp_size,) + wk.shape, BF16),
            pltpu.VMEM((dp_size,) + wv.shape, BF16),
            *attend_scratch(length, width),
            pltpu.SemaphoreType.DMA((7,)),
            pltpu.SemaphoreType.DMA((count,)),
            pltpu.SemaphoreType.DMA((count,)),
        ],
        compiler_params=vmem(60, collective_id=0, has_side_effects=True),
        name="attend_forward_gather",
    )(support, feat, mask, ew, *vecs, ub, wq, wk, wv, wo, wu, wd)


def attend_forward(support, x_all, wet, vec, wq, wk, wv, rows):
    micro, length, lanes = x_all.shape
    width = wq.shape[0]
    out, heads = attend_shapes(rows, length, width)
    return pl.pallas_call(
        attend_kernel,
        grid=(micro, HEADS // HEADS_STEP),
        in_specs=[
            pl.BlockSpec(memory_space=pltpu.SMEM),
            micro_spec((length, lanes)),
            const_spec(wet.shape),
            const_spec(vec.shape),
            const_spec(wq.shape),
            const_spec(wk.shape),
            const_spec(wv.shape),
        ],
        out_specs=[micro_spec(s) for s, _ in out] + [heads_spec(s) for s, _ in heads],
        out_shape=[jax.ShapeDtypeStruct((micro,) + s, d) for s, d in out]
        + [jax.ShapeDtypeStruct((micro, HEADS) + s, d) for s, d in heads],
        scratch_shapes=attend_scratch(length, width),
        compiler_params=vmem(58),
        name="attend_forward",
    )(support, x_all, wet, vec, wq, wk, wv)


def mlp_kernel(
    mixed_ref, emb_ref, cot_ref, wo_ref, wu_ref, wd_ref, vec_ref, bu_ref,
    act_ref, ghid_ref, gmix_ref, dwo_ref, dwu_ref, dwd_ref, dvec_ref,
    acc_o, acc_u, acc_d, gn2_ref, out_ref, *bufs,
):
    step, last = pl.program_id(0), pl.num_programs(0) - 1
    hidden_units = wu_ref.shape[1]
    chunk = 512

    @pl.when(step == 0)
    def _():
        acc_o[...] = jnp.zeros_like(acc_o)
        acc_u[...] = jnp.zeros_like(acc_u)
        acc_d[...] = jnp.zeros_like(acc_d)
        dvec_ref[...] = jnp.zeros_like(dvec_ref)

    gain, shift, dbias = vec_ref[3:4, :], vec_ref[4:5, :], vec_ref[5:6, :]
    mixed = mixed_ref[0]
    g_out = cot_ref[0]
    hidden = emb_ref[0] + dot_nn(mixed, wo_ref[...])
    unit, inv = norm_parts(hidden)
    normed = (unit * gain + shift).astype(BF16)
    out_ref[...] = hidden + dbias
    normed_t = normed.T
    g_out_t = g_out.T
    chunks = hidden_units // chunk

    def products(f):
        cols = slice(f * chunk, (f + 1) * chunk)
        bufs[2 * (f % 2)][...] = dot_nn(normed, wu_ref[:, cols])
        bufs[2 * (f % 2) + 1][...] = dot_nt(g_out, wd_ref[cols, :])

    products(0)
    for f in range(chunks):
        if f + 1 < chunks:
            products(f + 1)
        cols = slice(f * chunk, (f + 1) * chunk)
        pre = bufs[2 * (f % 2)][...] + bu_ref[:, cols]
        g_act = bufs[2 * (f % 2) + 1][...]
        cdf = 0.5 * (1.0 + lax.erf(pre * INV_SQRT_TWO))
        pdf = jnp.exp(-0.5 * pre * pre) * INV_SQRT_TWO_PI
        act = (pre * cdf).astype(BF16)
        out_ref[...] += dot_nn(act, wd_ref[cols, :])
        acc_d[:, cols] += dot_nn(g_out_t, act)
        g_pre_f = g_act * (cdf + pre * pdf)
        g_pre = g_pre_f.astype(BF16)
        acc_u[:, cols] += dot_nn(normed_t, g_pre)
        dvec_ref[8 + f : 9 + f, :] += row_sum(g_pre_f)
        g_part = dot_nt(g_pre, wu_ref[:, cols])
        if f == 0:
            gn2_ref[...] = g_part
        else:
            gn2_ref[...] += g_part
    act_ref[0] = out_ref[...].astype(BF16)
    g_norm = gn2_ref[...]
    g_out_f = g_out.astype(F32)
    dvec_ref[3:4, :] += row_sum(g_norm * unit)
    dvec_ref[4:5, :] += row_sum(g_norm)
    dvec_ref[5:6, :] += row_sum(g_out_f)
    g_hidden = g_out_f + norm_back(g_norm, unit, inv, gain)
    ghid_ref[0] = g_hidden
    branch = g_hidden.astype(BF16)
    acc_o[...] += dot_tn(mixed, branch)
    gmix_ref[0] = dot_nt(branch, wo_ref[...]).astype(BF16)

    @pl.when(step == last)
    def _():
        dwo_ref[...] = acc_o[...].astype(BF16)
        dwu_ref[...] = acc_u[...].astype(BF16)
        for f in range(hidden_units // chunk):
            cols = slice(f * chunk, (f + 1) * chunk)
            dwd_ref[cols, :] = acc_d[:, cols].T.astype(BF16)


def mlp_both(mixed, emb, cot, wo, wu, wd, vec, bu):
    micro, rows, width = mixed.shape
    hidden_units = wu.shape[1]
    per_micro = [((rows, width), BF16), ((rows, width), F32), ((rows, width), BF16)]
    summed = [
        ((width, width), BF16),
        ((width, hidden_units), BF16),
        ((hidden_units, width), BF16),
        ((16, width), F32),
    ]
    return pl.pallas_call(
        mlp_kernel,
        grid=(micro,),
        in_specs=[micro_spec((rows, width))] * 3
        + [const_spec(a.shape) for a in (wo, wu, wd, vec, bu)],
        out_specs=[micro_spec(s) for s, _ in per_micro] + [const_spec(s) for s, _ in summed],
        out_shape=[jax.ShapeDtypeStruct((micro,) + s, d) for s, d in per_micro]
        + [jax.ShapeDtypeStruct(s, d) for s, d in summed],
        scratch_shapes=[
            pltpu.VMEM((width, width), F32),
            pltpu.VMEM((width, hidden_units), F32),
            pltpu.VMEM((width, hidden_units), F32),
            pltpu.VMEM((rows, width), F32),
            pltpu.VMEM((rows, width), F32),
        ]
        + [pltpu.VMEM((rows, 512), F32)] * 4,
        compiler_params=vmem(60),
        name="mlp_both",
    )(mixed, emb, cot, wo, wu, wd, vec, bu)


def halves(lane, shift, low, high):
    half = LANES // 2
    return jnp.where(lane < half, pltpu.roll(low, shift, 1), pltpu.roll(high, half - shift, 1))


def mlp_reduce_kernel(dp_size, table_size, *refs):
    refs = list(refs)

    def take(n):
        out = refs[:n]
        del refs[:n]
        return out

    mixed_in, emb_in, cot_in, wo_in, wu_in, wd_in, vec_ref, bu_ref = take(8)
    act_out, ghid_out, gmix_out, dwo_out, small_out = take(5)
    part_outs = [take(2) for _ in range(CHUNKS)]
    mixed_s, emb_s, cot_s, wo_s, wu_s, wd_s = take(6)
    normed_s, normed_t, g_out_t, unit_s, out_s, gn2_s = take(6)
    act_s, gmix_s, ghid_s = normed_s, normed_t, emb_s
    wu_c, wd_c, acc_u, acc_d, acc_o, inv_s = take(6)
    pre_b, gact_b = take(2), take(2)
    grads = [take(2) for _ in range(CHUNKS)]
    hops = len(hops_of(dp_size))
    scratch = [[take(hops + 2) for _ in range(2)] for _ in range(CHUNKS)]
    in_sem, out_sem, send_sem, recv_sem = refs
    micro, rows, width = mixed_s.shape
    hidden_units = wu_s.shape[-1]
    place = Place(dp_size, table_size)
    chunk, last = pl.program_id(0), CHUNKS - 1
    forth, back = place.hops["dp"], place.hops["dp"][:1] + place.hops["dp"][:0:-1]
    flows = []
    base = 0
    for f in range(CHUNKS):
        pair = []
        for grad, order, scr in zip(grads[f], (forth, back), scratch[f]):
            pair.append(
                QuickShard(
                    place, order, lambda s, grad=grad: grad.at[toggled_by(place.me["dp"], s)], scr,
                    (send_sem, recv_sem), base,
                )
            )
            base += quick_sems(hops, table_size)
        flows.append(pair)

    names = []
    for m in range(micro):
        names += [(mixed_in.at[m], mixed_s.at[m])] + [(wo_in, wo_s)] * (m == 0)
        names += [(emb_in.at[m], emb_s.at[m]), (cot_in.at[m], cot_s.at[m])]
        names += [(wu_in, wu_s), (wd_in, wd_s)] * (m == 0)
    copies = [pltpu.make_async_copy(src, dst, in_sem.at[n]) for n, (src, dst) in enumerate(names)]
    gain, shift, dbias = vec_ref[3:4, :], vec_ref[4:5, :], vec_ref[5:6, :]
    half = LANES // 2
    own = hidden_units // dp_size

    def add(ref, first, value):
        ref[...] = value if first else ref[...] + value

    upto = {0: 5, 1: 4, 2: 3, 3: 2}

    def step(f, i):
        for flow in flows[f]:
            if i:
                flow.arrive(i - 1)
            if i < upto[f]:
                flow.start(i)

    def at(c, *steps):
        @pl.when(chunk == c)
        def _():
            for f, i in steps:
                step(f, i)

    @pl.when(chunk == 0)
    def _():
        for copy in copies:
            copy.start()
        wait_all = place.greet(False)
        small_out[...] = jnp.zeros_like(small_out)
        gn2_s[...] = jnp.zeros_like(gn2_s)
        n = 0
        for m in range(micro):
            copies[n].wait()
            copies[n + 1].wait()
            n += 2
            if m == 0:
                copies[n].wait()
                n += 1
            hidden = emb_s[m] + dot_nn(mixed_s[m], wo_s[...])
            unit, inv = norm_parts(hidden)
            unit_s[m] = unit
            inv_s[m] = jnp.broadcast_to(inv, (rows, LANES))
            normed = (unit * gain + shift).astype(BF16)
            normed_s[m] = normed
            normed_t[m] = normed.T
            out_s[m] = hidden + dbias
            copies[n].wait()
            n += 1
            g_out_t[m] = cot_s[m].T
            if m == 0:
                copies[n].wait()
                copies[n + 1].wait()
                n += 2
        wait_all()

    lane = lax.broadcasted_iota(jnp.int32, (width, LANES), 1)
    line = lax.broadcasted_iota(jnp.int32, (8, LANES), 1)
    turn = lax.rem(chunk, 2) * half
    biases = []
    for o in range(0, dp_size, 2):
        tiles = [pl.ds(pl.multiple_of((q * own // LANES + chunk // 2) * LANES, LANES), LANES) for q in (o, o + 1)]
        low, high = (wu_s[:, t].astype(F32) for t in tiles)
        wu_c[:, o * half : o * half + LANES] = halves(lane, turn, low, high).astype(BF16)
        low, high = (jnp.broadcast_to(bu_ref[:, t], (8, LANES)) for t in tiles)
        biases.append(halves(line, turn, low, high)[:1])
    bias = jnp.concatenate(biases, axis=1)
    wd_c[...] = wd_s[:, pl.ds(pl.multiple_of(chunk * half, half), half), :].reshape(width, width)

    def products(m):
        pre_b[m % 2][...] = dot_nn(normed_s[m], wu_c[...])
        gact_b[m % 2][...] = dot_nt(cot_s[m], wd_c[...])

    products(0)
    bias_rows = 0.0
    for m in range(micro):
        if m + 1 < micro:
            products(m + 1)
        pre = pre_b[m % 2][...] + bias
        cdf = 0.5 * (1.0 + lax.erf(pre * INV_SQRT_TWO))
        pdf = jnp.exp(-0.5 * pre * pre) * INV_SQRT_TWO_PI
        act = (pre * cdf).astype(BF16)
        out_s[m] += dot_nn(act, wd_c[...])
        add(acc_d, m == 0, dot_nn(g_out_t[m], act))
        g_pre_f = gact_b[m % 2][...] * (cdf + pre * pdf)
        g_pre = g_pre_f.astype(BF16)
        add(acc_u, m == 0, dot_nn(normed_t[m], g_pre))
        bias_rows = bias_rows + row_sum(g_pre_f)
        gn2_s[m] += dot_nt(g_pre, wu_c[...])
        if m == 0:
            at(2, (0, 2))
            at(3, (0, 3), (1, 2))
        if m == 1:
            at(1, (0, 1))
            at(2, (1, 1))
            at(3, (2, 1))
    row = lax.broadcasted_iota(jnp.int32, (8, width), 0)
    small_out[8:16, :] += jnp.where(row == chunk, jnp.broadcast_to(bias_rows, (8, width)), 0.0)
    up, down = acc_u[...].astype(BF16), acc_d[...].T.astype(BF16)
    for f in range(CHUNKS):

        @pl.when(chunk == f)
        def _():
            grads[f][0][...] = up.reshape(grads[f][0].shape)
            grads[f][1][...] = down.reshape(grads[f][1].shape)
            step(f, 0)

    @pl.when(chunk == last)
    def _():
        step(0, 4)
        step(1, 3)
        step(2, 2)
        outs = []
        for m in range(micro):
            if m == 2:
                step(3, 1)
            act_s[m] = out_s[m].astype(BF16)
            unit, g_norm = unit_s[m], gn2_s[m]
            g_out_f = cot_s[m].astype(F32)
            small_out[3:4, :] += row_sum(g_norm * unit)
            small_out[4:5, :] += row_sum(g_norm)
            small_out[5:6, :] += row_sum(g_out_f)
            g_hidden = g_out_f + norm_back(g_norm, unit, inv_s[m][:, :1], gain)
            ghid_s[m] = g_hidden
            branch = g_hidden.astype(BF16)
            add(acc_o, m == 0, dot_tn(mixed_s[m], branch))
            gmix_s[m] = dot_nt(branch, wo_s[...]).astype(BF16)
            for src, dst in ((act_s, act_out), (ghid_s, ghid_out), (gmix_s, gmix_out)):
                outs.append(pltpu.make_async_copy(src.at[m], dst.at[m], out_sem.at[len(outs)]))
                outs[-1].start()
        dwo_out[...] = acc_o[...].astype(BF16).reshape(dwo_out.shape)
        for f in range(CHUNKS):
            step(f, upto[f])
        for i in range(2):
            part_outs[0][i][...] = flows[0][i].full[...]
            part_outs[1][i][...] = flows[1][i].full[place.me["table"]]
            part_outs[2][i][...] = flows[2][i].dp_total()[...]
            part_outs[3][i][...] = flows[3][i].dp.bufs[1][...]
        for f in range(CHUNKS):
            for flow in flows[f]:
                flow.done = upto[f]
                flow.sent()
        for copy in outs:
            copy.wait()


def mlp_both_reduce(dp_size, table_size, mixed, emb, cot, wo, wu, wd, vec, bu):
    micro, rows, width = mixed.shape
    hidden_units = wu.shape[1]
    own = hidden_units // dp_size
    wd = wd.reshape(dp_size, own, width)
    far = pl.BlockSpec(memory_space=pl.ANY)
    whole = pl.BlockSpec(memory_space=pltpu.VMEM)
    block = (table_size, width // dp_size // table_size, width)
    parts = [block, block[1:], block, (2,) + block]
    hops = len(hops_of(dp_size))

    def per_micro(dtype):
        return pltpu.VMEM((micro, rows, width), dtype)

    def square(dtype):
        return pltpu.VMEM((width, width), dtype)

    scratch = [per_micro(BF16), per_micro(F32), per_micro(BF16)]
    scratch += [square(BF16), pltpu.VMEM(wu.shape, BF16), pltpu.VMEM(wd.shape, BF16)]
    scratch += [per_micro(BF16)] + [pltpu.VMEM((micro, width, rows), BF16)] * 2
    scratch += [per_micro(F32)] * 3
    scratch += [square(BF16)] * 2 + [square(F32)] * 3 + [pltpu.VMEM((micro, rows, LANES), F32)]
    scratch += [pltpu.VMEM((rows, width), F32)] * 4
    scratch += [pltpu.VMEM((dp_size,) + block, BF16)] * (2 * CHUNKS)
    for _ in range(2 * CHUNKS):
        scratch += quick_scratch(hops, table_size, block, BF16)
    count = 2 * CHUNKS * quick_sems(hops, table_size)
    scratch += [pltpu.SemaphoreType.DMA((3 * micro + 3,)), pltpu.SemaphoreType.DMA((3 * micro,))]
    scratch += [pltpu.SemaphoreType.DMA((count,))] * 2
    return pl.pallas_call(
        functools.partial(mlp_reduce_kernel, dp_size, table_size),
        grid=(CHUNKS,),
        in_specs=[far] * 6 + [whole] * 2,
        out_specs=[far] * 3 + [whole] * (2 + 2 * CHUNKS),
        out_shape=[jax.ShapeDtypeStruct((micro, rows, width), d) for d in (BF16, F32, BF16)]
        + [jax.ShapeDtypeStruct((dp_size,) + block, BF16), jax.ShapeDtypeStruct((16, width), F32)]
        + [jax.ShapeDtypeStruct(p, BF16) for p in parts for _ in range(2)],
        scratch_shapes=scratch,
        compiler_params=vmem(60, collective_id=2, has_side_effects=True),
        name="mlp_both_reduce",
    )(mixed, emb, cot, wo, wu, wd, vec, bu)


def attend_back_core(
    hooks, p_ref, linv_ref, k_ref, v_ref, q_ref, gmix_ref, mixed_ref, n_ref, x_ref, ghid_ref,
    wet_ref, vec_ref, wq_ref, wk_ref, wv_ref,
    sums_ref, dkv_ref, dq_ref, wkv_t, wq_t, acc_e, acc_q, acc_kv, d_bufs, e_bufs, g_bufs,
):
    step, pair = pl.program_id(0), pl.program_id(1)
    length, rows, width = n_ref.shape[1], dq_ref.shape[0], dq_ref.shape[1]
    heads = p_ref.shape[1]
    own = lax.axis_index("table")
    here = pl.ds(pl.multiple_of(own * rows, rows), rows)

    @pl.when((step == 0) & (pair == 0))
    def _():
        acc_e[...] = jnp.zeros_like(acc_e)
        acc_q[...] = jnp.zeros_like(acc_q)
        acc_kv[...] = jnp.zeros_like(acc_kv)
        sums_ref[...] = jnp.zeros_like(sums_ref)
        gain = vec_ref[1:2, :]

        def weigh(w):
            w = w.T.astype(F32) * gain
            return (w - jnp.mean(w, axis=-1, keepdims=True)).astype(BF16)

        for h in range(HEADS):
            cols = slice(h * HEAD_DIM, (h + 1) * HEAD_DIM)
            wkv_t[2 * h * HEAD_DIM : (2 * h + 1) * HEAD_DIM, :] = weigh(wk_ref[:, cols])
            wkv_t[(2 * h + 1) * HEAD_DIM : (2 * h + 2) * HEAD_DIM, :] = weigh(wv_ref[:, cols])
            wq_t[cols, :] = weigh(wq_ref[:, cols])

    keys = d_bufs[0].shape[1]
    units = [(h, j) for h in range(heads) for j in range(length // keys)]
    low, low_t, delta, q_t, dq = {}, {}, {}, {}, {}

    def prepare(h):
        cols = slice(h * HEAD_DIM, (h + 1) * HEAD_DIM)
        linv = linv_ref[0, h][:, :1]
        low[h] = (gmix_ref[0, :, cols].astype(F32) * linv).astype(BF16)
        delta[h] = jnp.sum(mixed_ref[0, :, cols] * low[h].astype(F32), axis=-1, keepdims=True)
        low_t[h] = low[h].T
        q_t[h] = q_ref[0, :, cols].T

    def grad_p(u):
        h, j = units[u]
        if j == 0:
            prepare(h)
        at = slice(j * keys, (j + 1) * keys)
        d_bufs[u % 2][...] = dot_nt(low[h], v_ref[0, at, h * HEAD_DIM : (h + 1) * HEAD_DIM])

    grad_p(0)
    for u, (h, j) in enumerate(units):
        if u + 1 < len(units):
            grad_p(u + 1)
        at = slice(j * keys, (j + 1) * keys)
        cols = slice(h * HEAD_DIM, (h + 1) * HEAD_DIM)
        k_rows = pl.ds(pl.multiple_of(2 * (pair * heads + h) * HEAD_DIM, HEAD_DIM), HEAD_DIM)
        v_rows = pl.ds(pl.multiple_of((2 * (pair * heads + h) + 1) * HEAD_DIM, HEAD_DIM), HEAD_DIM)
        p = p_ref[0, h, :, at]
        dkv_ref[v_rows, at] = dot_nn(low_t[h], p).astype(BF16)
        ds = (p.astype(F32) * (d_bufs[u % 2][...] - delta[h])).astype(BF16)
        dkv_ref[k_rows, at] = (dot_nn(q_t[h], ds) * SCALE).astype(BF16)
        dq_part = dot_nn(ds, k_ref[0, at, cols])
        dq[h] = dq_part if j == 0 else dq[h] + dq_part
    for h in range(heads):
        cols = pl.ds(pl.multiple_of((pair * heads + h) * HEAD_DIM, HEAD_DIM), HEAD_DIM)
        dq_ref[:, cols] = (dq[h] * SCALE).astype(BF16)
    for h in range(heads):
        at = pl.ds(pl.multiple_of((pair * heads + h) * 2 * HEAD_DIM, 2 * HEAD_DIM), 2 * HEAD_DIM)
        acc_kv[at, :] += dot_nn(dkv_ref[at, :], n_ref[0])
    both = pl.ds(pl.multiple_of(pair * heads * HEAD_DIM, heads * HEAD_DIM), heads * HEAD_DIM)
    acc_q[both, :] += dot_tn(dq_ref[:, both], n_ref[0, here, :])
    sums_ref[0:1, both] += row_sum(gmix_ref[0].astype(F32))
    sums_ref[1:2, both] += row_sum(dq_ref[:, both].astype(F32))
    hooks.pair_done()

    @pl.when(pair == HEADS // heads - 1)
    def _():
        part = e_bufs[0].shape[0]
        hooks.tick(HEADS // heads, None)

        def rows_back(block, mine):
            def spot(u):
                return pl.ds(pl.multiple_of(block * rows + u * part, part), part), slice(u * part, (u + 1) * part)

            def products(u):
                at, inner = spot(u)
                e_bufs[u % 2][...] = dot_nt(x_ref[0, at, :], wet_ref[...])
                q = dot_tn(dkv_ref[:, at], wkv_t[...])
                if mine:
                    q = q + dot_nn(dq_ref[inner, :], wq_t[...])
                g_bufs[u % 2][...] = q

            products(0)
            for u in range(rows // part):
                if u + 1 < rows // part:
                    products(u + 1)
                at, inner = spot(u)
                unit, inv = norm_parts(e_bufs[u % 2][...])
                q = g_bufs[u % 2][...]
                g_emb = inv * (q - unit * jnp.mean(q * unit, axis=-1, keepdims=True))
                if mine:
                    g_emb = g_emb + ghid_ref[0, inner, :]
                g_emb = g_emb.astype(BF16)
                acc_e[...] += dot_tn(x_ref[0, at, :], g_emb)
                hooks.put(block, mine, inner, dot_nn(g_emb, wet_ref[...]))

        size = length // rows

        def other(g, carry):
            block = lax.rem(own + 1 + g, size)
            rows_back(block, False)
            hooks.block_done(g, block)
            hooks.tick(HEADS // heads + 1, g)
            return carry

        lax.fori_loop(0, size - 1, other, 0)
        rows_back(own, True)
        hooks.own_done()


def norm_one_grads(vec_ref, wq_ref, wk_ref, wv_ref, sums_ref, acc_q, acc_kv):
    gain, shift = vec_ref[1:2, :], vec_ref[2:3, :]
    total = row_sum(wq_ref[...].T.astype(F32) * acc_q[...])
    for h in range(HEADS):
        cols = slice(h * HEAD_DIM, (h + 1) * HEAD_DIM)
        k_rows = slice(2 * h * HEAD_DIM, (2 * h + 1) * HEAD_DIM)
        v_rows = slice((2 * h + 1) * HEAD_DIM, (2 * h + 2) * HEAD_DIM)
        total += row_sum(wk_ref[:, cols].T.astype(F32) * acc_kv[k_rows, :])
        total += row_sum(wv_ref[:, cols].T.astype(F32) * acc_kv[v_rows, :])
    sums = sums_ref[...]
    high = sums.astype(BF16)
    rest = (sums - high.astype(F32)).astype(BF16)
    by_v = dot_nt(high, wv_ref[...]) + dot_nt(rest, wv_ref[...])
    by_q = dot_nt(high, wq_ref[...]) + dot_nt(rest, wq_ref[...])
    d_shift = by_v[0:1, :] + by_q[1:2, :]
    return (total - shift * d_shift) / gain, d_shift


class Alone:
    def __init__(self, ig_ref, rows):
        self.ig_ref, self.rows = ig_ref, rows

    def tick(self, k, g):
        pass

    def pair_done(self):
        pass

    def put(self, block, mine, inner, value):
        at = pl.ds(pl.multiple_of(block * self.rows + inner.start, 128), inner.stop - inner.start)
        self.ig_ref[0, at, :] = value.astype(BF16)

    def block_done(self, g, block):
        pass

    def own_done(self):
        pass


def attend_back_kernel(*refs):
    ins, rest = refs[:15], refs[15:]
    ig_ref, dwe_ref, dwq_ref, dwk_ref, dwv_ref, dvec_ref = rest[:6]
    scratch, bufs = rest[6:14], rest[14:]
    sums_ref, acc_e, acc_q, acc_kv = scratch[0], *scratch[5:8]
    vec_ref, wq_ref, wk_ref, wv_ref = ins[11:15]
    rows = scratch[2].shape[0]
    attend_back_core(Alone(ig_ref, rows), *ins, *scratch, bufs[:2], bufs[2:4], bufs[4:])

    @pl.when((pl.program_id(0) == pl.num_programs(0) - 1) & (pl.program_id(1) == pl.num_programs(1) - 1))
    def _():
        dwe_ref[...] = acc_e[...].T.astype(BF16)
        dwq_ref[...] = acc_q[...].T.astype(BF16)
        d_gain, d_shift = norm_one_grads(vec_ref, wq_ref, wk_ref, wv_ref, sums_ref, acc_q, acc_kv)
        dvec_ref[...] = jnp.zeros_like(dvec_ref)
        dvec_ref[1:2, :] = d_gain
        dvec_ref[2:3, :] = d_shift
        for h in range(HEADS):
            cols = slice(h * HEAD_DIM, (h + 1) * HEAD_DIM)
            dwk_ref[:, cols] = acc_kv[2 * h * HEAD_DIM : (2 * h + 1) * HEAD_DIM, :].T.astype(BF16)
            dwv_ref[:, cols] = acc_kv[(2 * h + 1) * HEAD_DIM : (2 * h + 2) * HEAD_DIM, :].T.astype(BF16)


class Sums:
    def __init__(self, tail, igs):
        self.tail, self.igs = tail, igs
        self.micro, self.head = pl.program_id(0), pl.program_id(1)
        self.count = len(igs)
        self.todo = {}

    def tick(self, k, g=None):
        for m in range(self.count):
            for i in range(1 if g is None else TABLE_STEPS):
                actions = self.todo.get((m, k + i), [])
                if not actions:
                    continue
                now = self.micro == m
                now = now & (self.head == k) if k < PAIRS else now if g is None else now & (g == i)

                @pl.when(now)
                def _():
                    for action in actions:
                        action()

    def start_of_step(self):
        for k in range(PAIRS):
            self.tick(k)

    def at(self, m, k, action):
        self.todo.setdefault((m, k), []).append(action)

    def step(self, flows, i):
        def action():
            for flow in flows:
                if i:
                    flow.arrive(i - 1)
                if i < flow.steps:
                    flow.start(i)

        return action

    def pair_done(self):
        for g in range(PAIRS):

            @pl.when((self.micro == self.count - 1) & (self.head == g))
            def _():
                self.write_pair(g)
                self.step(self.tail[g], 0)()

    def put(self, block, mine, inner, value):
        if mine:
            self.ig_own[inner, :] = value
        else:
            self.ig_bufs[self.micro, block, inner, :] = value.astype(BF16)

    def block_done(self, g, block):
        for m in range(self.count):

            @pl.when(self.micro == m)
            def _():
                self.igs[m].start_one(g + 1)

    def own_done(self):
        self.ig_out[self.micro] = self.ig_own[...]
        self.tick(PAIRS + 1 + TABLE_STEPS)

    def ig_finish(self, m):
        def action():
            total = self.ig_out[m]
            for got in self.igs[m].arrive():
                total = total + got[...].astype(F32)
            self.ig_out[m] = total

        return action


def attend_back_reduce_kernel(dp_size, table_size, *refs):
    refs = list(refs)

    def take(n):
        out = refs[:n]
        del refs[:n]
        return out

    ins = take(15)
    vec_ref, wq_ref, wk_ref, wv_ref = ins[11:15]
    parts = take(7)
    (small_in,) = take(1)
    ig_out, small_out, embed_out = take(3)
    totals = take(11)
    core = take(8)
    sums_ref, acc_e, acc_q, acc_kv = core[0], *core[5:8]
    bufs = take(6)
    place = Place(dp_size, table_size)
    hops = place.hops["dp"]
    part_scratch = [take(n) for n in [len(hops) + 2] + [3] * 2 + [2] * 2 + [1] * 2]
    tail_grads = take(4)
    tail_scratch = [take(len(hops) + 2) for _ in range(4)]
    embed_grad, small_grad = take(2)
    embed_scratch, small_scratch_ = take(3), take(3)
    micro = ig_out.shape[0]
    (ig_bufs,) = take(1)
    ig_got = take(micro)
    (ig_own,) = take(1)
    send_sem, recv_sem = refs
    sems = (send_sem, recv_sem)
    forth, back = hops, hops[:1] + hops[:0:-1]
    base = 0

    def count_up(n):
        nonlocal base
        base += n
        return base - n

    def quick(order, blocks, scratch, back_only=False):
        at = count_up(quick_sems(len(order), table_size, back_only))
        return QuickShard(place, order, blocks, scratch, sems, at, back_only)

    def by_owner(grad):
        return lambda s: grad.at[toggled_by(place.me["dp"], s)]

    out_flow = quick(forth, by_owner(parts[0]), part_scratch[0])
    thirds = [
        quick(order[-1:], lambda s, p=p: p.at[len(s)], scr)
        for order, p, scr in zip((forth, back), parts[1:3], part_scratch[1:3])
    ]
    seconds = [quick([], lambda s, p=p: p, scr) for p, scr in zip(parts[3:5], part_scratch[3:5])]
    firsts = [quick([], lambda s, p=p: p, scr, True) for p, scr in zip(parts[5:], part_scratch[5:])]
    mlp = [out_flow] + thirds + seconds + firsts
    tail = [
        [
            quick(order, by_owner(tail_grads[2 * g + i]), tail_scratch[2 * g + i])
            for i, order in enumerate((forth, back))
        ]
        for g in range(2)
    ]
    others = dp_size + table_size - 2
    embed = Small(place, lambda d: embed_grad.at[d], *embed_scratch, sems, count_up(others))
    small = Small(place, lambda d: small_grad.at[d // 2], *small_scratch_, sems, count_up(others))
    igs = []
    for m in range(micro):
        igs.append(
            Swap(
                place, "table", sems, count_up(table_size - 1),
                lambda t, m=m: ig_bufs.at[m, t],
                lambda t, s, m=m: ig_got[m].at[s - 1],
            )
        )
    hooks = Sums(tail, igs)
    hooks.ig_bufs, hooks.ig_own, hooks.ig_out = ig_bufs, ig_own, ig_out

    def write_pair(g):
        one, two = tail_grads[2 * g], tail_grads[2 * g + 1]
        shape = one.shape[:-1]

        def put(ref, at, value):
            ref[:, :, :, at * HEAD_DIM : at * HEAD_DIM + value.shape[1]] = value.astype(BF16).reshape(
                shape + (value.shape[1],)
            )

        def rows_of(h, side):
            at = (2 * h + side) * HEAD_DIM
            return acc_kv[at : at + HEAD_DIM, :].T

        put(one, 0, acc_q[2 * g * HEAD_DIM : (2 * g + 2) * HEAD_DIM, :].T)
        put(one, 2, rows_of(2 * g, 0))
        put(two, 0, rows_of(2 * g + 1, 0))
        put(two, 1, rows_of(2 * g, 1))
        put(two, 2, rows_of(2 * g + 1, 1))

    hooks.write_pair = write_pair

    last = micro - 1
    hooks.at(0, 0, lambda: place.greet(True)())
    for i, (m, k) in enumerate(((0, 0), (0, 1), (0, 2), (1, 0), (1, 1), (1, 2))):
        hooks.at(m, k, hooks.step([f for f in mlp if i <= f.steps], i))
    hooks.at(1, 2, hooks.ig_finish(0))
    hooks.at(2, 1, hooks.step(tail[0], 1))
    hooks.at(2, 2, hooks.step(tail[0], 2))
    hooks.at(2, 3, hooks.ig_finish(1))
    hooks.at(2, 3, hooks.step(tail[1], 1))
    hooks.at(2, 4, hooks.step(tail[0], 3))
    hooks.at(2, 5, hooks.step(tail[1], 2))

    def finish():
        embed_grad[...] = acc_e[...].T.astype(BF16).reshape(embed_grad.shape)
        hooks.step([embed], 0)()
        d_gain, d_shift = norm_one_grads(vec_ref, wq_ref, wk_ref, wv_ref, sums_ref, acc_q, acc_kv)
        for t in range(dp_size // 2):
            cols = slice(t * LANES, (t + 1) * LANES)
            small_grad[t] = small_in[:, cols]
            small_grad[t, 1:2, :] = d_gain[:, cols]
            small_grad[t, 2:3, :] = d_shift[:, cols]
        ends = [embed, small]
        hooks.step([small], 0)()
        hooks.step(tail[1], 3)()
        hooks.step(tail[0], 4)()
        hooks.step(ends, 1)()
        hooks.step(tail[1], 4)()
        hooks.step(tail[0], 5)()
        hooks.ig_finish(last)()
        hooks.step(ends, 2)()
        hooks.step(tail[1], 5)()
        for flow in mlp + tail[0] + tail[1] + ends + igs:
            flow.sent()
        embed_out[...] = embed.total
        small_out[...] = small.total
        for flow, out in zip(mlp + tail[0] + tail[1], totals):
            out[...] = flow.full[...]

    hooks.at(last, PAIRS + 1 + TABLE_STEPS, finish)
    hooks.start_of_step()
    attend_back_core(hooks, *ins, *core, bufs[:2], bufs[2:4], bufs[4:])


def back_scratch(length, rows, width):
    return [
        pltpu.VMEM((8, width), F32),
        pltpu.VMEM((2 * width, length), BF16),
        pltpu.VMEM((rows, width), BF16),
        pltpu.VMEM((2 * width, width), BF16),
        pltpu.VMEM((width, width), BF16),
        pltpu.VMEM((LANES, width), F32),
        pltpu.VMEM((width, width), F32),
        pltpu.VMEM((2 * width, width), F32),
    ]


def back_buffers(rows, width):
    return [pltpu.VMEM((rows, KEY_BLOCK), F32)] * 2 + [pltpu.VMEM((BACK_BLOCK, width), F32)] * 4


def back_specs(by_head, cols, varied, fixed):
    return (
        [heads_spec(a.shape[2:]) for a in by_head]
        + [pl.BlockSpec((1, a.shape[1], HEADS_STEP * HEAD_DIM), lambda m, h: (m, 0, h)) for a in cols]
        + [micro_spec(a.shape[1:]) for a in varied]
        + [const_spec(a.shape) for a in fixed]
    )


def attend_backward(p, linv, k, v, q, gmix, mixed, n, x, ghid, wet, vec, wq, wk, wv):
    micro, rows, width = q.shape
    length = k.shape[1]
    varied = (n, x, ghid)
    fixed = (wet, vec, wq, wk, wv)
    summed = [(wet.shape, BF16)] + [((width, width), BF16)] * 3 + [((8, width), F32)]
    return pl.pallas_call(
        attend_back_kernel,
        grid=(micro, HEADS // HEADS_STEP),
        in_specs=back_specs((p, linv), (k, v, q, gmix, mixed), varied, fixed),
        out_specs=[micro_spec((length, LANES))] + [const_spec(s) for s, _ in summed],
        out_shape=[jax.ShapeDtypeStruct((micro, length, LANES), BF16)]
        + [jax.ShapeDtypeStruct(s, d) for s, d in summed],
        scratch_shapes=back_scratch(length, rows, width) + back_buffers(rows, width),
        compiler_params=vmem(58),
        name="attend_backward",
    )(p, linv, k, v, q, gmix, mixed, *varied, *fixed)


def attend_backward_reduce(
    dp_size, table_size, parts, small, p, linv, k, v, q, gmix, mixed, n, x, ghid, wet, vec, wq, wk, wv
):
    micro, rows, width = q.shape
    length = k.shape[1]
    varied = (n, x, ghid)
    fixed = (wet, vec, wq, wk, wv)
    whole = pl.BlockSpec(memory_space=pltpu.VMEM)
    shard = width // dp_size
    block = (table_size, shard // table_size, width)
    tail = (dp_size, table_size, shard // table_size, 3 * HEAD_DIM)
    blocks = [block] * 7 + [tail[1:]] * 4
    hops = len(hops_of(dp_size))
    kinds = [(hops, False)] + [(1, False)] * 2 + [(0, False)] * 2 + [(0, True)] * 2
    scratch = back_scratch(length, rows, width) + back_buffers(rows, width)
    for n, back_only in kinds:
        scratch += quick_scratch(n, table_size, block, BF16, back_only)
    scratch += [pltpu.VMEM(tail, BF16)] * 4
    for _ in range(4):
        scratch += quick_scratch(hops, table_size, tail[1:], BF16)
    tile = (small.shape[0], LANES)
    scratch += [pltpu.VMEM((dp_size, shard, LANES), BF16), pltpu.VMEM((dp_size // 2,) + tile, F32)]
    scratch += small_scratch(dp_size, table_size, (shard, LANES), BF16)
    scratch += small_scratch(dp_size, table_size, tile, F32)
    scratch += [pltpu.VMEM((micro, table_size, rows, LANES), BF16)]
    scratch += [pltpu.VMEM((table_size - 1, rows, LANES), BF16)] * micro
    scratch += [pltpu.VMEM((rows, LANES), F32)]
    count = sum(quick_sems(n, table_size, back_only) for n, back_only in kinds + [(hops, False)] * 4)
    count += 2 * (dp_size + table_size - 2) + micro * (table_size - 1)
    scratch += [pltpu.SemaphoreType.DMA((count,))] * 2
    outs = [((micro, rows, LANES), F32), (tile, F32), ((shard, LANES), F32)]
    outs += [(b, BF16) for b in blocks]
    return pl.pallas_call(
        functools.partial(attend_back_reduce_kernel, dp_size, table_size),
        grid=(micro, PAIRS),
        in_specs=back_specs((p, linv), (k, v, q, gmix, mixed), varied, fixed)
        + [whole] * 7
        + [const_spec(small.shape)],
        out_specs=[const_spec(shape) for shape, _ in outs],
        out_shape=[jax.ShapeDtypeStruct(shape, dtype) for shape, dtype in outs],
        scratch_shapes=scratch,
        compiler_params=vmem(60, collective_id=1, has_side_effects=True),
        name="attend_backward_reduce",
    )(p, linv, k, v, q, gmix, mixed, *varied, *fixed, *parts, small)


def finish_kernel(feat, shard, mask_ref, ig_in, small_in, embed_in, *refs):
    chunk_ins, out_in, pair_ins, outs = refs[: 2 * CHUNKS], refs[2 * CHUNKS], refs[2 * CHUNKS + 1 : 2 * CHUNKS + 5], refs[2 * CHUNKS + 5 :]
    ig_out, dwe, dwq, dwk, dwv, dwo, dwu, dwd = outs[:8]
    vecs, bu = outs[8:14], outs[14]
    half = LANES // 2
    for m in range(ig_in.shape[0]):
        ig_out[m] = ig_in[m].T[:feat, :] * mask_ref[m].astype(F32)
    dwe[...] = embed_in[:, :feat]
    dwo[...] = out_in[...].astype(F32)
    lane = lax.broadcasted_iota(jnp.int32, (shard, LANES), 1)
    ups, downs = chunk_ins[::2], chunk_ins[1::2]
    for f in range(CHUNKS):
        dwd[f * half : (f + 1) * half, :] = downs[f][...].astype(F32)
    per_owner = bu.shape[1]
    for o in range(dwu.shape[1] // per_owner):
        for f in range(0, CHUNKS, 2):
            tile = slice(o // 2 * LANES, (o // 2 + 1) * LANES)
            low, high = ups[f][:, tile].astype(F32), ups[f + 1][:, tile].astype(F32)
            at = o * per_owner + f * half
            dwu[:, at : at + LANES] = halves(lane, o % 2 * half, low, high)
    for g in range(HEADS // 2):
        one, two = pair_ins[2 * g], pair_ins[2 * g + 1]
        at = 2 * g * HEAD_DIM
        dwq[:, at : at + 2 * HEAD_DIM] = one[:, : 2 * HEAD_DIM].astype(F32)
        dwk[:, at : at + HEAD_DIM] = one[:, 2 * HEAD_DIM :].astype(F32)
        dwk[:, at + HEAD_DIM : at + 2 * HEAD_DIM] = two[:, :HEAD_DIM].astype(F32)
        dwv[:, at : at + 2 * HEAD_DIM] = two[:, HEAD_DIM:].astype(F32)
    small = small_in[...]
    turned = pltpu.roll(small, lax.rem(lax.axis_index("dp"), 2) * half, 1)
    vecs[0][...] = embed_in[...].T[feat : feat + 1, :]
    for i, out in enumerate(vecs[1:]):
        out[...] = turned[i + 1 : i + 2, :shard]
    rows = turned[8:16, :]
    line = lax.broadcasted_iota(jnp.int32, (8, LANES), 1)
    for f in range(0, CHUNKS, 2):
        low = jnp.broadcast_to(rows[f : f + 1, :], (8, LANES))
        high = jnp.broadcast_to(rows[f + 1 : f + 2, :], (8, LANES))
        bu[:, f * half : f * half + LANES] = halves(line, 0, low, high)[:1]


def finish(feat, ff_shard, mask, ig, small, embed, chunks, rest):
    micro, rows, _ = ig.shape
    shard = embed.shape[0]
    width = rest[0].shape[1]
    out_shape = (
        [jax.ShapeDtypeStruct((micro, feat, rows), F32), jax.ShapeDtypeStruct((shard, feat), F32)]
        + [jax.ShapeDtypeStruct((shard, width), F32)] * 4
        + [jax.ShapeDtypeStruct((shard, CHUNKS * width), F32), jax.ShapeDtypeStruct((ff_shard, width), F32)]
        + [jax.ShapeDtypeStruct((1, shard), F32)] * 6
        + [jax.ShapeDtypeStruct((1, ff_shard), F32)]
    )
    return pl.pallas_call(
        functools.partial(finish_kernel, feat, shard),
        out_shape=out_shape,
        compiler_params=vmem(60),
        name="finish",
    )(mask, ig, small, embed, *chunks, *rest)


def body(
    dp_size, table_size, features, feature_mask, support_count, embed_weight, embed_bias, gain_first, shift_first,
    query_weight, key_weight, value_weight, out_weight, gain_second, shift_second, up_weight, up_bias,
    down_weight, down_bias, cotangent,
):
    micro, _, rows, feat = features.shape
    shard, width = query_weight.shape
    hidden_units = up_weight.shape[1]
    ff_shard = up_bias.shape[0]
    features, cotangent, support = features[:, 0], cotangent[:, 0], support_count[:, 0]
    vectors = (embed_bias, gain_first, shift_first, gain_second, shift_second, down_bias)
    if 2 * shard == LANES and micro == 3 and table_size == 4 and ff_shard == CHUNKS * shard:
        got = attend_forward_gather(
            dp_size, table_size, support, features.transpose(0, 2, 1), feature_mask, embed_weight.T,
            [a[None] for a in vectors], up_bias.reshape(-1, LANES),
            query_weight, key_weight, value_weight, out_weight, up_weight, down_weight,
        )
        q, k, v, n, emb, mixed, mixed_low, p, linv, x = got[:10]
        wet, wq, wk, wv = (g.reshape(-1, g.shape[-1]) for g in got[10:14])
        vec, bu = got[14:16]
        wo, wu, wd = (g.reshape(-1, g.shape[-1]) for g in got[16:])
        activations, ghid, gmix, dwo, small, *parts = mlp_both_reduce(
            dp_size, table_size, mixed_low, emb, cotangent, wo, wu, wd, vec, bu
        )
        ig, small, embed, *totals = attend_backward_reduce(
            dp_size, table_size, [dwo] + parts[6:] + parts[4:6] + parts[2:4], small,
            p, linv, k, v, q, gmix, mixed, n, x, ghid, wet, vec, wq, wk, wv,
        )
        totals = [t.reshape(-1, t.shape[-1]) for t in totals]
        chunks = [t.reshape(-1, t.shape[-1]) for t in parts[:2]] + totals[5:7] + totals[3:5] + totals[1:3]
        mask = feature_mask.reshape(micro, feat, 1)
        out = finish(feat, ff_shard, mask, ig, small, embed, chunks, totals[:1] + totals[7:])
        ig, dwe, dwq, dwk, dwv, dwo, dwu, dwd = out[:8]
        ig, dwe = ig.transpose(0, 2, 1), dwe.T
        smalls = [o.reshape(-1) for o in out[8:14]]
        dbu = out[14].reshape(-1)
    else:
        smalls = jnp.stack(vectors)
        mask = jnp.pad(feature_mask[:, 0], ((0, 0), (0, LANES - feat)))[:, None, :]
        x = jnp.pad(features, ((0, 0), (0, 0), (0, LANES - feat))) * mask.astype(BF16)
        x = x.at[:, :, feat].set(1.0)
        wet = jnp.concatenate([embed_weight, embed_bias[None]])
        wet = jnp.pad(wet, ((0, LANES - feat - 1), (0, 0))).T
        shards = [wet, query_weight, key_weight, value_weight, out_weight, up_weight, down_weight]
        wet, wq, wk, wv, wo, wu, wd = (lax.all_gather(s, "dp", axis=0, tiled=True) for s in shards)
        vec = jnp.pad(lax.all_gather(smalls, "dp", axis=1, tiled=True).astype(F32), ((0, 2), (0, 0)))
        bu = lax.all_gather(up_bias, "dp", axis=0, tiled=True).astype(F32)[None]
        x = lax.all_gather(x, "table", axis=1, tiled=True)
        q, k, v, n, emb, mixed, mixed_low, p, linv = attend_forward(support, x, wet, vec, wq, wk, wv, rows)
        activations, ghid, gmix, dwo, dwu, dwd, small = mlp_both(mixed_low, emb, cotangent, wo, wu, wd, vec, bu)
        ig, dwe, dwq, dwk, dwv, dvec = attend_backward(
            p, linv, k, v, q, gmix, mixed, n, x, ghid, wet, vec, wq, wk, wv
        )
        big = [dwe, dwq, dwk, dwv, dwo, dwu, dwd]
        own = [lax.psum_scatter(g.astype(F32), "dp", scatter_dimension=0, tiled=True) for g in big]
        dwe, dwq, dwk, dwv, dwo, dwu, dwd = (lax.psum(g, "table") for g in own)
        dbe, dwe = dwe[:, feat], dwe[:, :feat].T
        dvec = jnp.concatenate([dvec[:3], small[3:6]])
        smalls = lax.psum(lax.psum_scatter(dvec, "dp", scatter_dimension=1, tiled=True), "table")
        smalls = [dbe] + [smalls[i] for i in range(1, 6)]
        dbu = small[8:].reshape(-1)[:hidden_units]
        dbu = lax.psum(lax.psum_scatter(dbu, "dp", scatter_dimension=0, tiled=True), "table")
        ig = lax.psum_scatter(ig.astype(F32) * mask, "table", scatter_dimension=1, tiled=True)[:, :, :feat]
    return (
        activations[:, None], ig[:, None], dwe, smalls[0], smalls[1], smalls[2],
        dwq, dwk, dwv, dwo, smalls[3], smalls[4], dwu, dbu, dwd, smalls[5],
    )


def solution(mesh):
    rows, cols, vecs = P("dp", None), P(None, "dp"), P("dp")
    table = P(None, "dp", "table", None)
    return jax.shard_map(
        functools.partial(body, mesh.shape["dp"], mesh.shape["table"]),
        mesh=mesh,
        in_specs=(
            table, P(None, "dp", None), cols, cols, vecs, vecs, vecs, rows, rows, rows, rows,
            vecs, vecs, rows, vecs, rows, vecs, table,
        ),
        out_specs=(
            table, table, cols, vecs, vecs, vecs, rows, rows, rows, rows, vecs, vecs, rows, vecs, rows, vecs,
        ),
        check_vma=False,
    )
```

```python
import functools

import jax
import jax.numpy as jnp
from jax import lax
from jax.experimental import pallas as pl
from jax.experimental.pallas import tpu as pltpu
from jax.sharding import PartitionSpec as P

HEADS = 4
HEAD_DIM = 128
LANES = 128
EPSILON = 1e-5
SCALE = HEAD_DIM**-0.5
LOG2E = 1.4426950408889634
ROW_BLOCK = 256
KEY_BLOCK = 512
BACK_BLOCK = 256
GROUPS = 4
NORM_BLOCK = 256
HEADS_STEP = 2
PAIRS = HEADS // HEADS_STEP
CHUNKS = 4
TABLE_STEPS = 3
INV_SQRT_TWO = 0.7071067811865476
INV_SQRT_TWO_PI = 0.3989422804014327
BF16 = jnp.bfloat16
F32 = jnp.float32
MESH = pl.DeviceIdType.MESH


def dot_nn(a, b):
    return lax.dot_general(a, b, (((1,), (0,)), ((), ())), preferred_element_type=F32)


def dot_nt(a, b):
    return lax.dot_general(a, b, (((1,), (1,)), ((), ())), preferred_element_type=F32)


def dot_tn(a, b):
    return lax.dot_general(a, b, (((0,), (0,)), ((), ())), preferred_element_type=F32)


def norm_parts(v):
    mean = jnp.mean(v, axis=-1, keepdims=True)
    centred = v - mean
    inv = lax.rsqrt(jnp.mean(centred * centred, axis=-1, keepdims=True) + EPSILON)
    return centred * inv, inv


def norm_back(grad, unit, inv, gain):
    q = grad * gain
    return inv * (
        q
        - jnp.mean(q, axis=-1, keepdims=True)
        - unit * jnp.mean(q * unit, axis=-1, keepdims=True)
    )


def row_sum(v):
    return jnp.sum(v, axis=0, keepdims=True)


def const_spec(shape):
    return pl.BlockSpec(shape, lambda *g: (0,) * len(shape))


def micro_spec(shape):
    return pl.BlockSpec((1,) + shape, lambda m, *g: (m,) + (0,) * len(shape))


def head_spec(shape):
    return pl.BlockSpec((1, 1) + shape, lambda m, h: (m, h) + (0,) * len(shape))


def heads_spec(shape):
    return pl.BlockSpec((1, HEADS_STEP) + shape, lambda m, h: (m, h) + (0,) * len(shape))


def head_cols_spec(rows):
    return pl.BlockSpec((1, rows, HEAD_DIM), lambda m, h: (m, 0, h))


def vmem(mib, **extra):
    return pltpu.CompilerParams(vmem_limit_bytes=mib * 2**20, **extra)


def subsets(hops):
    out = [()]
    for hop in reversed(hops):
        out = out + [(hop,) + s for s in out]
    return out


def hops_of(size):
    return [1 << i for i in range(size.bit_length() - 1)]


class Place:
    def __init__(self, dp_size, table_size):
        self.size = {"dp": dp_size, "table": table_size}
        self.hops = {axis: hops_of(n) for axis, n in self.size.items()}
        self.me = {"dp": lax.axis_index("dp"), "table": lax.axis_index("table")}
        self.across, self.next = {}, {}
        for axis, n in self.size.items():
            me = self.me[axis]
            turn = {hop: hop * (1 - 2 * lax.rem(lax.div(me, hop), 2)) for hop in self.hops[axis]}
            for s in subsets(self.hops[axis]):
                self.across[axis, frozenset(s)] = sum([turn[hop] for hop in s], me)
            for shift in range(n):
                self.next[axis, shift] = lax.rem(me + shift, n)

    def toggled(self, axis, hops):
        return self.across[axis, frozenset(hops)]

    def partner(self, axis, hop):
        there = dict(self.me)
        there[axis] = self.toggled(axis, (hop,))
        return (there["dp"], there["table"])

    def at(self, axis, shift):
        n = self.size[axis]
        if isinstance(shift, int):
            return self.next[axis, shift % n]
        return lax.rem(self.me[axis] + shift, n)

    def ahead(self, axis, shift):
        there = dict(self.me)
        there[axis] = self.at(axis, shift)
        return (there["dp"], there["table"])

    def greet(self, all_dp):
        barrier = pltpu.get_barrier_semaphore()
        peers = [self.ahead("table", s) for s in range(1, self.size["table"])]
        if all_dp:
            peers += [self.ahead("dp", s) for s in range(1, self.size["dp"])]
        else:
            peers += [self.partner("dp", hop) for hop in self.hops["dp"]]
        for peer in peers:
            pl.semaphore_signal(barrier, inc=1, device_id=peer, device_id_type=MESH)
        return lambda: pl.semaphore_wait(barrier, len(peers))


class Swap:
    def __init__(self, place, axis, sems, base, send, put):
        self.place, self.axis, self.sems, self.base = place, axis, sems, base
        self.send, self.put = send, put
        self.shifts = range(1, place.size[axis])

    def copy(self, shift, src, dst):
        index = self.base + shift - 1
        return pltpu.make_async_remote_copy(
            src_ref=src, dst_ref=dst, send_sem=self.sems[0].at[index], recv_sem=self.sems[1].at[index],
            device_id=self.place.ahead(self.axis, shift), device_id_type=MESH,
        )

    def start_one(self, shift):
        to = self.place.at(self.axis, shift)
        self.copy(shift, self.send(to), self.put(self.place.me[self.axis], shift)).start()

    def start(self):
        for shift in self.shifts:
            self.start_one(shift)

    def arrive_one(self, shift):
        here = self.put(self.place.at(self.axis, -shift), shift)
        self.copy(shift, here, here).wait_recv()
        return here

    def arrive(self):
        return [self.arrive_one(shift) for shift in self.shifts]

    def sent(self):
        for shift in self.shifts:
            out = self.send(self.place.at(self.axis, shift))
            self.copy(shift, out, out).wait_send()


def remote(place, axis, hop, src, dst, sems, index):
    return pltpu.make_async_remote_copy(
        src_ref=src, dst_ref=dst, send_sem=sems[0].at[index], recv_sem=sems[1].at[index],
        device_id=place.partner(axis, hop), device_id_type=MESH,
    )


class Gather:
    def __init__(self, place, axis, hops, full, sems, base, own=None):
        self.place, self.axis, self.hops = place, axis, hops
        self.full, self.sems, self.base, self.own = full, sems, base, own
        self.steps = len(hops)

    def whole(self, step):
        part = self.full.at[pl.ds(0, 1 << step)]
        return remote(self.place, self.axis, self.hops[step], part, part, self.sems, self.base + step)

    def start(self, step):
        for s in subsets(self.hops[:step]):
            block = self.full.at[self.place.toggled(self.axis, s)]
            src = block if s or self.own is None else self.own
            remote(
                self.place, self.axis, self.hops[step], src, block, self.sems, self.base + step
            ).start()

    def arrive(self, step):
        self.whole(step).wait_recv()

    def sent(self):
        for step in range(self.steps):
            self.whole(step).wait_send()


def add_into(into, other):
    into[...] = (into[...].astype(F32) + other[...].astype(F32)).astype(into.dtype)


class Reduce:
    def __init__(self, place, axis, hops, blocks, bufs, sems, base, array=None):
        self.place, self.axis, self.hops = place, axis, hops
        self.blocks, self.array = blocks, array
        self.bufs, self.sems, self.base = bufs, sems, base
        self.steps = len(hops)

    def before(self, step):
        return self.bufs[step - 1] if step else self.array

    def copy(self, step, src, dst):
        return remote(self.place, self.axis, self.hops[step], src, dst, self.sems, self.base + step)

    def start(self, step):
        rest = subsets(self.hops[step + 1 :])
        held = self.before(step)
        if held is not None:
            self.copy(step, held.at[pl.ds(len(rest), len(rest))], self.bufs[step]).start()
            return
        for i, s in enumerate(rest):
            self.copy(step, self.blocks(s + (self.hops[step],)), self.bufs[step].at[i]).start()

    def arrive(self, step):
        self.copy(step, self.bufs[step], self.bufs[step]).wait_recv()
        rest = subsets(self.hops[step + 1 :])
        held = self.before(step)
        if held is not None:
            add_into(self.bufs[step], held.at[pl.ds(0, len(rest))])
            return
        for i, s in enumerate(rest):
            add_into(self.bufs[step].at[i], self.blocks(s))

    def total(self):
        return self.bufs[-1].at[0]

    def sent_one(self, step):
        self.copy(step, self.bufs[step], self.bufs[step]).wait_send()


class QuickShard:
    def __init__(self, place, dp_hops, blocks, scratch, sems, base, back_only=False, array=None):
        n = len(dp_hops)
        self.place, self.full, self.array = place, scratch[-1], array
        got = None if back_only else scratch[n]
        self.dp = Reduce(place, "dp", dp_hops, blocks, scratch[:n], sems, base, array)
        base += n
        self.out = self.back = None
        if not back_only:
            self.out = Swap(
                place, "table", sems, base, lambda t: self.dp_total().at[t], lambda t, s: got.at[s - 1]
            )
            base += place.size["table"] - 1
        self.back = Swap(
            place, "table", sems, base, lambda t: self.full.at[place.me["table"]], lambda t, s: self.full.at[t]
        )
        self.stages = [(self.dp, i) for i in range(n)] + ([] if back_only else [(self.out, 0)]) + [(self.back, 0)]
        self.steps = len(self.stages)
        self.done = 0

    def dp_total(self):
        return self.dp.total() if self.dp.steps else self.array

    def start(self, step):
        flow, i = self.stages[step]
        self.done = max(self.done, step + 1)
        if flow is self.dp:
            flow.start(i)
            return
        if flow is self.back and self.out is None:
            self.full[self.place.me["table"]] = self.array[...]
        flow.start()

    def arrive(self, step):
        flow, i = self.stages[step]
        if flow is self.dp:
            flow.arrive(i)
        elif flow is self.out:
            me = self.place.me["table"]
            total = self.dp_total()[me].astype(F32)
            for got in flow.arrive():
                total = total + got[...].astype(F32)
            self.full[me] = total.astype(self.full.dtype)
        else:
            flow.arrive()

    def sent(self):
        for flow, i in self.stages[: self.done]:
            if flow is self.dp:
                flow.sent_one(i)
            else:
                flow.sent()


def quick_scratch(dp_hops, table_size, block, dtype, back_only=False):
    out = [pltpu.VMEM((1 << (dp_hops - 1 - i),) + block, dtype) for i in range(dp_hops)]
    if not back_only:
        out.append(pltpu.VMEM((table_size - 1,) + block[1:], dtype))
    return out + [pltpu.VMEM(block, dtype)]


def quick_sems(dp_hops, table_size, back_only=False):
    return dp_hops + (1 if back_only else 2) * (table_size - 1)


class Small:
    def __init__(self, place, block, got_dp, part, got_table, sems, base, out):
        self.place, self.block, self.part, self.out = place, block, part, out
        self.first = Swap(place, "dp", sems, base, block, lambda t, s: got_dp.at[s - 1])
        base += place.size["dp"] - 1
        self.second = Swap(
            place, "table", sems, base, lambda t: part, lambda t, s: got_table.at[s - 1]
        )
        self.steps = 2

    def start(self, step):
        (self.first, self.second)[step].start()

    def arrive(self, step):
        if step == 0:
            total = self.block(self.place.me["dp"])[...].astype(F32)
            for got in self.first.arrive():
                total = total + got[...].astype(F32)
            self.part[...] = total.astype(self.part.dtype)
        else:
            total = self.part[...].astype(F32)
            for got in self.second.arrive():
                total = total + got[...].astype(F32)
            self.out[...] = total

    def sent(self):
        self.first.sent()
        self.second.sent()


def small_scratch(dp_size, table_size, block, dtype):
    return [
        pltpu.VMEM((dp_size - 1,) + block, dtype),
        pltpu.VMEM(block, dtype),
        pltpu.VMEM((table_size - 1,) + block, dtype),
    ]


def attend_core(
    support, project_all, wq, q_ref, k_ref, v_ref, n_ref, emb_ref, mixed_ref, mixed_low_ref, p_ref, linv_ref, s_bufs, get_x, wet,
):
    length, rows = n_ref.shape[1], q_ref.shape[1]
    own = lax.axis_index("table")

    @pl.when(pl.program_id(1) == 0)
    def _():
        project_all()
        here = pl.ds(pl.multiple_of(own * rows, rows), rows)
        emb_ref[0] = dot_nt(get_x(own, slice(0, rows)), wet())
        q_ref[0] = dot_nn(n_ref[0, here, :], wq()).astype(BF16)

    block = s_bufs[0].shape[0]
    sure = length - rows
    columns = sure + lax.broadcasted_iota(jnp.int32, (1, rows), 1)
    allowed = columns < support
    heads = p_ref.shape[1]
    units = [(h, i) for h in range(heads) for i in range(rows // block)]
    first_head = pl.program_id(1) * heads

    def cols_of(h):
        return pl.ds(pl.multiple_of((first_head + h) * HEAD_DIM, HEAD_DIM), HEAD_DIM)

    def score(j):
        h, i = units[j]
        q = q_ref[0, i * block : (i + 1) * block, cols_of(h)]
        s_bufs[j % 2][...] = dot_nt(q, k_ref[0, :, cols_of(h)])

    score(0)
    for j, (h, i) in enumerate(units):
        if j + 1 < len(units):
            score(j + 1)
        at = slice(i * block, (i + 1) * block)
        first = s_bufs[j % 2][:, :sure]
        last = jnp.where(allowed, s_bufs[j % 2][:, sure:], -1e30)
        top = jnp.maximum(
            jnp.max(first, axis=-1, keepdims=True), jnp.max(last, axis=-1, keepdims=True)
        )
        pf = jnp.exp2((first - top) * (SCALE * LOG2E))
        pt = jnp.exp2((last - top) * (SCALE * LOG2E))
        total = jnp.sum(pf, axis=-1, keepdims=True) + jnp.sum(pt, axis=-1, keepdims=True)
        pf, pt = pf.astype(BF16), pt.astype(BF16)
        p_ref[0, h, at, :sure] = pf
        p_ref[0, h, at, sure:] = pt
        linv = 1.0 / total
        linv_ref[0, h, at, :] = jnp.broadcast_to(linv, (block, LANES))
        out = dot_nn(pf, v_ref[0, :sure, cols_of(h)]) + dot_nn(pt, v_ref[0, sure:, cols_of(h)])
        out = out * linv
        mixed_ref[0, at, cols_of(h)] = out
        mixed_low_ref[0, at, cols_of(h)] = out.astype(BF16)


def project(blocks, rows, get_x, wet, vec_ref, wk, wv, k_ref, v_ref, n_ref, e_bufs):
    gain, shift = vec_ref[1:2, :], vec_ref[2:3, :]
    chunk = e_bufs[0].shape[0]
    units = [(b, i) for b in blocks for i in range(rows // chunk)]

    def embed(j):
        b, i = units[j]
        e_bufs[j % 2][...] = dot_nt(get_x(b, slice(i * chunk, (i + 1) * chunk)), wet())

    embed(0)
    for j, (b, i) in enumerate(units):
        if j + 1 < len(units):
            embed(j + 1)
        at = pl.ds(pl.multiple_of(b * rows + i * chunk, chunk), chunk)
        unit, _ = norm_parts(e_bufs[j % 2][...])
        normed = (unit * gain + shift).astype(BF16)
        n_ref[0, at, :] = normed
        k_ref[0, at, :] = dot_nn(normed, wk()).astype(BF16)
        v_ref[0, at, :] = dot_nn(normed, wv()).astype(BF16)


def attend_kernel(support_ref, x_ref, wet_ref, vec_ref, wq_ref, wk_ref, wv_ref, *rest):
    outs, bufs = rest[:9], rest[9:]
    q_ref, k_ref, v_ref, n_ref = outs[:4]
    rows = q_ref.shape[1]

    def get_x(block, part):
        at = pl.ds(pl.multiple_of(block * rows + part.start, NORM_BLOCK), part.stop - part.start)
        return x_ref[0, at, :]

    def project_all():
        project(
            range(x_ref.shape[1] // rows), rows, get_x, lambda: wet_ref[...], vec_ref,
            lambda: wk_ref[...], lambda: wv_ref[...], k_ref, v_ref, n_ref, bufs[:2],
        )

    attend_core(
        support_ref[pl.program_id(0)], project_all, lambda: wq_ref[...], *outs, bufs[2:], get_x, lambda: wet_ref[...]
    )


def attend_scratch(length, width):
    return [pltpu.VMEM((NORM_BLOCK, width), F32)] * 2 + [pltpu.VMEM((ROW_BLOCK, length), F32)] * 2


def attend_gather_kernel(
    dp_size, table_size, support_ref, feat_ref, mask_ref, ew_ref,
    v0_ref, v1_ref, v2_ref, v3_ref, v4_ref, v5_ref, ub_ref, wq_in, wk_in, wv_in, wo_in, wu_in, wd_in,
    q_ref, k_ref, v_ref, n_ref, emb_ref, mixed_ref, mixed_low_ref, p_ref, linv_ref,
    x_out, wet_out, wq_out, wk_out, wv_out, vec_ref, bu_ref, wo_out, wu_out, wd_out, mask_out,
    x_buf, wet_buf, packed_buf, wq_buf, wk_buf, wv_buf, e_one, e_two, s_one, s_two, own_sem, send_sem, recv_sem,
):
    micro_id, head = pl.program_id(0), pl.program_id(1)
    micro, feat, rows = feat_ref.shape
    shard = wq_in.shape[0]
    width = wq_in.shape[1]
    place = Place(dp_size, table_size)
    dp, table = place.me["dp"], place.me["table"]
    sems = (send_sem, recv_sem)
    hops = place.hops["dp"]
    forth, back = hops[1:] + hops[:1], hops[:0:-1] + hops[:1]
    last = len(hops) - 1
    base = 0

    def gather(order, full, own=None):
        nonlocal base
        flow = Gather(place, "dp", order, full, sems, base, own)
        base += flow.steps
        return flow

    early = [
        gather(forth, wk_buf),
        gather(back, wv_buf),
        gather(forth, wet_buf),
        gather(back, packed_buf),
    ]
    query = gather(forth, wq_buf)
    late = [gather(forth, wo_out, wo_in), gather(forth, wu_out, wu_in), gather(back, wd_out, wd_in)]
    feats = []
    for m in range(micro):
        own_x = x_buf.at[m, table]
        feats.append(
            Swap(
                place, "table", sems, base,
                lambda t, own_x=own_x: own_x,
                lambda t, s, m=m: x_buf.at[m, t],
            )
        )
        base += table_size - 1
    own_copies = [
        pltpu.make_async_copy(src, dst.at[dp], own_sem.at[i])
        for i, (src, dst) in enumerate(((wo_in, wo_out), (wu_in, wu_out), (wd_in, wd_out)))
    ]
    out_copies = [
        pltpu.make_async_copy(src, dst, own_sem.at[3 + i])
        for i, (src, dst) in enumerate(
            ((wet_buf, wet_out), (wq_buf, wq_out), (wk_buf, wk_out), (wv_buf, wv_out))
        )
    ]

    def at_step(m, h):
        return pl.when((micro_id == m) & (head == h))

    @at_step(0, 0)
    def _():
        wait_all = place.greet(False)
        packed_buf[dp] = jnp.zeros((8, LANES), F32)
        for i, ref in enumerate((v0_ref, v1_ref, v2_ref, v3_ref, v4_ref, v5_ref)):
            packed_buf[dp, i : i + 1, :shard] = ref[...].astype(F32)
        place_of = lax.broadcasted_iota(jnp.int32, (LANES, LANES), 0) == feat
        bias = jnp.where(place_of, jnp.broadcast_to(packed_buf[dp, 0:1, :], (LANES, LANES)), 0.0)
        wet_buf[dp] = bias.T[:shard, :].astype(BF16)
        wet_buf[dp, :, :feat] = ew_ref[...]
        packed_buf[dp, 6:8, :] = ub_ref[...].astype(F32)
        wk_buf[dp] = wk_in[...]
        wv_buf[dp] = wv_in[...]
        wq_buf[dp] = wq_in[...]

        def fill(m):
            mask_out[m] = jnp.zeros((8, LANES), F32)
            mask_out[m, :, :feat] = jnp.broadcast_to(mask_ref[m].astype(F32), (8, feat))
            tall = jnp.concatenate(
                [feat_ref[m].astype(F32), jnp.zeros((LANES - feat, rows), F32)], axis=0
            ).T
            lane = lax.broadcasted_iota(jnp.int32, (rows, LANES), 1)
            x_buf[m, table] = jnp.where(lane == feat, 1.0, 0.0).astype(BF16)
            x_buf[m, table, :, :feat] = (tall[:, :feat] * mask_ref[m].astype(F32)).astype(BF16)

        fill(0)
        wait_all()
        for flow in early:
            flow.start(0)
        feats[0].start()
        for copy in own_copies:
            copy.start()
        for m in range(1, micro):
            fill(m)
        for step in range(last):
            for flow in early:
                flow.arrive(step)
                flow.start(step + 1)
            if step == 0:
                query.start(0)
            else:
                query.arrive(step - 1)
                query.start(step)
        for flow in early:
            flow.arrive(last)
        for flow in late:
            flow.start(0)
        lane = lax.broadcasted_iota(jnp.int32, (8, LANES), 1)
        for d in range(0, dp_size, 2):
            pair = jnp.where(lane < shard, packed_buf[d], pltpu.roll(packed_buf[d + 1], shard, 1))
            vec_ref[:, d * shard : (d + 2) * shard] = pair
        for d in range(dp_size):
            bu_ref[:, 2 * d * LANES : (2 * d + 1) * LANES] = packed_buf[d, 6:7, :]
            bu_ref[:, (2 * d + 1) * LANES : (2 * d + 2) * LANES] = packed_buf[d, 7:8, :]

    @at_step(0, 1)
    def _():
        for flow in late:
            flow.arrive(0)
            flow.start(1)
        for copy in out_copies:
            copy.start()

    @at_step(1, 0)
    def _():
        feats[1].arrive()
        feats[2].start()

    @at_step(2, 0)
    def _():
        feats[2].arrive()
        for flow in late:
            flow.arrive(1)
            flow.start(2)

    def get_x(block, part):
        return x_buf[micro_id, block, part, :]

    shifts = sorted(range(1, table_size), key=lambda s: (min(s, table_size - s), s))

    def full(buf):
        return lambda: buf[...].reshape(-1, buf.shape[-1])

    def some(blocks):
        project(
            blocks, rows, get_x, full(wet_buf), vec_ref, full(wk_buf), full(wv_buf), k_ref, v_ref, n_ref, (e_one, e_two)
        )

    def project_all():
        @pl.when(micro_id == 0)
        def _():
            query.arrive(last - 1)
            query.start(last)
            for shift in shifts:
                feats[0].arrive_one(shift)
            feats[1].start()
            query.arrive(last)

        some([place.at("table", shift) for shift in range(table_size)])

        x_out[0] = x_buf[micro_id].reshape(x_out.shape[1:])

    attend_core(
        support_ref[micro_id], project_all, full(wq_buf),
        q_ref, k_ref, v_ref, n_ref, emb_ref, mixed_ref, mixed_low_ref, p_ref, linv_ref, (s_one, s_two), get_x, full(wet_buf),
    )

    @at_step(micro - 1, HEADS // HEADS_STEP - 1)
    def _():
        for flow in late:
            flow.arrive(2)
        for flow in feats + early + [query] + late:
            flow.sent()
        for copy in own_copies + out_copies:
            copy.wait()


def attend_shapes(rows, length, width):
    out = [
        ((rows, width), BF16),
        ((length, width), BF16),
        ((length, width), BF16),
        ((length, width), BF16),
        ((rows, width), F32),
        ((rows, width), F32),
        ((rows, width), BF16),
    ]
    return out, [((rows, length), BF16), ((rows, LANES), F32)]


def attend_forward_gather(dp_size, table_size, support, feat, mask, ew, vecs, ub, wq, wk, wv, wo, wu, wd):
    micro, _, rows = feat.shape
    length = rows * table_size
    width = wq.shape[1]
    out, heads = attend_shapes(rows, length, width)
    whole = pl.BlockSpec(memory_space=pltpu.VMEM)
    far = pl.BlockSpec(memory_space=pl.ANY)

    def gathered(a):
        return jax.ShapeDtypeStruct((dp_size,) + a.shape, a.dtype)

    wet = jax.ShapeDtypeStruct((dp_size, wq.shape[0], LANES), BF16)
    count = micro * (table_size - 1) + 8 * len(hops_of(dp_size))
    return pl.pallas_call(
        functools.partial(attend_gather_kernel, dp_size, table_size),
        grid=(micro, HEADS // HEADS_STEP),
        in_specs=[pl.BlockSpec(memory_space=pltpu.SMEM)] + [whole] * 13 + [far] * 3,
        out_specs=[micro_spec(s) for s, _ in out]
        + [heads_spec(s) for s, _ in heads]
        + [micro_spec((length, LANES))]
        + [far] * 4
        + [const_spec((8, width)), const_spec((1, wu.shape[1]))]
        + [far] * 3
        + [const_spec((micro, 8, LANES))],
        out_shape=[jax.ShapeDtypeStruct((micro,) + s, d) for s, d in out]
        + [jax.ShapeDtypeStruct((micro, HEADS) + s, d) for s, d in heads]
        + [jax.ShapeDtypeStruct((micro, length, LANES), BF16)]
        + [wet, gathered(wq), gathered(wk), gathered(wv)]
        + [jax.ShapeDtypeStruct((8, width), F32), jax.ShapeDtypeStruct((1, wu.shape[1]), F32)]
        + [gathered(wo), gathered(wu), gathered(wd)]
        + [jax.ShapeDtypeStruct((micro, 8, LANES), F32)],
        scratch_shapes=[
            pltpu.VMEM((micro, table_size, rows, LANES), BF16),
            pltpu.VMEM(wet.shape, BF16),
            pltpu.VMEM((dp_size, 8, LANES), F32),
            pltpu.VMEM((dp_size,) + wq.shape, BF16),
            pltpu.VMEM((dp_size,) + wk.shape, BF16),
            pltpu.VMEM((dp_size,) + wv.shape, BF16),
            *attend_scratch(length, width),
            pltpu.SemaphoreType.DMA((7,)),
            pltpu.SemaphoreType.DMA((count,)),
            pltpu.SemaphoreType.DMA((count,)),
        ],
        compiler_params=vmem(60, collective_id=0, has_side_effects=True),
        name="attend_forward_gather",
    )(support, feat, mask, ew, *vecs, ub, wq, wk, wv, wo, wu, wd)


def attend_forward(support, x_all, wet, vec, wq, wk, wv, rows):
    micro, length, lanes = x_all.shape
    width = wq.shape[0]
    out, heads = attend_shapes(rows, length, width)
    return pl.pallas_call(
        attend_kernel,
        grid=(micro, HEADS // HEADS_STEP),
        in_specs=[
            pl.BlockSpec(memory_space=pltpu.SMEM),
            micro_spec((length, lanes)),
            const_spec(wet.shape),
            const_spec(vec.shape),
            const_spec(wq.shape),
            const_spec(wk.shape),
            const_spec(wv.shape),
        ],
        out_specs=[micro_spec(s) for s, _ in out] + [heads_spec(s) for s, _ in heads],
        out_shape=[jax.ShapeDtypeStruct((micro,) + s, d) for s, d in out]
        + [jax.ShapeDtypeStruct((micro, HEADS) + s, d) for s, d in heads],
        scratch_shapes=attend_scratch(length, width),
        compiler_params=vmem(58),
        name="attend_forward",
    )(support, x_all, wet, vec, wq, wk, wv)


def mlp_kernel(
    mixed_ref, emb_ref, cot_ref, wo_ref, wu_ref, wd_ref, vec_ref, bu_ref,
    act_ref, ghid_ref, gmix_ref, dwo_ref, dwu_ref, dwd_ref, dvec_ref,
    acc_o, acc_u, acc_d, gn2_ref, out_ref, *bufs,
):
    step, last = pl.program_id(0), pl.num_programs(0) - 1
    hidden_units = wu_ref.shape[1]
    chunk = 512

    @pl.when(step == 0)
    def _():
        acc_o[...] = jnp.zeros_like(acc_o)
        acc_u[...] = jnp.zeros_like(acc_u)
        acc_d[...] = jnp.zeros_like(acc_d)
        dvec_ref[...] = jnp.zeros_like(dvec_ref)

    gain, shift, dbias = vec_ref[3:4, :], vec_ref[4:5, :], vec_ref[5:6, :]
    mixed = mixed_ref[0]
    g_out = cot_ref[0]
    hidden = emb_ref[0] + dot_nn(mixed, wo_ref[...])
    unit, inv = norm_parts(hidden)
    normed = (unit * gain + shift).astype(BF16)
    out_ref[...] = hidden + dbias
    normed_t = normed.T
    g_out_t = g_out.T
    chunks = hidden_units // chunk

    def products(f):
        cols = slice(f * chunk, (f + 1) * chunk)
        bufs[2 * (f % 2)][...] = dot_nn(normed, wu_ref[:, cols])
        bufs[2 * (f % 2) + 1][...] = dot_nt(g_out, wd_ref[cols, :])

    products(0)
    for f in range(chunks):
        if f + 1 < chunks:
            products(f + 1)
        cols = slice(f * chunk, (f + 1) * chunk)
        pre = bufs[2 * (f % 2)][...] + bu_ref[:, cols]
        g_act = bufs[2 * (f % 2) + 1][...]
        cdf = 0.5 * (1.0 + lax.erf(pre * INV_SQRT_TWO))
        pdf = jnp.exp(-0.5 * pre * pre) * INV_SQRT_TWO_PI
        act = (pre * cdf).astype(BF16)
        out_ref[...] += dot_nn(act, wd_ref[cols, :])
        acc_d[:, cols] += dot_nn(g_out_t, act)
        g_pre_f = g_act * (cdf + pre * pdf)
        g_pre = g_pre_f.astype(BF16)
        acc_u[:, cols] += dot_nn(normed_t, g_pre)
        dvec_ref[8 + f : 9 + f, :] += row_sum(g_pre_f)
        g_part = dot_nt(g_pre, wu_ref[:, cols])
        if f == 0:
            gn2_ref[...] = g_part
        else:
            gn2_ref[...] += g_part
    act_ref[0] = out_ref[...].astype(BF16)
    g_norm = gn2_ref[...]
    g_out_f = g_out.astype(F32)
    dvec_ref[3:4, :] += row_sum(g_norm * unit)
    dvec_ref[4:5, :] += row_sum(g_norm)
    dvec_ref[5:6, :] += row_sum(g_out_f)
    g_hidden = g_out_f + norm_back(g_norm, unit, inv, gain)
    ghid_ref[0] = g_hidden
    branch = g_hidden.astype(BF16)
    acc_o[...] += dot_tn(mixed, branch)
    gmix_ref[0] = dot_nt(branch, wo_ref[...]).astype(BF16)

    @pl.when(step == last)
    def _():
        dwo_ref[...] = acc_o[...].astype(BF16)
        dwu_ref[...] = acc_u[...].astype(BF16)
        for f in range(hidden_units // chunk):
            cols = slice(f * chunk, (f + 1) * chunk)
            dwd_ref[cols, :] = acc_d[:, cols].T.astype(BF16)


def mlp_both(mixed, emb, cot, wo, wu, wd, vec, bu):
    micro, rows, width = mixed.shape
    hidden_units = wu.shape[1]
    per_micro = [((rows, width), BF16), ((rows, width), F32), ((rows, width), BF16)]
    summed = [
        ((width, width), BF16),
        ((width, hidden_units), BF16),
        ((hidden_units, width), BF16),
        ((16, width), F32),
    ]
    return pl.pallas_call(
        mlp_kernel,
        grid=(micro,),
        in_specs=[micro_spec((rows, width))] * 3
        + [const_spec(a.shape) for a in (wo, wu, wd, vec, bu)],
        out_specs=[micro_spec(s) for s, _ in per_micro] + [const_spec(s) for s, _ in summed],
        out_shape=[jax.ShapeDtypeStruct((micro,) + s, d) for s, d in per_micro]
        + [jax.ShapeDtypeStruct(s, d) for s, d in summed],
        scratch_shapes=[
            pltpu.VMEM((width, width), F32),
            pltpu.VMEM((width, hidden_units), F32),
            pltpu.VMEM((width, hidden_units), F32),
            pltpu.VMEM((rows, width), F32),
            pltpu.VMEM((rows, width), F32),
        ]
        + [pltpu.VMEM((rows, 512), F32)] * 4,
        compiler_params=vmem(60),
        name="mlp_both",
    )(mixed, emb, cot, wo, wu, wd, vec, bu)


def halves(lane, shift, low, high):
    half = LANES // 2
    return jnp.where(lane < half, pltpu.roll(low, shift, 1), pltpu.roll(high, half - shift, 1))


def mlp_reduce_kernel(dp_size, table_size, *refs):
    refs = list(refs)

    def take(n):
        out = refs[:n]
        del refs[:n]
        return out

    mixed_in, emb_in, cot_in, wo_in, wu_in, wd_in, vec_ref, bu_ref = take(8)
    act_out, ghid_out, gmix_out, dwo_out, small_out = take(5)
    part_outs = take(4)
    mixed_s, emb_s, cot_s, wo_s, wu_s, wd_s = take(6)
    normed_s, normed_t, g_out_t, unit_s, out_s, gn2_s = take(6)
    act_s, gmix_s, ghid_s = normed_s, normed_t, emb_s
    wu_c, wd_c, acc_u, acc_d, acc_o, inv_s = take(6)
    pre_b, gact_b = take(2), take(2)
    grads = [take(2) for _ in range(CHUNKS)]
    hops = len(hops_of(dp_size))
    scratch = [[take(hops + 2) for _ in range(2)] for _ in range(CHUNKS)]
    in_sem, out_sem, send_sem, recv_sem = refs
    micro, rows, width = mixed_s.shape
    hidden_units = wu_s.shape[-1]
    place = Place(dp_size, table_size)
    chunk, last = pl.program_id(0), CHUNKS - 1
    forth, back = place.hops["dp"], place.hops["dp"][:1] + place.hops["dp"][:0:-1]
    flows = []
    base = 0
    for f in range(CHUNKS):
        pair = []
        for grad, order, scr in zip(grads[f], (forth, back), scratch[f]):
            pair.append(
                QuickShard(
                    place, order, lambda s, grad=grad: grad.at[place.toggled("dp", s)], scr,
                    (send_sem, recv_sem), base,
                )
            )
            base += quick_sems(hops, table_size)
        flows.append(pair)

    names = []
    for m in range(micro):
        names += [(mixed_in.at[m], mixed_s.at[m])] + [(wo_in, wo_s)] * (m == 0)
        names += [(emb_in.at[m], emb_s.at[m]), (cot_in.at[m], cot_s.at[m])]
        names += [(wu_in, wu_s), (wd_in, wd_s)] * (m == 0)
    copies = [pltpu.make_async_copy(src, dst, in_sem.at[n]) for n, (src, dst) in enumerate(names)]
    gain, shift, dbias = vec_ref[3:4, :], vec_ref[4:5, :], vec_ref[5:6, :]
    half = LANES // 2
    own = hidden_units // dp_size

    def add(ref, first, value):
        ref[...] = value if first else ref[...] + value

    upto = {0: 4, 1: 3, 2: 1, 3: 1}

    def step(f, i):
        for flow in flows[f]:
            if i:
                flow.arrive(i - 1)
            if i < upto[f]:
                flow.start(i)

    @pl.when(chunk == 0)
    def _():
        for copy in copies:
            copy.start()
        wait_all = place.greet(False)
        small_out[...] = jnp.zeros_like(small_out)
        gn2_s[...] = jnp.zeros_like(gn2_s)
        n = 0
        for m in range(micro):
            copies[n].wait()
            copies[n + 1].wait()
            n += 2
            if m == 0:
                copies[n].wait()
                n += 1
            hidden = emb_s[m] + dot_nn(mixed_s[m], wo_s[...])
            unit, inv = norm_parts(hidden)
            unit_s[m] = unit
            inv_s[m] = jnp.broadcast_to(inv, (rows, LANES))
            normed = (unit * gain + shift).astype(BF16)
            normed_s[m] = normed
            normed_t[m] = normed.T
            out_s[m] = hidden + dbias
            copies[n].wait()
            n += 1
            g_out_t[m] = cot_s[m].T
            if m == 0:
                copies[n].wait()
                copies[n + 1].wait()
                n += 2
        wait_all()

    lane = lax.broadcasted_iota(jnp.int32, (width, LANES), 1)
    line = lax.broadcasted_iota(jnp.int32, (8, LANES), 1)
    turn = lax.rem(chunk, 2) * half
    biases = []
    for o in range(0, dp_size, 2):
        tiles = [pl.ds(pl.multiple_of((q * own // LANES + chunk // 2) * LANES, LANES), LANES) for q in (o, o + 1)]
        low, high = (wu_s[:, t].astype(F32) for t in tiles)
        wu_c[:, o * half : o * half + LANES] = halves(lane, turn, low, high).astype(BF16)
        low, high = (jnp.broadcast_to(bu_ref[:, t], (8, LANES)) for t in tiles)
        biases.append(halves(line, turn, low, high)[:1])
    bias = jnp.concatenate(biases, axis=1)
    wd_c[...] = wd_s[:, pl.ds(pl.multiple_of(chunk * half, half), half), :].reshape(width, width)

    def products(m):
        pre_b[m % 2][...] = dot_nn(normed_s[m], wu_c[...])
        gact_b[m % 2][...] = dot_nt(cot_s[m], wd_c[...])

    products(0)
    bias_rows = 0.0
    for m in range(micro):
        if m + 1 < micro:
            products(m + 1)
        pre = pre_b[m % 2][...] + bias
        cdf = 0.5 * (1.0 + lax.erf(pre * INV_SQRT_TWO))
        pdf = jnp.exp(-0.5 * pre * pre) * INV_SQRT_TWO_PI
        act = (pre * cdf).astype(BF16)
        out_s[m] += dot_nn(act, wd_c[...])
        add(acc_d, m == 0, dot_nn(g_out_t[m], act))
        g_pre_f = gact_b[m % 2][...] * (cdf + pre * pdf)
        g_pre = g_pre_f.astype(BF16)
        add(acc_u, m == 0, dot_nn(normed_t[m], g_pre))
        bias_rows = bias_rows + row_sum(g_pre_f)
        gn2_s[m] += dot_nt(g_pre, wu_c[...])
    row = lax.broadcasted_iota(jnp.int32, (8, width), 0)
    small_out[8:16, :] += jnp.where(row == chunk, jnp.broadcast_to(bias_rows, (8, width)), 0.0)
    up, down = acc_u[...].astype(BF16), acc_d[...].T.astype(BF16)
    for f in range(CHUNKS):

        @pl.when(chunk == f)
        def _():
            grads[f][0][...] = up.reshape(grads[f][0].shape)
            grads[f][1][...] = down.reshape(grads[f][1].shape)
            for k in range(f + 1):
                if f - k < upto[k]:
                    step(k, f - k)

    @pl.when(chunk == last)
    def _():
        outs = []
        for m in range(micro):
            act_s[m] = out_s[m].astype(BF16)
            unit, g_norm = unit_s[m], gn2_s[m]
            g_out_f = cot_s[m].astype(F32)
            small_out[3:4, :] += row_sum(g_norm * unit)
            small_out[4:5, :] += row_sum(g_norm)
            small_out[5:6, :] += row_sum(g_out_f)
            g_hidden = g_out_f + norm_back(g_norm, unit, inv_s[m][:, :1], gain)
            ghid_s[m] = g_hidden
            branch = g_hidden.astype(BF16)
            add(acc_o, m == 0, dot_tn(mixed_s[m], branch))
            gmix_s[m] = dot_nt(branch, wo_s[...]).astype(BF16)
            for src, dst in ((act_s, act_out), (ghid_s, ghid_out), (gmix_s, gmix_out)):
                outs.append(pltpu.make_async_copy(src.at[m], dst.at[m], out_sem.at[len(outs)]))
                outs[-1].start()
        dwo_out[...] = acc_o[...].astype(BF16).reshape(dwo_out.shape)
        for f in range(CHUNKS):
            step(f, upto[f])
        for i in range(2):
            side = slice(i * width, (i + 1) * width)
            part_outs[3][:, side] = flows[0][i].full[place.me["table"]]
            part_outs[2][:, :, side] = flows[1][i].dp_total()[...]
            part_outs[i][:, :, :, :width] = flows[2][i].dp.bufs[0][...]
            part_outs[i][:, :, :, width:] = flows[3][i].dp.bufs[0][...]
        for f in range(CHUNKS):
            for flow in flows[f]:
                flow.done = upto[f]
                flow.sent()
        for copy in outs:
            copy.wait()


def mlp_both_reduce(dp_size, table_size, mixed, emb, cot, wo, wu, wd, vec, bu):
    micro, rows, width = mixed.shape
    hidden_units = wu.shape[1]
    own = hidden_units // dp_size
    wd = wd.reshape(dp_size, own, width)
    far = pl.BlockSpec(memory_space=pl.ANY)
    whole = pl.BlockSpec(memory_space=pltpu.VMEM)
    block = (table_size, width // dp_size // table_size, width)
    two = block[:2] + (2 * width,)
    parts = [(4,) + two, (4,) + two, two, two[1:]]
    hops = len(hops_of(dp_size))

    def per_micro(dtype):
        return pltpu.VMEM((micro, rows, width), dtype)

    def square(dtype):
        return pltpu.VMEM((width, width), dtype)

    scratch = [per_micro(BF16), per_micro(F32), per_micro(BF16)]
    scratch += [square(BF16), pltpu.VMEM(wu.shape, BF16), pltpu.VMEM(wd.shape, BF16)]
    scratch += [per_micro(BF16)] + [pltpu.VMEM((micro, width, rows), BF16)] * 2
    scratch += [per_micro(F32)] * 3
    scratch += [square(BF16)] * 2 + [square(F32)] * 3 + [pltpu.VMEM((micro, rows, LANES), F32)]
    scratch += [pltpu.VMEM((rows, width), F32)] * 4
    scratch += [pltpu.VMEM((dp_size,) + block, BF16)] * (2 * CHUNKS)
    for _ in range(2 * CHUNKS):
        scratch += quick_scratch(hops, table_size, block, BF16)
    count = 2 * CHUNKS * quick_sems(hops, table_size)
    scratch += [pltpu.SemaphoreType.DMA((3 * micro + 3,)), pltpu.SemaphoreType.DMA((3 * micro,))]
    scratch += [pltpu.SemaphoreType.DMA((count,))] * 2
    return pl.pallas_call(
        functools.partial(mlp_reduce_kernel, dp_size, table_size),
        grid=(CHUNKS,),
        in_specs=[far] * 6 + [whole] * 2,
        out_specs=[far] * 3 + [whole] * 6,
        out_shape=[jax.ShapeDtypeStruct((micro, rows, width), d) for d in (BF16, F32, BF16)]
        + [jax.ShapeDtypeStruct((dp_size, width // dp_size, width), BF16), jax.ShapeDtypeStruct((16, width), F32)]
        + [jax.ShapeDtypeStruct(p, BF16) for p in parts],
        scratch_shapes=scratch,
        compiler_params=vmem(60, collective_id=2, has_side_effects=True),
        name="mlp_both_reduce",
    )(mixed, emb, cot, wo, wu, wd, vec, bu)


def attend_back_core(
    hooks, p_ref, linv_ref, k_ref, v_ref, q_ref, gmix_ref, mixed_ref, n_ref, x_ref, ghid_ref,
    wet_ref, vec_ref, wq_ref, wk_ref, wv_ref,
    sums_ref, dkv_ref, dq_ref, wkv_t, wq_t, acc_e, acc_q, acc_kv, d_bufs, e_bufs, g_bufs,
):
    step, pair = pl.program_id(0), pl.program_id(1)
    length, rows, width = n_ref.shape[1], dq_ref.shape[0], dq_ref.shape[1]
    heads = p_ref.shape[1]
    own = lax.axis_index("table")
    here = pl.ds(pl.multiple_of(own * rows, rows), rows)

    @pl.when((step == 0) & (pair == 0))
    def _():
        acc_e[...] = jnp.zeros_like(acc_e)
        acc_q[...] = jnp.zeros_like(acc_q)
        acc_kv[...] = jnp.zeros_like(acc_kv)
        sums_ref[...] = jnp.zeros_like(sums_ref)
        gain = vec_ref[1:2, :]

        def weigh(w):
            w = w.T.astype(F32) * gain
            return (w - jnp.mean(w, axis=-1, keepdims=True)).astype(BF16)

        for h in range(HEADS):
            cols = slice(h * HEAD_DIM, (h + 1) * HEAD_DIM)
            wkv_t[2 * h * HEAD_DIM : (2 * h + 1) * HEAD_DIM, :] = weigh(wk_ref[:, cols])
            wkv_t[(2 * h + 1) * HEAD_DIM : (2 * h + 2) * HEAD_DIM, :] = weigh(wv_ref[:, cols])
            wq_t[cols, :] = weigh(wq_ref[:, cols])

    keys = d_bufs[0].shape[1]
    units = [(h, j) for h in range(heads) for j in range(length // keys)]
    low, low_t, delta, q_t, dq = {}, {}, {}, {}, {}

    def prepare(h):
        cols = slice(h * HEAD_DIM, (h + 1) * HEAD_DIM)
        linv = linv_ref[0, h][:, :1]
        low[h] = (gmix_ref[0, :, cols].astype(F32) * linv).astype(BF16)
        delta[h] = jnp.sum(mixed_ref[0, :, cols] * low[h].astype(F32), axis=-1, keepdims=True)
        low_t[h] = low[h].T
        q_t[h] = q_ref[0, :, cols].T

    def grad_p(u):
        h, j = units[u]
        if j == 0:
            prepare(h)
        at = slice(j * keys, (j + 1) * keys)
        d_bufs[u % 2][...] = dot_nt(low[h], v_ref[0, at, h * HEAD_DIM : (h + 1) * HEAD_DIM])

    grad_p(0)
    for u, (h, j) in enumerate(units):
        if u + 1 < len(units):
            grad_p(u + 1)
        at = slice(j * keys, (j + 1) * keys)
        cols = slice(h * HEAD_DIM, (h + 1) * HEAD_DIM)
        k_rows = pl.ds(pl.multiple_of(2 * (pair * heads + h) * HEAD_DIM, HEAD_DIM), HEAD_DIM)
        v_rows = pl.ds(pl.multiple_of((2 * (pair * heads + h) + 1) * HEAD_DIM, HEAD_DIM), HEAD_DIM)
        p = p_ref[0, h, :, at]
        dkv_ref[v_rows, at] = dot_nn(low_t[h], p).astype(BF16)
        ds = (p.astype(F32) * (d_bufs[u % 2][...] - delta[h])).astype(BF16)
        dkv_ref[k_rows, at] = (dot_nn(q_t[h], ds) * SCALE).astype(BF16)
        dq_part = dot_nn(ds, k_ref[0, at, cols])
        dq[h] = dq_part if j == 0 else dq[h] + dq_part
    for h in range(heads):
        cols = pl.ds(pl.multiple_of((pair * heads + h) * HEAD_DIM, HEAD_DIM), HEAD_DIM)
        dq_ref[:, cols] = (dq[h] * SCALE).astype(BF16)
    for h in range(heads):
        at = pl.ds(pl.multiple_of((pair * heads + h) * 2 * HEAD_DIM, 2 * HEAD_DIM), 2 * HEAD_DIM)
        acc_kv[at, :] += dot_nn(dkv_ref[at, :], n_ref[0])
    both = pl.ds(pl.multiple_of(pair * heads * HEAD_DIM, heads * HEAD_DIM), heads * HEAD_DIM)
    acc_q[both, :] += dot_tn(dq_ref[:, both], n_ref[0, here, :])
    sums_ref[0:1, both] += row_sum(gmix_ref[0].astype(F32))
    sums_ref[1:2, both] += row_sum(dq_ref[:, both].astype(F32))
    hooks.pair_done()

    @pl.when(pair == HEADS // heads - 1)
    def _():
        part = e_bufs[0].shape[0]
        hooks.tick(HEADS // heads, None)

        def rows_back(block, mine):
            def spot(u):
                return pl.ds(pl.multiple_of(block * rows + u * part, part), part), slice(u * part, (u + 1) * part)

            def products(u):
                at, inner = spot(u)
                e_bufs[u % 2][...] = dot_nt(x_ref[0, at, :], wet_ref[...])
                q = dot_tn(dkv_ref[:, at], wkv_t[...])
                if mine:
                    q = q + dot_nn(dq_ref[inner, :], wq_t[...])
                g_bufs[u % 2][...] = q

            products(0)
            for u in range(rows // part):
                if u + 1 < rows // part:
                    products(u + 1)
                at, inner = spot(u)
                unit, inv = norm_parts(e_bufs[u % 2][...])
                q = g_bufs[u % 2][...]
                g_emb = inv * (q - unit * jnp.mean(q * unit, axis=-1, keepdims=True))
                if mine:
                    g_emb = g_emb + ghid_ref[0, inner, :]
                g_emb = g_emb.astype(BF16)
                acc_e[...] += dot_tn(x_ref[0, at, :], g_emb)
                hooks.put(block, mine, inner, dot_nn(g_emb, wet_ref[...]))

        size = length // rows

        def other(g, carry):
            block = lax.rem(own + 1 + g, size)
            rows_back(block, False)
            hooks.block_done(g, block)
            hooks.tick(HEADS // heads + 1, g)
            return carry

        lax.fori_loop(0, size - 1, other, 0)
        rows_back(own, True)
        hooks.own_done()


def norm_one_grads(vec_ref, wq_ref, wk_ref, wv_ref, sums_ref, acc_q, acc_kv):
    gain, shift = vec_ref[1:2, :], vec_ref[2:3, :]
    total = row_sum(wq_ref[...].T.astype(F32) * acc_q[...])
    for h in range(HEADS):
        cols = slice(h * HEAD_DIM, (h + 1) * HEAD_DIM)
        k_rows = slice(2 * h * HEAD_DIM, (2 * h + 1) * HEAD_DIM)
        v_rows = slice((2 * h + 1) * HEAD_DIM, (2 * h + 2) * HEAD_DIM)
        total += row_sum(wk_ref[:, cols].T.astype(F32) * acc_kv[k_rows, :])
        total += row_sum(wv_ref[:, cols].T.astype(F32) * acc_kv[v_rows, :])
    sums = sums_ref[...]
    high = sums.astype(BF16)
    rest = (sums - high.astype(F32)).astype(BF16)
    by_v = dot_nt(high, wv_ref[...]) + dot_nt(rest, wv_ref[...])
    by_q = dot_nt(high, wq_ref[...]) + dot_nt(rest, wq_ref[...])
    d_shift = by_v[0:1, :] + by_q[1:2, :]
    return (total - shift * d_shift) / gain, d_shift


class Alone:
    def __init__(self, ig_ref, rows):
        self.ig_ref, self.rows = ig_ref, rows

    def tick(self, k, g):
        pass

    def pair_done(self):
        pass

    def put(self, block, mine, inner, value):
        at = pl.ds(pl.multiple_of(block * self.rows + inner.start, 128), inner.stop - inner.start)
        self.ig_ref[0, at, :] = value.astype(BF16)

    def block_done(self, g, block):
        pass

    def own_done(self):
        pass


def attend_back_kernel(*refs):
    ins, rest = refs[:15], refs[15:]
    ig_ref, dwe_ref, dwq_ref, dwk_ref, dwv_ref, dvec_ref = rest[:6]
    scratch, bufs = rest[6:14], rest[14:]
    sums_ref, acc_e, acc_q, acc_kv = scratch[0], *scratch[5:8]
    vec_ref, wq_ref, wk_ref, wv_ref = ins[11:15]
    rows = scratch[2].shape[0]
    attend_back_core(Alone(ig_ref, rows), *ins, *scratch, bufs[:2], bufs[2:4], bufs[4:])

    @pl.when((pl.program_id(0) == pl.num_programs(0) - 1) & (pl.program_id(1) == pl.num_programs(1) - 1))
    def _():
        dwe_ref[...] = acc_e[...].T.astype(BF16)
        dwq_ref[...] = acc_q[...].T.astype(BF16)
        d_gain, d_shift = norm_one_grads(vec_ref, wq_ref, wk_ref, wv_ref, sums_ref, acc_q, acc_kv)
        dvec_ref[...] = jnp.zeros_like(dvec_ref)
        dvec_ref[1:2, :] = d_gain
        dvec_ref[2:3, :] = d_shift
        for h in range(HEADS):
            cols = slice(h * HEAD_DIM, (h + 1) * HEAD_DIM)
            dwk_ref[:, cols] = acc_kv[2 * h * HEAD_DIM : (2 * h + 1) * HEAD_DIM, :].T.astype(BF16)
            dwv_ref[:, cols] = acc_kv[(2 * h + 1) * HEAD_DIM : (2 * h + 2) * HEAD_DIM, :].T.astype(BF16)


class Sums:
    def __init__(self, tail, igs):
        self.tail, self.igs = tail, igs
        self.micro, self.head = pl.program_id(0), pl.program_id(1)
        self.count = len(igs)
        self.todo = {}

    def tick(self, k, g=None):
        for m in range(self.count):
            for i in range(1 if g is None else TABLE_STEPS):
                actions = self.todo.get((m, k + i), [])
                if not actions:
                    continue
                now = self.micro == m
                now = now & (self.head == k) if k < PAIRS else now if g is None else now & (g == i)

                @pl.when(now)
                def _():
                    for action in actions:
                        action()

    def start_of_step(self):
        for k in range(PAIRS):
            self.tick(k)

    def at(self, m, k, action):
        self.todo.setdefault((m, k), []).append(action)

    def step(self, flows, i):
        def action():
            for flow in flows:
                if i:
                    flow.arrive(i - 1)
                if i < flow.steps:
                    flow.start(i)

        return action

    def pair_done(self):
        for g in range(PAIRS):

            @pl.when((self.micro == self.count - 1) & (self.head == g))
            def _():
                self.write_pair(g)
                self.step(self.tail[g], 0)()

    def put(self, block, mine, inner, value):
        if mine:
            self.ig_own[inner, :] = value
        else:
            self.ig_bufs[self.micro, block, inner, :] = value.astype(BF16)

    def block_done(self, g, block):
        for m in range(self.count):

            @pl.when(self.micro == m)
            def _():
                self.igs[m].start_one(g + 1)

    def own_done(self):
        self.ig_out[self.micro] = self.ig_own[...]
        self.tick(PAIRS + 1 + TABLE_STEPS)

    def ig_finish(self, m):
        def action():
            total = self.ig_out[m]
            for got in self.igs[m].arrive():
                total = total + got[...].astype(F32)
            self.ig_out[m] = total

        return action


def attend_back_reduce_kernel(dp_size, table_size, *refs):
    refs = list(refs)

    def take(n):
        out = refs[:n]
        del refs[:n]
        return out

    ins = take(15)
    vec_ref, wq_ref, wk_ref, wv_ref = ins[11:15]
    parts = take(5)
    (small_in,) = take(1)
    ig_out, small_out, embed_out, dwo_out = take(4)
    totals = take(8)
    core = take(8)
    sums_ref, acc_e, acc_q, acc_kv = core[0], *core[5:8]
    bufs = take(6)
    place = Place(dp_size, table_size)
    hops = place.hops["dp"]
    out_scratch = take(3)
    part_scratch = [take(n) for n in (4, 4, 2, 1)]
    tail_grads = take(4)
    tail_scratch = [take(len(hops) + 2) for _ in range(4)]
    embed_grad, small_grad = take(2)
    embed_scratch, small_scratch_ = take(3), take(3)
    micro = ig_out.shape[0]
    (ig_bufs,) = take(1)
    ig_got = take(micro)
    (ig_own,) = take(1)
    send_sem, recv_sem = refs
    sems = (send_sem, recv_sem)
    forth, back = hops, hops[:1] + hops[:0:-1]
    base = 0

    def count_up(n):
        nonlocal base
        base += n
        return base - n

    def quick(order, blocks, scratch, back_only=False, array=None):
        at = count_up(quick_sems(len(order), table_size, back_only))
        return QuickShard(place, order, blocks, scratch, sems, at, back_only, array)

    mlp = []
    for order, back_only, part, scr in zip((forth[1:], back[1:], [], []), (False,) * 3 + (True,), parts[1:], part_scratch):
        mlp.append(quick(order, None, scr, back_only, part))
    others = dp_size + table_size - 2
    mlp_out = Small(place, lambda d: parts[0].at[d], *out_scratch, sems, count_up(others), dwo_out)
    tail = [
        [
            quick(
                order,
                lambda s, grad=tail_grads[2 * g + i]: grad.at[place.toggled("dp", s)],
                tail_scratch[2 * g + i],
            )
            for i, order in enumerate((forth, back))
        ]
        for g in range(2)
    ]
    embed = Small(place, lambda d: embed_grad.at[d], *embed_scratch, sems, count_up(others), embed_out)
    small = Small(place, lambda d: small_grad.at[d // 2], *small_scratch_, sems, count_up(others), small_out)
    igs = []
    for m in range(micro):
        igs.append(
            Swap(
                place, "table", sems, count_up(table_size - 1),
                lambda t, m=m: ig_bufs.at[m, t],
                lambda t, s, m=m: ig_got[m].at[s - 1],
            )
        )
    hooks = Sums(tail, igs)
    hooks.ig_bufs, hooks.ig_own, hooks.ig_out = ig_bufs, ig_own, ig_out

    def write_pair(g):
        one, two = tail_grads[2 * g], tail_grads[2 * g + 1]
        shape = one.shape[:-1]

        def put(ref, at, value):
            ref[:, :, :, at * HEAD_DIM : at * HEAD_DIM + value.shape[1]] = value.astype(BF16).reshape(
                shape + (value.shape[1],)
            )

        def rows_of(h, side):
            at = (2 * h + side) * HEAD_DIM
            return acc_kv[at : at + HEAD_DIM, :].T

        put(one, 0, acc_q[2 * g * HEAD_DIM : (2 * g + 2) * HEAD_DIM, :].T)
        put(one, 2, rows_of(2 * g, 0))
        put(two, 0, rows_of(2 * g + 1, 0))
        put(two, 1, rows_of(2 * g, 1))
        put(two, 2, rows_of(2 * g + 1, 1))

    hooks.write_pair = write_pair

    last = micro - 1
    hooks.at(0, 0, lambda: place.greet(True)())
    for i, (m, k) in enumerate(((0, 0), (0, 2), (1, 1), (2, 0), (2, 2))):
        hooks.at(m, k, hooks.step([f for f in mlp if i <= f.steps], i))
    for i, (m, k) in enumerate(((0, 0), (0, 2), (1, 1))):
        hooks.at(m, k, hooks.step([mlp_out], i))

    def start_small():
        d_gain, d_shift = norm_one_grads(vec_ref, wq_ref, wk_ref, wv_ref, sums_ref, acc_q, acc_kv)
        for t in range(dp_size // 2):
            cols = slice(t * LANES, (t + 1) * LANES)
            small_grad[t] = small_in[:, cols]
            small_grad[t, 1:2, :] = d_gain[:, cols]
            small_grad[t, 2:3, :] = d_shift[:, cols]
        hooks.step([small], 0)()

    hooks.at(2, 0, hooks.ig_finish(0))
    hooks.at(2, 2, hooks.step(tail[0], 1))
    hooks.at(2, 2, start_small)
    hooks.at(2, 5, hooks.step(tail[1], 1))

    def finish():
        embed_grad[...] = acc_e[...].T.astype(BF16).reshape(embed_grad.shape)
        hooks.step([embed], 0)()
        hooks.step([small], 1)()
        hooks.step(tail[0], 2)()
        hooks.step(tail[1], 2)()
        hooks.step(tail[0], 3)()
        hooks.step(tail[1], 3)()
        hooks.ig_finish(1)()
        hooks.step([embed], 1)()
        hooks.step(tail[0], 4)()
        hooks.step(tail[1], 4)()
        hooks.ig_finish(last)()
        hooks.step([small, embed], 2)()
        hooks.step(tail[0], 5)()
        hooks.step(tail[1], 5)()
        for flow in mlp + [mlp_out, small, embed] + tail[0] + tail[1] + igs:
            flow.sent()
        for flow, out in zip(mlp + tail[0] + tail[1], totals):
            out[...] = flow.full[...]

    hooks.at(last, PAIRS + 1 + TABLE_STEPS, finish)
    hooks.start_of_step()
    attend_back_core(hooks, *ins, *core, bufs[:2], bufs[2:4], bufs[4:])


def back_scratch(length, rows, width):
    return [
        pltpu.VMEM((8, width), F32),
        pltpu.VMEM((2 * width, length), BF16),
        pltpu.VMEM((rows, width), BF16),
        pltpu.VMEM((2 * width, width), BF16),
        pltpu.VMEM((width, width), BF16),
        pltpu.VMEM((LANES, width), F32),
        pltpu.VMEM((width, width), F32),
        pltpu.VMEM((2 * width, width), F32),
    ]


def back_buffers(rows, width):
    return [pltpu.VMEM((rows, KEY_BLOCK), F32)] * 2 + [pltpu.VMEM((BACK_BLOCK, width), F32)] * 4


def back_specs(by_head, cols, varied, fixed):
    return (
        [heads_spec(a.shape[2:]) for a in by_head]
        + [pl.BlockSpec((1, a.shape[1], HEADS_STEP * HEAD_DIM), lambda m, h: (m, 0, h)) for a in cols]
        + [micro_spec(a.shape[1:]) for a in varied]
        + [const_spec(a.shape) for a in fixed]
    )


def attend_backward(p, linv, k, v, q, gmix, mixed, n, x, ghid, wet, vec, wq, wk, wv):
    micro, rows, width = q.shape
    length = k.shape[1]
    varied = (n, x, ghid)
    fixed = (wet, vec, wq, wk, wv)
    summed = [(wet.shape, BF16)] + [((width, width), BF16)] * 3 + [((8, width), F32)]
    return pl.pallas_call(
        attend_back_kernel,
        grid=(micro, HEADS // HEADS_STEP),
        in_specs=back_specs((p, linv), (k, v, q, gmix, mixed), varied, fixed),
        out_specs=[micro_spec((length, LANES))] + [const_spec(s) for s, _ in summed],
        out_shape=[jax.ShapeDtypeStruct((micro, length, LANES), BF16)]
        + [jax.ShapeDtypeStruct(s, d) for s, d in summed],
        scratch_shapes=back_scratch(length, rows, width) + back_buffers(rows, width),
        compiler_params=vmem(58),
        name="attend_backward",
    )(p, linv, k, v, q, gmix, mixed, *varied, *fixed)


def attend_backward_reduce(
    dp_size, table_size, parts, small, p, linv, k, v, q, gmix, mixed, n, x, ghid, wet, vec, wq, wk, wv
):
    micro, rows, width = q.shape
    length = k.shape[1]
    varied = (n, x, ghid)
    fixed = (wet, vec, wq, wk, wv)
    whole = pl.BlockSpec(memory_space=pltpu.VMEM)
    shard = width // dp_size
    block = (table_size, shard // table_size, width)
    tail = (dp_size, table_size, shard // table_size, 3 * HEAD_DIM)
    two = block[:2] + (2 * width,)
    blocks = [two] * 4 + [tail[1:]] * 4
    hops = len(hops_of(dp_size))
    kinds = [(2, False)] * 2 + [(0, False), (0, True)]
    scratch = back_scratch(length, rows, width) + back_buffers(rows, width)
    scratch += small_scratch(dp_size, table_size, (shard, width), BF16)
    for n, back_only in kinds:
        scratch += quick_scratch(n, table_size, two, BF16, back_only)
    scratch += [pltpu.VMEM(tail, BF16)] * 4
    for _ in range(4):
        scratch += quick_scratch(hops, table_size, tail[1:], BF16)
    tile = (small.shape[0], LANES)
    scratch += [pltpu.VMEM((dp_size, shard, LANES), BF16), pltpu.VMEM((dp_size // 2,) + tile, F32)]
    scratch += small_scratch(dp_size, table_size, (shard, LANES), BF16)
    scratch += small_scratch(dp_size, table_size, tile, F32)
    scratch += [pltpu.VMEM((micro, table_size, rows, LANES), BF16)]
    scratch += [pltpu.VMEM((table_size - 1, rows, LANES), BF16)] * micro
    scratch += [pltpu.VMEM((rows, LANES), F32)]
    count = sum(quick_sems(n, table_size, back_only) for n, back_only in kinds + [(hops, False)] * 4)
    count += 3 * (dp_size + table_size - 2) + micro * (table_size - 1)
    scratch += [pltpu.SemaphoreType.DMA((count,))] * 2
    outs = [((micro, rows, LANES), F32), (tile, F32), ((shard, LANES), F32), ((shard, width), F32)]
    outs += [(b, BF16) for b in blocks]
    return pl.pallas_call(
        functools.partial(attend_back_reduce_kernel, dp_size, table_size),
        grid=(micro, PAIRS),
        in_specs=back_specs((p, linv), (k, v, q, gmix, mixed), varied, fixed)
        + [whole] * 5
        + [const_spec(small.shape)],
        out_specs=[const_spec(shape) for shape, _ in outs],
        out_shape=[jax.ShapeDtypeStruct(shape, dtype) for shape, dtype in outs],
        scratch_shapes=scratch,
        compiler_params=vmem(60, collective_id=1, has_side_effects=True),
        name="attend_backward_reduce",
    )(p, linv, k, v, q, gmix, mixed, *varied, *fixed, *parts, small)


def finish_kernel(feat, shard, mask_ref, ig_in, small_in, embed_in, *refs):
    chunk_ins, out_in, pair_ins, outs = refs[:4], refs[4], refs[5:9], refs[9:]
    ig_out, dwe, dwq, dwk, dwv, dwo, dwu, dwd = outs[:8]
    vecs, bu = outs[8:14], outs[14]
    half = LANES // 2
    for m in range(ig_in.shape[0]):
        ig_out[m] = (ig_in[m] * mask_ref[m][:1]).T[:feat, :]
    dwe[...] = embed_in[:, :feat]
    dwo[...] = out_in[...]
    lane = lax.broadcasted_iota(jnp.int32, (shard, LANES), 1)
    width = dwo.shape[1]
    ups = [(3, 0), (2, 0), (0, 0), (0, width)]
    downs = [(3, width), (2, width), (1, 0), (1, width)]
    for f, (ref, side) in enumerate(downs):
        dwd[f * half : (f + 1) * half, :] = chunk_ins[ref][:, side : side + width].astype(F32)

    def up_tile(f, o):
        ref, side = ups[f]
        at = side + o // 2 * LANES
        return chunk_ins[ref][:, at : at + LANES].astype(F32)

    per_owner = bu.shape[1]
    for o in range(dwu.shape[1] // per_owner):
        for f in range(0, CHUNKS, 2):
            low, high = up_tile(f, o), up_tile(f + 1, o)
            at = o * per_owner + f * half
            dwu[:, at : at + LANES] = halves(lane, o % 2 * half, low, high)
    for g in range(HEADS // 2):
        one, two = pair_ins[2 * g], pair_ins[2 * g + 1]
        at = 2 * g * HEAD_DIM
        dwq[:, at : at + 2 * HEAD_DIM] = one[:, : 2 * HEAD_DIM].astype(F32)
        dwk[:, at : at + HEAD_DIM] = one[:, 2 * HEAD_DIM :].astype(F32)
        dwk[:, at + HEAD_DIM : at + 2 * HEAD_DIM] = two[:, :HEAD_DIM].astype(F32)
        dwv[:, at : at + 2 * HEAD_DIM] = two[:, HEAD_DIM:].astype(F32)
    small = small_in[...]
    turned = pltpu.roll(small, lax.rem(lax.axis_index("dp"), 2) * half, 1)
    vecs[0][...] = embed_in[...].T[feat : feat + 1, :]
    for i, out in enumerate(vecs[1:]):
        out[...] = turned[i + 1 : i + 2, :shard]
    rows = turned[8:16, :]
    line = lax.broadcasted_iota(jnp.int32, (8, LANES), 1)
    for f in range(0, CHUNKS, 2):
        low = jnp.broadcast_to(rows[f : f + 1, :], (8, LANES))
        high = jnp.broadcast_to(rows[f + 1 : f + 2, :], (8, LANES))
        bu[:, f * half : f * half + LANES] = halves(line, 0, low, high)[:1]


def finish(feat, ff_shard, mask, ig, small, embed, chunks, rest):
    micro, rows, _ = ig.shape
    shard = embed.shape[0]
    width = rest[0].shape[1]
    out_shape = (
        [jax.ShapeDtypeStruct((micro, feat, rows), F32), jax.ShapeDtypeStruct((shard, feat), F32)]
        + [jax.ShapeDtypeStruct((shard, width), F32)] * 4
        + [jax.ShapeDtypeStruct((shard, CHUNKS * width), F32), jax.ShapeDtypeStruct((ff_shard, width), F32)]
        + [jax.ShapeDtypeStruct((1, shard), F32)] * 6
        + [jax.ShapeDtypeStruct((1, ff_shard), F32)]
    )
    return pl.pallas_call(
        functools.partial(finish_kernel, feat, shard),
        out_shape=out_shape,
        compiler_params=vmem(60),
        name="finish",
    )(mask, ig, small, embed, *chunks, *rest)


def body(
    dp_size, table_size, features, feature_mask, support_count, embed_weight, embed_bias, gain_first, shift_first,
    query_weight, key_weight, value_weight, out_weight, gain_second, shift_second, up_weight, up_bias,
    down_weight, down_bias, cotangent,
):
    micro, _, rows, feat = features.shape
    shard, width = query_weight.shape
    hidden_units = up_weight.shape[1]
    ff_shard = up_bias.shape[0]
    features, cotangent, support = features[:, 0], cotangent[:, 0], support_count[:, 0]
    vectors = (embed_bias, gain_first, shift_first, gain_second, shift_second, down_bias)
    if 2 * shard == LANES and micro == 3 and table_size == 4 and ff_shard == CHUNKS * shard:
        got = attend_forward_gather(
            dp_size, table_size, support, features.transpose(0, 2, 1), feature_mask, embed_weight.T,
            [a[None] for a in vectors], up_bias.reshape(-1, LANES),
            query_weight, key_weight, value_weight, out_weight, up_weight, down_weight,
        )
        q, k, v, n, emb, mixed, mixed_low, p, linv, x = got[:10]
        wet, wq, wk, wv = (g.reshape(-1, g.shape[-1]) for g in got[10:14])
        vec, bu = got[14:16]
        wo, wu, wd = (g.reshape(-1, g.shape[-1]) for g in got[16:19])
        activations, ghid, gmix, dwo, small, *parts = mlp_both_reduce(
            dp_size, table_size, mixed_low, emb, cotangent, wo, wu, wd, vec, bu
        )
        ig, small, embed, dwo, *totals = attend_backward_reduce(
            dp_size, table_size, [dwo] + parts, small, p, linv, k, v, q, gmix, mixed, n, x, ghid, wet, vec, wq, wk, wv
        )
        totals = [t.reshape(-1, t.shape[-1]) for t in totals]
        out = finish(feat, ff_shard, got[-1], ig, small, embed, totals[:4], [dwo] + totals[4:])
        ig, dwe, dwq, dwk, dwv, dwo, dwu, dwd = out[:8]
        ig, dwe = ig.transpose(0, 2, 1), dwe.T
        smalls = [o.reshape(-1) for o in out[8:14]]
        dbu = out[14].reshape(-1)
    else:
        smalls = jnp.stack(vectors)
        mask = jnp.pad(feature_mask[:, 0], ((0, 0), (0, LANES - feat)))[:, None, :]
        x = jnp.pad(features, ((0, 0), (0, 0), (0, LANES - feat))) * mask.astype(BF16)
        x = x.at[:, :, feat].set(1.0)
        wet = jnp.concatenate([embed_weight, embed_bias[None]])
        wet = jnp.pad(wet, ((0, LANES - feat - 1), (0, 0))).T
        shards = [wet, query_weight, key_weight, value_weight, out_weight, up_weight, down_weight]
        wet, wq, wk, wv, wo, wu, wd = (lax.all_gather(s, "dp", axis=0, tiled=True) for s in shards)
        vec = jnp.pad(lax.all_gather(smalls, "dp", axis=1, tiled=True).astype(F32), ((0, 2), (0, 0)))
        bu = lax.all_gather(up_bias, "dp", axis=0, tiled=True).astype(F32)[None]
        x = lax.all_gather(x, "table", axis=1, tiled=True)
        q, k, v, n, emb, mixed, mixed_low, p, linv = attend_forward(support, x, wet, vec, wq, wk, wv, rows)
        activations, ghid, gmix, dwo, dwu, dwd, small = mlp_both(mixed_low, emb, cotangent, wo, wu, wd, vec, bu)
        ig, dwe, dwq, dwk, dwv, dvec = attend_backward(
            p, linv, k, v, q, gmix, mixed, n, x, ghid, wet, vec, wq, wk, wv
        )
        big = [dwe, dwq, dwk, dwv, dwo, dwu, dwd]
        own = [lax.psum_scatter(g.astype(F32), "dp", scatter_dimension=0, tiled=True) for g in big]
        dwe, dwq, dwk, dwv, dwo, dwu, dwd = (lax.psum(g, "table") for g in own)
        dbe, dwe = dwe[:, feat], dwe[:, :feat].T
        dvec = jnp.concatenate([dvec[:3], small[3:6]])
        smalls = lax.psum(lax.psum_scatter(dvec, "dp", scatter_dimension=1, tiled=True), "table")
        smalls = [dbe] + [smalls[i] for i in range(1, 6)]
        dbu = small[8:].reshape(-1)[:hidden_units]
        dbu = lax.psum(lax.psum_scatter(dbu, "dp", scatter_dimension=0, tiled=True), "table")
        ig = lax.psum_scatter(ig.astype(F32) * mask, "table", scatter_dimension=1, tiled=True)[:, :, :feat]
    return (
        activations[:, None], ig[:, None], dwe, smalls[0], smalls[1], smalls[2],
        dwq, dwk, dwv, dwo, smalls[3], smalls[4], dwu, dbu, dwd, smalls[5],
    )


def solution(mesh):
    rows, cols, vecs = P("dp", None), P(None, "dp"), P("dp")
    table = P(None, "dp", "table", None)
    return jax.shard_map(
        functools.partial(body, mesh.shape["dp"], mesh.shape["table"]),
        mesh=mesh,
        in_specs=(
            table, P(None, "dp", None), cols, cols, vecs, vecs, vecs, rows, rows, rows, rows,
            vecs, vecs, rows, vecs, rows, vecs, table,
        ),
        out_specs=(
            table, table, cols, vecs, vecs, vecs, rows, rows, rows, rows, vecs, vecs, rows, vecs, rows, vecs,
        ),
        check_vma=False,
    )
```
